32 devices in a mesh: ctx: 8 (over z, x), tp: 4 (over y, core).
Axes of the slice: x: 2, y: 2, z: 4, core: 2. Of those that a mesh axis runs over, the one named last changes fastest.
Arguments:
- q_one: bfloat16 [2048, 4096], P('ctx', 'tp'), may hold values from -880 to 880
- k_one: bfloat16 [2048, 4096], P('ctx', 'tp'), may hold values from -6 to 6
- v_one: bfloat16 [2048, 4096], P('ctx', 'tp'), may hold values from -6 to 6
- q_two: bfloat16 [2048, 4096], P('ctx', 'tp'), may hold values from -6 to 6
- k_two: bfloat16 [2048, 4096], P('ctx', 'tp'), may hold values from -6 to 6
- short_taps: bfloat16 [3, 7, 256], P(None, None, 'tp'), may hold values from -2 to 2
- medium_taps: bfloat16 [128, 256], P(None, 'tp'), may hold values from -0.5 to 0.5
- long_taps: bfloat16 [256, 2048], P('tp', 'ctx'), may hold values from -0.125 to 0.125
- skip_gain: float32 [4096], P('tp'), may hold values from -4 to 4
- block_order: int32 [8], replicated, may hold values from 0 to 7, as said below
- prev_owner: int32 [8], replicated, may hold values from 0 to 7, as said below
Outputs:
- gated_out: bfloat16 [2048, 4096], P('ctx', 'tp')
The draws below stay inside these ranges and needn't reach their ends.
Inputs may be any that keep to these rules, and one draw needn't show every extreme that they name: `block_order`: A permutation of the 8 sequence blocks over the devices of ctx. prev_owner[b] is the device d with block_order[d] = b - 1 for b > 0, and prev_owner[0] the device holding block 7.
All inputs are finite; a program needn't handle non-finite values.
Results may differ from the reference program's by a relative error of at most 0.008.
Values may be sent and summed in bfloat16 or wider, within the bound.
No kernel may reach another device: no remote copies, remote signals or barrier semaphores. Data moves between devices by JAX's collectives and lax.ppermute only.
A program may use at most 128 MiB of HBM per device.

```python
import math
import jax
import jax.numpy as jnp
from jax import lax

CH = 4096
GROUP = 16
SE = 7
MR = 128
T_DEV = 256
GROUPS = 256
SEQ = 2048
N_CTX = 8


def draw_q_one(key, part):
    noise_key, row_key, col_key = jax.random.split(key, 3)
    channel = jnp.arange(CH, dtype=jnp.float32) / CH
    noise = jax.random.truncated_normal(noise_key, -4.0, 4.0, (SEQ, CH), jnp.float32)
    ramp = 1.0 + 1.2 * channel
    row_scale = jnp.exp(jax.random.uniform(row_key, (SEQ, 1), jnp.float32, 0.0, math.log(10.0)))
    col_scale = jnp.exp(jax.random.uniform(col_key, (1, CH), jnp.float32, 0.0, math.log(10.0)))
    return (noise * row_scale * col_scale * ramp[None, :]).astype(jnp.bfloat16)


def block_layout(key):
    return jax.random.permutation(jax.random.fold_in(key, 11), N_CTX).astype(jnp.int32)


def draw_block_order(key, part):
    return block_layout(key)


def draw_prev_owner(key, part):
    order = block_layout(key)
    holder = jnp.zeros((N_CTX,), jnp.int32).at[order].set(jnp.arange(N_CTX, dtype=jnp.int32))
    return jnp.roll(holder, 1)


def block_levels(own_key, dims, pieces, smallest, high):
    level, own = 1.0, jax.random.fold_in(own_key, 6)
    for axis_at, shards_of in pieces:
        steps = jnp.exp(jax.random.uniform(jax.random.fold_in(own, axis_at), (shards_of,), jnp.float32, smallest / len(pieces), high / len(pieces)))
        level = level * jnp.repeat(steps, dims[axis_at] // shards_of).reshape([-1 if axis == axis_at else 1 for axis in range(len(dims))])
    return level


def bell_draw(rng, extent, spread, most, pieces=(), kind=jnp.bfloat16):
    result = jax.random.normal(rng, extent, jnp.float32) * spread
    if len(pieces) > 0:
        result = block_levels(rng, extent, pieces, -0.22, 0.18) * result
    return jnp.clip(result, min=-most, max=most).astype(kind)


def setup_inputs(seed: int = 0) -> dict:
    splits = jax.random.split(jax.random.key(seed), 12)
    q_one = draw_q_one(jax.random.fold_in(splits[11], 71), 0)
    k_one = bell_draw(splits[1], (SEQ, CH), 1.0, 6.0, ((0, 8), (1, 4)))
    v_one = bell_draw(splits[2], (SEQ, CH), 1.0, 6.0, ((0, 8), (1, 4)))
    q_two = bell_draw(splits[3], (SEQ, CH), 1.0, 6.0, ((0, 8), (1, 4)))
    k_two = bell_draw(splits[4], (SEQ, CH), 1.0, 6.0, ((0, 8), (1, 4)))
    short_taps = bell_draw(splits[5], (3, SE, GROUPS), SE ** -0.5, 2.0, ((2, 4),))
    medium_taps = bell_draw(splits[6], (MR, GROUPS), MR ** -0.5, 0.5, ((1, 4),))
    long_taps = bell_draw(splits[7], (GROUPS, SEQ), SEQ ** -0.5, 0.125, ((0, 4), (1, 8)))
    skip_gain = bell_draw(splits[8], (CH,), 1.0, 4.0, ((0, 4),), jnp.float32)
    block_order = draw_block_order(jax.random.fold_in(splits[11], 71), 0)
    prev_owner = draw_prev_owner(jax.random.fold_in(splits[11], 71), 0)
    return {"q_one": q_one, "k_one": k_one, "v_one": v_one, "q_two": q_two, "k_two": k_two, "short_taps": short_taps, "medium_taps": medium_taps, "long_taps": long_taps, "skip_gain": skip_gain, "block_order": block_order, "prev_owner": prev_owner}


EPSILON = 1e-06
BLOCK_LANES = 256

def causal_filter(padded, kernel_taps):
    reach = kernel_taps.shape[0] - 1

    def add_tap(j, total):
        piece = lax.dynamic_slice_in_dim(padded, reach - j, T_DEV, axis=1).astype(jnp.float32)
        return total + piece * kernel_taps[j].astype(jnp.float32)[None, None, :]
    start_total = jnp.zeros((padded.shape[0], T_DEV, padded.shape[2]), jnp.float32)
    return lax.fori_loop(0, reach + 1, add_tap, start_total)

def with_before(blocks, source, first_block, count):
    before = blocks[source][:, T_DEV - count:]
    before = jnp.where(first_block[:, None, None], jnp.zeros_like(before), before)
    return jnp.concatenate([before, blocks], axis=1)

def long_group(group_item):
    group_taps, group_rows = group_item
    padded_len = 2 * SEQ
    spectrum = jnp.fft.rfft(group_rows, n=padded_len, axis=1) * jnp.fft.rfft(group_taps, n=padded_len)[None, :]
    return jnp.fft.irfft(spectrum, n=padded_len, axis=1)[:, :SEQ]

def reference(q_one, k_one, v_one, q_two, k_two, short_taps, medium_taps, long_taps, skip_gain, block_order, prev_owner):
    block_shape = (N_CTX, T_DEV, CH)
    col_count = CH // BLOCK_LANES
    group_count = BLOCK_LANES // GROUP
    source = prev_owner[block_order]
    first_block = block_order == 0
    short_lanes = jnp.repeat(short_taps, GROUP, axis=2)
    medium_lanes = jnp.repeat(medium_taps, GROUP, axis=1)
    q_blocks = q_one.reshape(block_shape)
    k_blocks = k_one.reshape(block_shape)
    v_blocks = v_one.reshape(block_shape)
    gate_blocks = k_two.reshape(block_shape)
    out_gate = q_two.reshape(block_shape)

    def lanes_of(array, start):
        return lax.dynamic_slice_in_dim(array, start, BLOCK_LANES, axis=2)

    def mixed_block(col):
        start = col * BLOCK_LANES
        short_here = lax.dynamic_slice_in_dim(short_lanes, start, BLOCK_LANES, axis=2)
        medium_here = lax.dynamic_slice_in_dim(medium_lanes, start, BLOCK_LANES, axis=1)
        q_feat = causal_filter(with_before(lanes_of(q_blocks, start), source, first_block, SE - 1), short_here[0])
        k_feat = causal_filter(with_before(lanes_of(k_blocks, start), source, first_block, SE - 1), short_here[1])
        v_feat = causal_filter(with_before(lanes_of(v_blocks, start), source, first_block, SE - 1), short_here[2])
        z_one = (k_feat * v_feat).astype(jnp.bfloat16)
        medium = causal_filter(with_before(z_one, source, first_block, MR - 1), medium_here)
        return q_feat * medium
    mixed_all = lax.map(mixed_block, jnp.arange(col_count, dtype=jnp.int32))
    energy = lax.optimization_barrier(jnp.sum(lax.optimization_barrier(jnp.sum(mixed_all * mixed_all, axis=3)), axis=0))
    scale = lax.rsqrt(energy / CH + EPSILON)[:, :, None]
    holder = jnp.argsort(block_order).astype(jnp.int32)

    def output_block(item):
        col, mixed = item
        start = col * BLOCK_LANES
        v_two = (lanes_of(gate_blocks, start).astype(jnp.float32) * mixed * scale).astype(jnp.bfloat16)
        ordered = v_two[holder].reshape(SEQ, BLOCK_LANES)
        lanes = jnp.transpose(ordered).astype(jnp.float32).reshape(group_count, GROUP, SEQ)
        taps_here = lax.dynamic_slice_in_dim(long_taps, col * group_count, group_count, axis=0).astype(jnp.float32)
        long_part = lax.map(long_group, (taps_here, lanes))
        long_part = jnp.transpose(long_part.reshape(BLOCK_LANES, SEQ))
        gain_here = lax.dynamic_slice_in_dim(skip_gain, start, BLOCK_LANES)
        mixed_seq = (long_part + gain_here[None, :] * ordered.astype(jnp.float32)).astype(jnp.bfloat16)
        placed = mixed_seq.reshape(N_CTX, T_DEV, BLOCK_LANES)[block_order]
        return (lanes_of(out_gate, start).astype(jnp.float32) * placed.astype(jnp.float32)).astype(jnp.bfloat16)
    outputs = lax.map(output_block, (jnp.arange(col_count, dtype=jnp.int32), mixed_all))
    return jnp.transpose(outputs, (1, 2, 0, 3)).reshape(SEQ, CH)
```

```python
import jax
import jax.numpy as jnp
from jax import lax
from jax.experimental import pallas as pl
from jax.experimental.pallas import tpu as pltpu
from jax.sharding import PartitionSpec as P

EPSILON = 1e-06
LANES = 128
EDGE = 8
VMEM_BYTES = 56 * 1024 * 1024


def params(*semantics):
    return pltpu.CompilerParams(dimension_semantics=semantics, vmem_limit_bytes=VMEM_BYTES)


def short_filter(extended, taps, start, rows):
    total = extended[start : start + rows] * taps[0:1]
    for j in range(1, taps.shape[0]):
        total = total + extended[start - j : start - j + rows] * taps[j : j + 1]
    return total


def tail_kernel(q_ref, k_ref, v_ref, taps_ref, out_ref):
    rows = q_ref.shape[0]
    reach = out_ref.shape[1] - 4 * EDGE
    first = rows - reach - 16
    k_part = k_ref[first:, :].astype(jnp.float32)
    v_part = v_ref[first:, :].astype(jnp.float32)
    k_feat = short_filter(k_part, taps_ref[1], 16, reach)
    v_feat = short_filter(v_part, taps_ref[2], 16, reach)
    out_ref[0, :reach, :] = (k_feat * v_feat).astype(jnp.bfloat16)
    q_part = q_ref[rows - 16 :, :].astype(jnp.float32)
    edges = jnp.concatenate(
        [q_part[16 - EDGE :], k_part[-EDGE:], v_part[-EDGE:], jnp.zeros((EDGE, LANES), jnp.float32)],
        axis=0,
    )
    out_ref[0, reach:, :] = edges.astype(jnp.bfloat16)


def medium_table_kernel(base_ref, out_ref):
    reach, wide = out_ref.shape[1], base_ref.shape[2]
    for g in range(base_ref.shape[1]):
        row = jnp.broadcast_to(base_ref[0, g : g + 1, :], (reach, wide))
        out_ref[0, :, g * wide : (g + 1) * wide] = pltpu.roll(
            row, 0, 1, stride=1, stride_axis=0
        ).astype(jnp.bfloat16)


def long_table_kernel(base_ref, out_ref):
    lags, rows, _ = out_ref.shape[1:]
    strip = jnp.broadcast_to(base_ref[0], (rows, base_ref.shape[2]))
    strip = pltpu.roll(strip, 0, 1, stride=1, stride_axis=0)
    for lag in range(lags):
        out_ref[0, lag] = strip[:, (lag + 1) * rows : (lag + 2) * rows].astype(jnp.bfloat16)


def mix_kernel(
    first_ref, q_ref, k_ref, v_ref, gate_ref, halo_ref, taps_ref, table_ref, out_ref, energy_ref, squares_ref
):
    rows = q_ref.shape[0]
    reach = table_ref.shape[1]
    tile = pl.program_id(0)
    keep = jnp.where(first_ref[0] != 0, 0.0, 1.0)
    edges = halo_ref[0, reach:, :].astype(jnp.float32) * keep

    def feature(ref, which):
        extended = jnp.concatenate(
            [edges[which * EDGE : (which + 1) * EDGE], ref[...].astype(jnp.float32)], axis=0
        )
        return short_filter(extended, taps_ref[which], EDGE, rows)

    q_feat = feature(q_ref, 0)
    z_own = (feature(k_ref, 1) * feature(v_ref, 2)).astype(jnp.bfloat16)
    z_halo = (halo_ref[0, :reach, :].astype(jnp.float32) * keep).astype(jnp.bfloat16)
    window = jnp.concatenate(
        [jnp.concatenate([z_halo, z_own[:reach]], axis=0), z_own], axis=1
    )
    wide = window.shape[0]
    groups = table_ref.shape[2] // wide
    lane_group = lax.broadcasted_iota(jnp.int32, (1, 2 * LANES), 1) % LANES // (LANES // groups)
    medium = jnp.zeros((reach, 2 * LANES), jnp.float32)
    for g in range(groups):
        masked = window * (lane_group == g).astype(jnp.bfloat16)
        medium = medium + jnp.dot(
            table_ref[0, :, g * wide : (g + 1) * wide], masked, preferred_element_type=jnp.float32
        )
    mixed = q_feat * jnp.concatenate([medium[:, :LANES], medium[:, LANES:]], axis=0)
    out_ref[0] = jnp.transpose(mixed * gate_ref[...].astype(jnp.float32))

    @pl.when(tile == 0)
    def _():
        squares_ref[...] = mixed * mixed

    @pl.when(tile != 0)
    def _():
        squares_ref[...] += mixed * mixed

    @pl.when(tile == pl.num_programs(0) - 1)
    def _():
        energy_ref[...] = jnp.sum(jnp.transpose(squares_ref[...]), axis=0, keepdims=True)


def long_kernel(holder_ref, value_ref, table_ref, gain_ref, out_ref, ordered_ref, total_ref):
    blocks, size, rows = value_ref.shape
    lags = table_ref.shape[1]
    piece = pl.program_id(1)
    reach = blocks * size

    @pl.when(piece == 0)
    def _():
        ordered_ref[:reach] = jnp.zeros((reach, rows), jnp.bfloat16)
        for b in range(blocks):
            ordered_ref[reach + b * size : reach + (b + 1) * size] = value_ref[holder_ref[b]]
        total_ref[...] = ordered_ref[reach:].astype(jnp.float32) * gain_ref[0]

    def lagged(lag):
        if lags == blocks:
            return ordered_ref[(blocks - lag) * size : (2 * blocks - lag) * size]
        start = pl.multiple_of((blocks - piece * lags - lag) * size, size)
        return ordered_ref[pl.ds(start, reach)]

    left = jnp.concatenate([lagged(lag) for lag in range(lags)], axis=1)
    right = table_ref[0].reshape(lags * rows, rows)
    total_ref[...] += jnp.dot(left, right, preferred_element_type=jnp.float32)

    @pl.when(piece == pl.num_programs(1) - 1)
    def _():
        for b in range(blocks):
            out_ref[holder_ref[b]] = total_ref[b * size : (b + 1) * size].astype(jnp.bfloat16)


def gate_kernel(mixed_ref, gate_ref, out_ref):
    mixed = jnp.transpose(mixed_ref[0].astype(jnp.float32))
    out_ref[...] = (gate_ref[...].astype(jnp.float32) * mixed).astype(jnp.bfloat16)


def per_device(
    q_one,
    k_one,
    v_one,
    q_two,
    k_two,
    short_taps,
    medium_taps,
    long_taps,
    skip_gain,
    block_order,
    prev_owner,
):
    rows, width = q_one.shape
    ctx_count = lax.axis_size("ctx")
    tp_count = lax.axis_size("tp")
    me = lax.axis_index("ctx")
    local_groups = short_taps.shape[2]
    size = width // local_groups
    reach = medium_taps.shape[0]
    assert rows == 2 * reach and short_taps.shape[1] <= EDGE + 1
    tiles = width // LANES
    tile_groups = LANES // size
    shard = width // ctx_count
    shard_groups = shard // size
    full_width = width * tp_count

    slots = jnp.arange(ctx_count, dtype=jnp.int32)
    holder = jnp.sum(jnp.where(block_order[None, :] == slots[:, None], slots[None, :], 0), axis=1)
    source = jnp.take(prev_owner, block_order, mode="clip")
    is_first = (lax.dynamic_slice_in_dim(block_order, me, 1) == 0).astype(jnp.int32)
    short_lanes = jnp.repeat(short_taps, size, axis=2).astype(jnp.float32)

    column = pl.BlockSpec((rows, LANES), lambda i: (0, i))
    taps_spec = pl.BlockSpec((3, short_taps.shape[1], LANES), lambda i: (0, 0, i))
    tail_rows = reach + 4 * EDGE
    tail_spec = pl.BlockSpec((1, tail_rows, LANES), lambda i: (i, 0, 0))
    turned_spec = pl.BlockSpec((1, LANES, rows), lambda i: (i, 0, 0))

    tails = pl.pallas_call(
        tail_kernel,
        grid=(tiles,),
        in_specs=[column, column, column, taps_spec],
        out_specs=tail_spec,
        out_shape=jax.ShapeDtypeStruct((tiles, tail_rows, LANES), jnp.bfloat16),
        compiler_params=params("arbitrary"),
        name="tails",
    )(q_one, k_one, v_one, short_lanes)
    halo_rows = tiles * tail_rows // ctx_count
    taps_rows = shard_groups * rows // LANES
    payload = jnp.concatenate(
        [
            tails.reshape(ctx_count, halo_rows, LANES),
            long_taps.reshape(ctx_count, taps_rows, LANES),
        ],
        axis=1,
    )
    spread = lax.all_to_all(payload, "ctx", split_axis=0, concat_axis=0, tiled=True)
    routed = jnp.take(spread[:, :halo_rows], source, axis=0, mode="clip")
    halo = lax.all_to_all(routed, "ctx", split_axis=0, concat_axis=0, tiled=True)
    halo = halo.reshape(tiles, tail_rows, LANES)

    base = jnp.pad(jnp.transpose(medium_taps[::-1]), ((0, 0), (1, rows - reach - 1)))
    medium_table = pl.pallas_call(
        medium_table_kernel,
        grid=(tiles,),
        in_specs=[pl.BlockSpec((1, tile_groups, rows), lambda i: (i, 0, 0))],
        out_specs=pl.BlockSpec((1, reach, tile_groups * rows), lambda i: (i, 0, 0)),
        out_shape=jax.ShapeDtypeStruct((tiles, reach, tile_groups * rows), jnp.bfloat16),
        compiler_params=params("arbitrary"),
        name="medium_table",
    )(base.astype(jnp.float32).reshape(tiles, tile_groups, rows))

    lags = min(ctx_count, 8)
    pieces = ctx_count // lags
    long_rows = jnp.transpose(
        spread[:, halo_rows:].reshape(ctx_count, shard_groups, rows), (1, 0, 2)
    ).reshape(shard_groups, ctx_count * rows)
    long_rows = jnp.pad(long_rows.astype(jnp.float32), ((0, 0), (rows, 0)))
    windows = jnp.stack(
        [long_rows[:, p * lags * rows : (p * lags + lags + 1) * rows] for p in range(pieces)], axis=1
    ).reshape(shard_groups * pieces, 1, (lags + 1) * rows)
    long_table = pl.pallas_call(
        long_table_kernel,
        grid=(shard_groups * pieces,),
        in_specs=[pl.BlockSpec((1, 1, (lags + 1) * rows), lambda i: (i, 0, 0))],
        out_specs=pl.BlockSpec((1, lags, rows, rows), lambda i: (i, 0, 0, 0)),
        out_shape=jax.ShapeDtypeStruct((shard_groups * pieces, lags, rows, rows), jnp.bfloat16),
        compiler_params=params("arbitrary"),
        name="long_table",
    )(windows)

    gated, energy = pl.pallas_call(
        mix_kernel,
        grid=(tiles,),
        in_specs=[
            pl.BlockSpec(memory_space=pltpu.SMEM),
            column,
            column,
            column,
            column,
            tail_spec,
            taps_spec,
            pl.BlockSpec((1, reach, tile_groups * rows), lambda i: (i, 0, 0)),
        ],
        out_specs=[turned_spec, pl.BlockSpec((1, rows), lambda i: (0, 0))],
        out_shape=[
            jax.ShapeDtypeStruct((tiles, LANES, rows), jnp.float32),
            jax.ShapeDtypeStruct((1, rows), jnp.float32),
        ],
        scratch_shapes=[pltpu.VMEM((rows, LANES), jnp.float32)],
        compiler_params=params("arbitrary"),
        name="mix",
    )(is_first, q_one, k_one, v_one, k_two, halo, short_lanes, medium_table)

    total = energy
    for step in range(1, tp_count):
        total = total + lax.ppermute(
            energy, "tp", [(i, (i + step) % tp_count) for i in range(tp_count)]
        )
    scale = lax.rsqrt(total / full_width + EPSILON)
    values = (gated * scale[None]).astype(jnp.bfloat16).reshape(ctx_count, shard, rows)
    values = lax.all_to_all(values, "ctx", split_axis=0, concat_axis=0, tiled=True)

    gain = lax.dynamic_slice_in_dim(skip_gain, me * shard, shard).reshape(shard_groups, 1, size, 1)
    gain = jnp.broadcast_to(gain, (shard_groups, ctx_count, size, 1))
    gain = gain.reshape(shard_groups, ctx_count * size, 1)
    group_spec = pl.BlockSpec((ctx_count, size, rows), lambda g, p, order: (0, g, 0))
    long_out = pl.pallas_call(
        long_kernel,
        grid_spec=pltpu.PrefetchScalarGridSpec(
            num_scalar_prefetch=1,
            grid=(shard_groups, pieces),
            in_specs=[
                group_spec,
                pl.BlockSpec(
                    (1, lags, rows, rows), lambda g, p, order: (g * pieces + p, 0, 0, 0)
                ),
                pl.BlockSpec((1, ctx_count * size, 1), lambda g, p, order: (g, 0, 0)),
            ],
            out_specs=group_spec,
            scratch_shapes=[
                pltpu.VMEM((2 * ctx_count * size, rows), jnp.bfloat16),
                pltpu.VMEM((ctx_count * size, rows), jnp.float32),
            ],
        ),
        out_shape=jax.ShapeDtypeStruct((ctx_count, shard, rows), jnp.bfloat16),
        compiler_params=params("arbitrary", "arbitrary"),
        name="long",
    )(holder, values, long_table, gain)
    returned = lax.all_to_all(long_out, "ctx", split_axis=0, concat_axis=0, tiled=True)

    return pl.pallas_call(
        gate_kernel,
        grid=(tiles,),
        in_specs=[turned_spec, column],
        out_specs=column,
        out_shape=jax.ShapeDtypeStruct((rows, width), jnp.bfloat16),
        compiler_params=params("arbitrary"),
        name="gate",
    )(returned.reshape(tiles, LANES, rows), q_two)


def solution(mesh):
    in_specs = (
        P("ctx", "tp"),
        P("ctx", "tp"),
        P("ctx", "tp"),
        P("ctx", "tp"),
        P("ctx", "tp"),
        P(None, None, "tp"),
        P(None, "tp"),
        P("tp", "ctx"),
        P("tp"),
        P(),
        P(),
    )
    out_specs = P("ctx", "tp")
    return jax.shard_map(
        per_device, mesh=mesh, in_specs=in_specs, out_specs=out_specs, check_vma=False
    )
```

```python
import jax
import jax.numpy as jnp
from jax import lax
from jax.experimental import pallas as pl
from jax.experimental.pallas import tpu as pltpu
from jax.sharding import PartitionSpec as P

EPSILON = 1e-06
LANES = 128
EDGE = 8
VMEM_BYTES = 24 * 1024 * 1024
TAIL_TILES = 4
MIX_TILES = 2
GATE_TILES = 4
F32 = jnp.float32
BF16 = jnp.bfloat16


def params(*semantics):
    return pltpu.CompilerParams(dimension_semantics=semantics, vmem_limit_bytes=VMEM_BYTES)


def lane_taps(taps_ref, which, size, width):
    groups = taps_ref.shape[2]
    group = lax.broadcasted_iota(jnp.int32, (groups, width), 0)
    lane = lax.broadcasted_iota(jnp.int32, (groups, width), 1) + pl.program_id(0) * width
    spread = (group == lane // size).astype(BF16)
    return jnp.dot(taps_ref[which], spread, preferred_element_type=F32)


def short_filter(extended, taps, start, rows):
    total = extended[start : start + rows] * taps[0:1]
    for j in range(1, taps.shape[0]):
        total = total + extended[start - j : start - j + rows] * taps[j : j + 1]
    return total


def tail_kernel(size, reach, q_ref, k_ref, v_ref, taps_ref, *rest):
    out_ref = rest[-1]
    rows, width = q_ref.shape
    first = rows - reach - 16
    k_part = k_ref[first:, :].astype(F32)
    v_part = v_ref[first:, :].astype(F32)
    q_part = q_ref[rows - 16 :, :].astype(F32)
    k_feat = short_filter(k_part, lane_taps(taps_ref, 1, size, width), 16, reach)
    v_feat = short_filter(v_part, lane_taps(taps_ref, 2, size, width), 16, reach)
    z_tail = (k_feat * v_feat).astype(BF16)
    edges = jnp.concatenate(
        [q_part[16 - EDGE :], k_part[-EDGE:], v_part[-EDGE:], jnp.zeros((EDGE, width), F32)], axis=0
    ).astype(BF16)
    for t in range(width // LANES):
        lanes = slice(t * LANES, (t + 1) * LANES)
        out_ref[t, :reach, :] = z_tail[:, lanes]
        out_ref[t, reach : reach + 4 * EDGE, :] = edges[:, lanes]
        if len(rest) == 2:
            out_ref[t, reach + 4 * EDGE :, :] = rest[0][t]


def call_tails(q_one, k_one, v_one, short_taps, reach, extra):
    rows, width = q_one.shape
    tiles = width // LANES
    size = width // short_taps.shape[2]
    wide = TAIL_TILES * LANES
    column = pl.BlockSpec((rows, wide), lambda i: (0, i))
    inputs = [q_one, k_one, v_one, short_taps]
    in_specs = [column, column, column, pl.BlockSpec(short_taps.shape, lambda i: (0, 0, 0))]
    out_rows = reach + 4 * EDGE
    if extra is not None:
        inputs.append(extra)
        in_specs.append(pl.BlockSpec((TAIL_TILES,) + extra.shape[1:], lambda i: (i, 0, 0)))
        out_rows += extra.shape[1]

    def kernel(*refs):
        tail_kernel(size, reach, *refs)

    return pl.pallas_call(
        kernel,
        grid=(tiles // TAIL_TILES,),
        in_specs=in_specs,
        out_specs=pl.BlockSpec((TAIL_TILES, out_rows, LANES), lambda i: (i, 0, 0)),
        out_shape=jax.ShapeDtypeStruct((tiles, out_rows, LANES), BF16),
        compiler_params=params("arbitrary"),
        name="tails",
    )(*inputs)


def route_kernel(order_ref, owner_ref, spread_ref, out_ref):
    kept = out_ref.shape[1]
    for d in range(out_ref.shape[0]):
        out_ref[d] = spread_ref[owner_ref[order_ref[d]], :kept, :]


def call_route(block_order, prev_owner, spread, kept):
    count, _, lanes = spread.shape
    return pl.pallas_call(
        route_kernel,
        in_specs=[
            pl.BlockSpec(memory_space=pltpu.SMEM),
            pl.BlockSpec(memory_space=pltpu.SMEM),
            pl.BlockSpec(memory_space=pltpu.VMEM),
        ],
        out_specs=pl.BlockSpec(memory_space=pltpu.VMEM),
        out_shape=jax.ShapeDtypeStruct((count, kept, lanes), BF16),
        compiler_params=params(),
        name="route",
    )(block_order, prev_owner, spread)


def medium_table_kernel(base_ref, out_ref):
    reach, wide = out_ref.shape[2], base_ref.shape[2]
    for g in range(base_ref.shape[1]):
        row = jnp.broadcast_to(base_ref[0, g : g + 1, :], (reach, wide))
        out_ref[0, g] = pltpu.roll(row, 0, 1, stride=1, stride_axis=0).astype(BF16)


def call_medium_table(medium_taps, tile_groups, rows):
    reach, groups = medium_taps.shape
    tiles = groups // tile_groups
    base = jnp.pad(jnp.transpose(medium_taps[::-1]), ((0, 0), (1, rows - reach - 1)))
    return pl.pallas_call(
        medium_table_kernel,
        grid=(tiles,),
        in_specs=[pl.BlockSpec((1, tile_groups, rows), lambda i: (i, 0, 0))],
        out_specs=pl.BlockSpec((1, tile_groups, reach, rows), lambda i: (i, 0, 0, 0)),
        out_shape=jax.ShapeDtypeStruct((tiles, tile_groups, reach, rows), BF16),
        compiler_params=params("arbitrary"),
        name="medium_table",
    )(base.astype(F32).reshape(tiles, tile_groups, rows))


def long_table_kernel(base_ref, out_ref):
    lags, rows, _ = out_ref.shape[1:]
    strip = jnp.broadcast_to(base_ref[0], (rows, base_ref.shape[2]))
    strip = pltpu.roll(strip, 0, 1, stride=1, stride_axis=0)
    for lag in range(lags):
        out_ref[0, lag] = strip[:, (lag + 1) * rows : (lag + 2) * rows].astype(BF16)


def call_long_table(long_rows, rows, lags):
    groups, length = long_rows.shape
    pieces = length // (lags * rows)
    padded = jnp.pad(long_rows.astype(F32), ((0, 0), (rows, 0)))
    windows = jnp.stack(
        [padded[:, p * lags * rows : (p * lags + lags + 1) * rows] for p in range(pieces)], axis=1
    ).reshape(groups * pieces, 1, (lags + 1) * rows)
    return pl.pallas_call(
        long_table_kernel,
        grid=(groups * pieces,),
        in_specs=[pl.BlockSpec((1, 1, (lags + 1) * rows), lambda i: (i, 0, 0))],
        out_specs=pl.BlockSpec((1, lags, rows, rows), lambda i: (i, 0, 0, 0)),
        out_shape=jax.ShapeDtypeStruct((groups * pieces, lags, rows, rows), BF16),
        compiler_params=params("arbitrary"),
        name="long_table",
    )(windows)


def mix_kernel(
    size, first_ref, q_ref, k_ref, v_ref, gate_ref, halo_ref, taps_ref, table_ref, out_ref, energy_ref, squares_ref
):
    rows, width = q_ref.shape
    tiles, groups, reach, wide = table_ref.shape
    step = pl.program_id(0)
    keep = jnp.where(first_ref[0] != 0, 0.0, 1.0)
    taps = [lane_taps(taps_ref, which, size, width) for which in range(3)]
    lane_group = lax.broadcasted_iota(jnp.int32, (1, 2 * LANES), 1) % LANES // size
    squares = jnp.zeros((rows, LANES), F32)
    for t in range(tiles):
        lanes = slice(t * LANES, (t + 1) * LANES)
        edges = halo_ref[t, reach:, :].astype(F32) * keep

        def feature(ref, which):
            extended = jnp.concatenate(
                [edges[which * EDGE : (which + 1) * EDGE], ref[:, lanes].astype(F32)], axis=0
            )
            return short_filter(extended, taps[which][:, lanes], EDGE, rows)

        q_feat = feature(q_ref, 0)
        z_own = (feature(k_ref, 1) * feature(v_ref, 2)).astype(BF16)
        z_halo = (halo_ref[t, :reach, :].astype(F32) * keep).astype(BF16)
        window = jnp.concatenate([jnp.concatenate([z_halo, z_own[:reach]], axis=0), z_own], axis=1)
        every = jnp.dot(
            table_ref[t].reshape(groups * reach, wide), window, preferred_element_type=F32
        )
        medium = every[:reach]
        for g in range(1, groups):
            medium = jnp.where(lane_group == g, every[g * reach : (g + 1) * reach], medium)
        mixed = q_feat * jnp.concatenate([medium[:, :LANES], medium[:, LANES:]], axis=0)
        out_ref[t] = jnp.transpose(mixed * gate_ref[:, lanes].astype(F32))
        squares = squares + mixed * mixed

    @pl.when(step == 0)
    def _():
        squares_ref[...] = squares

    @pl.when(step != 0)
    def _():
        squares_ref[...] += squares

    @pl.when(step == pl.num_programs(0) - 1)
    def _():
        energy_ref[...] = jnp.sum(jnp.transpose(squares_ref[...]), axis=0, keepdims=True)


def call_mix(is_first, q_one, k_one, v_one, k_two, halo, short_taps, medium_table):
    rows, width = q_one.shape
    size = width // short_taps.shape[2]
    wide = MIX_TILES * LANES
    column = pl.BlockSpec((rows, wide), lambda i: (0, i))

    def kernel(*refs):
        mix_kernel(size, *refs)

    return pl.pallas_call(
        kernel,
        grid=(width // wide,),
        in_specs=[
            pl.BlockSpec(memory_space=pltpu.SMEM),
            column,
            column,
            column,
            column,
            pl.BlockSpec((MIX_TILES,) + halo.shape[1:], lambda i: (i, 0, 0)),
            pl.BlockSpec(short_taps.shape, lambda i: (0, 0, 0)),
            pl.BlockSpec((MIX_TILES,) + medium_table.shape[1:], lambda i: (i, 0, 0, 0)),
        ],
        out_specs=[
            pl.BlockSpec((MIX_TILES, LANES, rows), lambda i: (i, 0, 0)),
            pl.BlockSpec((1, rows), lambda i: (0, 0)),
        ],
        out_shape=[
            jax.ShapeDtypeStruct((width // LANES, LANES, rows), F32),
            jax.ShapeDtypeStruct((1, rows), F32),
        ],
        scratch_shapes=[pltpu.VMEM((rows, LANES), F32)],
        compiler_params=params("arbitrary"),
        name="mix",
    )(is_first, q_one, k_one, v_one, k_two, halo, short_taps, medium_table)


def long_kernel(holder_ref, value_ref, table_ref, gain_ref, out_ref, ordered_ref, total_ref):
    blocks, size, rows = value_ref.shape
    lags = table_ref.shape[1]
    piece = pl.program_id(1)
    reach = blocks * size

    @pl.when(piece == 0)
    def _():
        ordered_ref[:reach] = jnp.zeros((reach, rows), BF16)
        for b in range(blocks):
            ordered_ref[reach + b * size : reach + (b + 1) * size] = value_ref[holder_ref[b]]
        total_ref[...] = ordered_ref[reach:].astype(F32) * gain_ref[0]

    def lagged(lag):
        if lags == blocks:
            return ordered_ref[(blocks - lag) * size : (2 * blocks - lag) * size]
        start = pl.multiple_of((blocks - piece * lags - lag) * size, size)
        return ordered_ref[pl.ds(start, reach)]

    left = jnp.concatenate([lagged(lag) for lag in range(lags)], axis=1)
    right = table_ref[0].reshape(lags * rows, rows)
    total_ref[...] += jnp.dot(left, right, preferred_element_type=F32)

    @pl.when(piece == pl.num_programs(1) - 1)
    def _():
        for b in range(blocks):
            out_ref[holder_ref[b]] = total_ref[b * size : (b + 1) * size].astype(BF16)


def call_long(holder, values, long_table, gain, size):
    blocks, channels, rows = values.shape
    lags = long_table.shape[1]
    groups = channels // size
    pieces = blocks // lags
    group_spec = pl.BlockSpec((blocks, size, rows), lambda g, p, order: (0, g, 0))
    return pl.pallas_call(
        long_kernel,
        grid_spec=pltpu.PrefetchScalarGridSpec(
            num_scalar_prefetch=1,
            grid=(groups, pieces),
            in_specs=[
                group_spec,
                pl.BlockSpec(
                    (1, lags, rows, rows), lambda g, p, order: (g * pieces + p, 0, 0, 0)
                ),
                pl.BlockSpec((1, blocks * size, 1), lambda g, p, order: (g, 0, 0)),
            ],
            out_specs=group_spec,
            scratch_shapes=[
                pltpu.VMEM((2 * blocks * size, rows), BF16),
                pltpu.VMEM((blocks * size, rows), F32),
            ],
        ),
        out_shape=jax.ShapeDtypeStruct((blocks, channels, rows), BF16),
        compiler_params=params("arbitrary", "arbitrary"),
        name="long",
    )(holder, values, long_table, gain)


def gate_kernel(mixed_ref, gate_ref, out_ref):
    for t in range(mixed_ref.shape[0]):
        lanes = slice(t * LANES, (t + 1) * LANES)
        mixed = jnp.transpose(mixed_ref[t]).astype(F32)
        out_ref[:, lanes] = (gate_ref[:, lanes].astype(F32) * mixed).astype(BF16)


def call_gate(mixed, q_two):
    rows, width = q_two.shape
    wide = GATE_TILES * LANES
    column = pl.BlockSpec((rows, wide), lambda i: (0, i))
    return pl.pallas_call(
        gate_kernel,
        grid=(width // wide,),
        in_specs=[pl.BlockSpec((GATE_TILES, LANES, rows), lambda i: (i, 0, 0)), column],
        out_specs=column,
        out_shape=jax.ShapeDtypeStruct((rows, width), BF16),
        compiler_params=params("arbitrary"),
        name="gate",
    )(mixed, q_two)


def exchange(array):
    return lax.all_to_all(array, "ctx", split_axis=0, concat_axis=0, tiled=True)


def per_device(
    q_one,
    k_one,
    v_one,
    q_two,
    k_two,
    short_taps,
    medium_taps,
    long_taps,
    skip_gain,
    block_order,
    prev_owner,
):
    rows, width = q_one.shape
    ctx_count = lax.axis_size("ctx")
    tp_count = lax.axis_size("tp")
    me = lax.axis_index("ctx")
    size = width // short_taps.shape[2]
    reach = medium_taps.shape[0]
    assert rows == 2 * reach and short_taps.shape[1] <= EDGE + 1
    tiles = width // LANES
    shard = width // ctx_count
    shard_groups = shard // size
    full_width = width * tp_count

    slots = jnp.arange(ctx_count, dtype=jnp.int32)
    holder = jnp.sum(jnp.where(block_order[None, :] == slots[:, None], slots[None, :], 0), axis=1)
    is_first = (lax.dynamic_slice_in_dim(block_order, me, 1) == 0).astype(jnp.int32)

    tail_rows = reach + 4 * EDGE
    halo_rows = tiles * tail_rows // ctx_count
    taps_sent = long_taps.reshape(ctx_count, shard_groups * rows // LANES, LANES)
    if ctx_count == tiles:
        payload = call_tails(q_one, k_one, v_one, short_taps, reach, taps_sent)
    else:
        tails = call_tails(q_one, k_one, v_one, short_taps, reach, None)
        payload = jnp.concatenate([tails.reshape(ctx_count, halo_rows, LANES), taps_sent], axis=1)
    spread = exchange(payload)
    halo = exchange(call_route(block_order, prev_owner, spread, halo_rows))
    halo = halo.reshape(tiles, tail_rows, LANES)

    medium_table = call_medium_table(medium_taps, LANES // size, rows)
    long_rows = jnp.transpose(
        spread[:, halo_rows:].reshape(ctx_count, shard_groups, rows), (1, 0, 2)
    ).reshape(shard_groups, ctx_count * rows)
    long_table = call_long_table(long_rows, rows, min(ctx_count, 8))

    gated, energy = call_mix(is_first, q_one, k_one, v_one, k_two, halo, short_taps, medium_table)
    total = energy
    for step in range(1, tp_count):
        total = total + lax.ppermute(
            energy, "tp", [(i, (i + step) % tp_count) for i in range(tp_count)]
        )
    scale = lax.rsqrt(total / full_width + EPSILON)
    values = (gated * scale[None]).astype(BF16).reshape(ctx_count, shard, rows)
    values = exchange(values)

    gain = lax.dynamic_slice_in_dim(skip_gain, me * shard, shard).reshape(shard_groups, 1, size, 1)
    gain = jnp.broadcast_to(gain, (shard_groups, ctx_count, size, 1))
    gain = gain.reshape(shard_groups, ctx_count * size, 1)
    returned = exchange(call_long(holder, values, long_table, gain, size))
    return call_gate(returned.reshape(tiles, LANES, rows), q_two)


def solution(mesh):
    in_specs = (
        P("ctx", "tp"),
        P("ctx", "tp"),
        P("ctx", "tp"),
        P("ctx", "tp"),
        P("ctx", "tp"),
        P(None, None, "tp"),
        P(None, "tp"),
        P("tp", "ctx"),
        P("tp"),
        P(),
        P(),
    )
    out_specs = P("ctx", "tp")
    return jax.shard_map(
        per_device, mesh=mesh, in_specs=in_specs, out_specs=out_specs, check_vma=False
    )
```

```python
import jax
import jax.numpy as jnp
from jax import lax
from jax.experimental import pallas as pl
from jax.experimental.pallas import tpu as pltpu
from jax.sharding import PartitionSpec as P

EPSILON = 1e-06
LANES = 128
EDGE = 8
VMEM_BYTES = 24 * 1024 * 1024
TAIL_TILES = 2
GATE_TILES = 4
F32 = jnp.float32
BF16 = jnp.bfloat16


def params(*semantics):
    return pltpu.CompilerParams(dimension_semantics=semantics, vmem_limit_bytes=VMEM_BYTES)


def in_vmem(array):
    return pltpu.with_memory_space_constraint(array, pltpu.VMEM)


def lane_taps(taps_ref, which, size, width, first=0):
    groups = taps_ref.shape[2]
    group = lax.broadcasted_iota(jnp.int32, (groups, width), 0)
    lane = lax.broadcasted_iota(jnp.int32, (groups, width), 1) + first
    spread = (group == lane // size).astype(BF16)
    return jnp.dot(taps_ref[which], spread, preferred_element_type=F32)


def short_filter(extended, taps, start, rows):
    total = extended[start : start + rows] * taps[0:1]
    for j in range(1, taps.shape[0]):
        total = total + extended[start - j : start - j + rows] * taps[j : j + 1]
    return total


def tail_kernel(size, reach, q_hbm, k_hbm, v_hbm, taps_ref, *rest):
    q_ref, k_ref, v_ref, sems = rest[-4:]
    out_ref = rest[-5]
    rows, width = q_hbm.shape
    first = rows - k_ref.shape[0]
    wide = TAIL_TILES * LANES
    parts = width // wide
    copies = []
    for p in range(parts):
        lanes = pl.ds(p * wide, wide)
        for which, (source, target, start) in enumerate(
            ((k_hbm, k_ref, first), (v_hbm, v_ref, first), (q_hbm, q_ref, rows - 16))
        ):
            copy = pltpu.make_async_copy(
                source.at[pl.ds(start, target.shape[0]), lanes], target.at[:, lanes], sems.at[p, which]
            )
            copy.start()
            copies.append(copy)
    k_taps = lane_taps(taps_ref, 1, size, width)
    v_taps = lane_taps(taps_ref, 2, size, width)
    for t in range(width // LANES):
        if t % TAIL_TILES == 0:
            for copy in copies[3 * (t // TAIL_TILES) : 3 * (t // TAIL_TILES) + 3]:
                copy.wait()
        lanes = slice(t * LANES, (t + 1) * LANES)
        k_part = k_ref[:, lanes].astype(F32)
        v_part = v_ref[:, lanes].astype(F32)
        q_part = q_ref[:, lanes].astype(F32)
        k_feat = short_filter(k_part, k_taps[:, lanes], 16, reach)
        v_feat = short_filter(v_part, v_taps[:, lanes], 16, reach)
        out_ref[t, :reach, :] = (k_feat * v_feat).astype(BF16)
        edges = [q_part[-EDGE:], k_part[-EDGE:], v_part[-EDGE:], jnp.zeros((EDGE, LANES), F32)]
        out_ref[t, reach : reach + 4 * EDGE, :] = jnp.concatenate(edges, axis=0).astype(BF16)
        if len(rest) == 6:
            out_ref[t, reach + 4 * EDGE :, :] = rest[0][t]


def call_tails(q_one, k_one, v_one, short_taps, reach, extra):
    rows, width = q_one.shape
    tiles = width // LANES
    size = width // short_taps.shape[2]
    inputs = [q_one, k_one, v_one, short_taps]
    out_rows = reach + 4 * EDGE
    if extra is not None:
        inputs.append(extra)
        out_rows += extra.shape[1]

    def kernel(*refs):
        tail_kernel(size, reach, *refs)

    return pl.pallas_call(
        kernel,
        in_specs=[pl.BlockSpec(memory_space=pltpu.HBM)] * 3
        + [pl.BlockSpec(memory_space=pltpu.VMEM)] * (len(inputs) - 3),
        out_specs=pl.BlockSpec(memory_space=pltpu.VMEM),
        out_shape=jax.ShapeDtypeStruct((tiles, out_rows, LANES), BF16),
        scratch_shapes=[
            pltpu.VMEM((16, width), BF16),
            pltpu.VMEM((reach + 16, width), BF16),
            pltpu.VMEM((reach + 16, width), BF16),
            pltpu.SemaphoreType.DMA((tiles // TAIL_TILES, 3)),
        ],
        compiler_params=params(),
        name="tails",
    )(*inputs)


def route_kernel(source_ref, spread_ref, out_ref):
    kept = out_ref.shape[1]
    for d in range(out_ref.shape[0]):
        out_ref[d] = spread_ref[source_ref[d], :kept, :]


def call_route(source, spread, kept):
    count, _, lanes = spread.shape
    return pl.pallas_call(
        route_kernel,
        in_specs=[
            pl.BlockSpec(memory_space=pltpu.SMEM),
            pl.BlockSpec(memory_space=pltpu.VMEM),
        ],
        out_specs=pl.BlockSpec(memory_space=pltpu.VMEM),
        out_shape=jax.ShapeDtypeStruct((count, kept, lanes), BF16),
        compiler_params=params(),
        name="route",
    )(source, spread)


def medium_table_kernel(base_ref, out_ref):
    reach, wide = out_ref.shape[2], base_ref.shape[2]
    for g in range(base_ref.shape[1]):
        row = jnp.broadcast_to(base_ref[0, g : g + 1, :], (reach, wide))
        out_ref[0, g] = pltpu.roll(row, 0, 1, stride=1, stride_axis=0).astype(BF16)


def call_medium_table(medium_taps, tile_groups, rows):
    reach, groups = medium_taps.shape
    tiles = groups // tile_groups
    base = jnp.pad(jnp.transpose(medium_taps[::-1]), ((0, 0), (1, rows - reach - 1)))
    return pl.pallas_call(
        medium_table_kernel,
        grid=(tiles,),
        in_specs=[pl.BlockSpec((1, tile_groups, rows), lambda i: (i, 0, 0))],
        out_specs=pl.BlockSpec((1, tile_groups, reach, rows), lambda i: (i, 0, 0, 0)),
        out_shape=pltpu.VMEM((tiles, tile_groups, reach, rows), BF16),
        compiler_params=params("arbitrary"),
        name="medium_table",
    )(base.astype(F32).reshape(tiles, tile_groups, rows))


def long_table_kernel(base_ref, out_ref):
    half, wide = out_ref.shape[1:]
    strip = jnp.broadcast_to(base_ref[0], (half, base_ref.shape[2]))
    strip = pltpu.roll(strip, 0, 1, stride=1, stride_axis=0)
    out_ref[0] = strip[:, half:].astype(BF16)


def call_long_table(long_rows, rows, lags):
    groups, length = long_rows.shape
    pieces = length // (lags * rows)
    half = rows // 2
    reach = lags * rows
    padded = jnp.pad(long_rows.astype(F32), ((0, 0), (rows, 0)))
    windows = jnp.stack(
        [padded[:, p * reach : p * reach + reach + rows] for p in range(pieces)], axis=1
    ).reshape(groups * pieces, 1, reach + rows)
    return pl.pallas_call(
        long_table_kernel,
        grid=(groups * pieces,),
        in_specs=[pl.BlockSpec((1, 1, reach + rows), lambda i: (i, 0, 0))],
        out_specs=pl.BlockSpec((1, half, reach + half), lambda i: (i, 0, 0)),
        out_shape=pltpu.VMEM((groups * pieces, half, reach + half), BF16),
        compiler_params=params("arbitrary"),
        name="long_table",
    )(windows)


def mix_kernel(
    size, keep_ref, q_ref, k_ref, v_ref, gate_ref, halo_ref, taps_ref, table_ref, out_ref, energy_ref
):
    rows, width = q_ref.shape
    tiles, groups, reach, wide = table_ref.shape
    keep = keep_ref[0:1, :]
    taps = [lane_taps(taps_ref, which, size, width) for which in range(3)]
    lane_group = lax.broadcasted_iota(jnp.int32, (1, 2 * LANES), 1) % LANES // size
    squares = jnp.zeros((rows, LANES), F32)
    for t in range(tiles):
        lanes = slice(t * LANES, (t + 1) * LANES)
        edges = halo_ref[t, reach:, :].astype(F32) * keep

        def feature(ref, which):
            extended = jnp.concatenate(
                [edges[which * EDGE : (which + 1) * EDGE], ref[:, lanes].astype(F32)], axis=0
            )
            return short_filter(extended, taps[which][:, lanes], EDGE, rows)

        q_feat = feature(q_ref, 0)
        z_own = (feature(k_ref, 1) * feature(v_ref, 2)).astype(BF16)
        z_halo = (halo_ref[t, :reach, :].astype(F32) * keep).astype(BF16)
        window = jnp.concatenate([jnp.concatenate([z_halo, z_own[:reach]], axis=0), z_own], axis=1)
        every = jnp.dot(
            table_ref[t].reshape(groups * reach, wide), window, preferred_element_type=F32
        )
        medium = every[:reach]
        for g in range(1, groups):
            medium = jnp.where(lane_group == g, every[g * reach : (g + 1) * reach], medium)
        mixed = q_feat * jnp.concatenate([medium[:, :LANES], medium[:, LANES:]], axis=0)
        out_ref[t] = jnp.transpose(mixed * gate_ref[:, lanes].astype(F32)).astype(BF16)
        squares = squares + mixed * mixed
    energy_ref[...] = jnp.sum(jnp.transpose(squares), axis=0, keepdims=True)


def call_mix(keep, q_one, k_one, v_one, k_two, halo, short_taps, medium_table):
    rows, width = q_one.shape
    size = width // short_taps.shape[2]

    def kernel(*refs):
        mix_kernel(size, *refs)

    return pl.pallas_call(
        kernel,
        in_specs=[pl.BlockSpec(memory_space=pltpu.VMEM)] * 8,
        out_specs=[pl.BlockSpec(memory_space=pltpu.VMEM)] * 2,
        out_shape=[
            jax.ShapeDtypeStruct((width // LANES, LANES, rows), BF16),
            jax.ShapeDtypeStruct((1, rows), F32),
        ],
        compiler_params=params(),
        name="mix",
    )(keep, q_one, k_one, v_one, k_two, halo, short_taps, in_vmem(medium_table))


def long_kernel(full_width, size, holder_ref, value_ref, energy_ref, table_ref, gain_ref, out_ref, ordered_ref):
    blocks, channels, rows = value_ref.shape
    slots, half, wide = table_ref.shape
    lags = wide // rows
    pieces = blocks // lags
    reach = blocks * size
    holders = [holder_ref[b] for b in range(blocks)]
    scales = [lax.rsqrt(energy_ref[holder] / full_width + EPSILON) for holder in holders]
    for g in range(channels // size):
        here = slice(g * size, (g + 1) * size)
        ordered_ref[g, :reach] = jnp.zeros((reach, rows), BF16)
        for b, holder in enumerate(holders):
            scaled = (value_ref[holder, here].astype(F32) * scales[b]).astype(BF16)
            ordered_ref[g, reach + b * size : reach + (b + 1) * size] = scaled
        total = ordered_ref[g, reach:].astype(F32) * gain_ref[g]
        for p in range(pieces):
            left = jnp.concatenate(
                [
                    ordered_ref[g, (blocks - lag) * size : (2 * blocks - lag) * size]
                    for lag in range(p * lags, (p + 1) * lags)
                ],
                axis=1,
            )
            right = jnp.concatenate(
                [
                    table_ref[g * pieces + p, :, lag * rows + shift : (lag + 1) * rows + shift]
                    for lag in range(lags)
                    for shift in (half, 0)
                ],
                axis=0,
            )
            total = total + jnp.dot(left, right, preferred_element_type=F32)
        for b, holder in enumerate(holders):
            out_ref[holder, here] = total[b * size : (b + 1) * size].astype(BF16)


def call_long(holder, values, energy, long_table, gain, size, full_width):
    blocks, channels, rows = values.shape

    def kernel(*refs):
        long_kernel(full_width, size, *refs)

    return pl.pallas_call(
        kernel,
        in_specs=[pl.BlockSpec(memory_space=pltpu.SMEM)]
        + [pl.BlockSpec(memory_space=pltpu.VMEM)] * 4,
        out_specs=pl.BlockSpec(memory_space=pltpu.VMEM),
        out_shape=jax.ShapeDtypeStruct((blocks, channels, rows), BF16),
        scratch_shapes=[pltpu.VMEM((channels // size, 2 * blocks * size, rows), BF16)],
        compiler_params=params(),
        name="long",
    )(holder, values, energy, in_vmem(long_table), gain)


def gate_kernel(mixed_ref, gate_ref, out_ref):
    for t in range(mixed_ref.shape[0]):
        lanes = slice(t * LANES, (t + 1) * LANES)
        mixed = jnp.transpose(mixed_ref[t]).astype(F32)
        out_ref[:, lanes] = (gate_ref[:, lanes].astype(F32) * mixed).astype(BF16)


def call_gate(mixed, q_two):
    rows, width = q_two.shape
    wide = GATE_TILES * LANES
    column = pl.BlockSpec((rows, wide), lambda i: (0, i))
    return pl.pallas_call(
        gate_kernel,
        grid=(width // wide,),
        in_specs=[pl.BlockSpec((GATE_TILES, LANES, rows), lambda i: (i, 0, 0)), column],
        out_specs=column,
        out_shape=jax.ShapeDtypeStruct((rows, width), BF16),
        compiler_params=params("arbitrary"),
        name="gate",
    )(mixed, q_two)


def exchange(array):
    return lax.all_to_all(array, "ctx", split_axis=0, concat_axis=0, tiled=True)


def sum_by_pairs(array, axis):
    count = lax.axis_size(axis)
    assert count & (count - 1) == 0
    bit = 1
    while bit < count:
        array = array + lax.ppermute(array, axis, [(i, i ^ bit) for i in range(count)])
        bit *= 2
    return array


def per_device(
    q_one,
    k_one,
    v_one,
    q_two,
    k_two,
    short_taps,
    medium_taps,
    long_taps,
    skip_gain,
    block_order,
    prev_owner,
):
    rows, width = q_one.shape
    ctx_count = lax.axis_size("ctx")
    tp_count = lax.axis_size("tp")
    me = lax.axis_index("ctx")
    size = width // short_taps.shape[2]
    reach = medium_taps.shape[0]
    assert rows == 2 * reach and short_taps.shape[1] <= EDGE + 1
    tiles = width // LANES
    shard = width // ctx_count
    shard_groups = shard // size
    full_width = width * tp_count

    slots = jnp.arange(ctx_count, dtype=jnp.int32)
    holder = jnp.sum(jnp.where(block_order[None, :] == slots[:, None], slots[None, :], 0), axis=1)
    source = jnp.take(prev_owner, block_order, mode="clip")
    is_first = jnp.sum(jnp.where(slots == me, block_order, 0)) == 0
    keep = jnp.broadcast_to(jnp.where(is_first, 0.0, 1.0), (EDGE, LANES)).astype(F32)

    tail_rows = reach + 4 * EDGE
    halo_rows = tiles * tail_rows // ctx_count
    taps_sent = long_taps.reshape(ctx_count, shard_groups * rows // LANES, LANES)
    if ctx_count == tiles:
        payload = call_tails(q_one, k_one, v_one, short_taps, reach, taps_sent)
    else:
        tails = call_tails(q_one, k_one, v_one, short_taps, reach, None)
        payload = jnp.concatenate([tails.reshape(ctx_count, halo_rows, LANES), taps_sent], axis=1)
    spread = exchange(payload)
    halo = exchange(call_route(source, spread, halo_rows))
    halo = halo.reshape(tiles, tail_rows, LANES)

    medium_table = call_medium_table(medium_taps, LANES // size, rows)
    long_rows = jnp.transpose(
        spread[:, halo_rows:].reshape(ctx_count, shard_groups, rows), (1, 0, 2)
    ).reshape(shard_groups, ctx_count * rows)
    long_table = call_long_table(long_rows, rows, min(ctx_count, 8))

    gated, energy = call_mix(keep, q_one, k_one, v_one, k_two, halo, short_taps, medium_table)
    values = exchange(gated.reshape(ctx_count, shard, rows))
    energy = sum_by_pairs(energy, "tp")
    energy = sum_by_pairs(jnp.where(slots[:, None] == me, energy, 0.0), "ctx")
    energy = energy.reshape(ctx_count, 1, rows)

    gain = lax.dynamic_slice_in_dim(skip_gain, me * shard, shard).reshape(shard_groups, 1, size, 1)
    gain = jnp.broadcast_to(gain, (shard_groups, ctx_count, size, 1))
    gain = gain.reshape(shard_groups, ctx_count * size, 1)
    returned = exchange(call_long(holder, values, energy, long_table, gain, size, full_width))
    return call_gate(returned.reshape(tiles, LANES, rows), q_two)


def solution(mesh):
    in_specs = (
        P("ctx", "tp"),
        P("ctx", "tp"),
        P("ctx", "tp"),
        P("ctx", "tp"),
        P("ctx", "tp"),
        P(None, None, "tp"),
        P(None, "tp"),
        P("tp", "ctx"),
        P("tp"),
        P(),
        P(),
    )
    out_specs = P("ctx", "tp")
    return jax.shard_map(
        per_device, mesh=mesh, in_specs=in_specs, out_specs=out_specs, check_vma=False
    )
```

```python
import jax
import jax.numpy as jnp
from jax import lax
from jax.experimental import pallas as pl
from jax.experimental.pallas import tpu as pltpu
from jax.sharding import PartitionSpec as P

EPSILON = 1e-06
LANES = 128
EDGE = 8
VMEM_BYTES = 24 * 1024 * 1024
TAIL_TILES = 2
MIX_AHEAD = 1
GATE_TILES = 4
F32 = jnp.float32
BF16 = jnp.bfloat16


def params(*semantics):
    return pltpu.CompilerParams(dimension_semantics=semantics, vmem_limit_bytes=VMEM_BYTES)


def in_hbm(array):
    return pltpu.with_memory_space_constraint(array, pltpu.HBM)


def lane_taps(taps_ref, which, size, width, first=0):
    groups = taps_ref.shape[2]
    group = lax.broadcasted_iota(jnp.int32, (groups, width), 0)
    lane = lax.broadcasted_iota(jnp.int32, (groups, width), 1) + first
    spread = (group == lane // size).astype(BF16)
    return jnp.dot(taps_ref[which], spread, preferred_element_type=F32)


def short_filter(extended, taps, start, rows):
    total = extended[start : start + rows] * taps[0:1]
    for j in range(1, taps.shape[0]):
        total = total + extended[start - j : start - j + rows] * taps[j : j + 1]
    return total


def tail_kernel(
    size,
    reach,
    carry,
    q_hbm,
    k_hbm,
    v_hbm,
    taps_hbm,
    long_hbm,
    out_ref,
    q_ref,
    k_ref,
    v_ref,
    taps_ref,
    long_ref,
    wide_ref,
    sems,
):
    rows, width = q_hbm.shape
    first = rows - k_ref.shape[0]
    wide = TAIL_TILES * LANES
    taps_copy = pltpu.make_async_copy(taps_hbm, taps_ref, sems.at[0, 3])
    taps_copy.start()
    parts = []
    for p in range(width // wide):
        lanes = pl.ds(p * wide, wide)
        copies = []
        for which, (source, target, start) in enumerate(
            ((k_hbm, k_ref, first), (v_hbm, v_ref, first), (q_hbm, q_ref, rows - 16))
        ):
            copy = pltpu.make_async_copy(
                source.at[pl.ds(start, target.shape[0]), lanes], target.at[:, lanes], sems.at[p, which]
            )
            copy.start()
            copies.append(copy)
        parts.append(copies)
    long_copy = pltpu.make_async_copy(long_hbm, long_ref, sems.at[1, 3])
    long_copy.start()
    taps_copy.wait()
    k_taps = lane_taps(taps_ref, 1, size, width)
    v_taps = lane_taps(taps_ref, 2, size, width)
    for t in range(width // LANES):
        if t % TAIL_TILES == 0:
            for copy in parts[t // TAIL_TILES]:
                copy.wait()
        lanes = slice(t * LANES, (t + 1) * LANES)
        wide_ref[t, 0] = k_ref[:, lanes].astype(F32)
        wide_ref[t, 1] = v_ref[:, lanes].astype(F32)
        q_part = q_ref[:, lanes].astype(F32)
        k_feat = short_filter(wide_ref.at[t, 0], k_taps[:, lanes], 16, reach)
        v_feat = short_filter(wide_ref.at[t, 1], v_taps[:, lanes], 16, reach)
        out_ref[t, :reach, :] = (k_feat * v_feat).astype(BF16)
        last = slice(reach + 16 - EDGE, reach + 16)
        edges = [q_part[-EDGE:], wide_ref[t, 0, last], wide_ref[t, 1, last], jnp.zeros((EDGE, LANES), F32)]
        out_ref[t, reach : reach + 4 * EDGE, :] = jnp.concatenate(edges, axis=0).astype(BF16)
    long_copy.wait()
    if carry:
        groups = LANES // size
        for t in range(width // LANES):
            taps = long_ref[t * groups : (t + 1) * groups, :].astype(F32)
            pieces = [taps[:, a : a + LANES] for a in range(0, rows, LANES)]
            out_ref[t, reach + 4 * EDGE :, :] = jnp.concatenate(pieces, axis=0).astype(BF16)


def call_tails(q_one, k_one, v_one, short_taps, long_taps, reach, carry):
    rows, width = q_one.shape
    tiles = width // LANES
    size = width // short_taps.shape[2]
    out_rows = reach + 4 * EDGE + (long_taps.size // width if carry else 0)

    def kernel(*refs):
        tail_kernel(size, reach, carry, *refs)

    inputs = [in_hbm(array) for array in (q_one, k_one, v_one, short_taps, long_taps)]
    return pl.pallas_call(
        kernel,
        in_specs=[pl.BlockSpec(memory_space=pltpu.HBM)] * 5,
        out_specs=pl.BlockSpec(memory_space=pltpu.VMEM),
        out_shape=jax.ShapeDtypeStruct((tiles, out_rows, LANES), BF16),
        scratch_shapes=[
            pltpu.VMEM((16, width), BF16),
            pltpu.VMEM((reach + 16, width), BF16),
            pltpu.VMEM((reach + 16, width), BF16),
            pltpu.VMEM(short_taps.shape, BF16),
            pltpu.VMEM(long_taps.shape, BF16),
            pltpu.VMEM((tiles, 2, reach + 16, LANES), F32),
            pltpu.SemaphoreType.DMA((tiles // TAIL_TILES, 4)),
        ],
        compiler_params=params(),
        name="tails",
    )(*inputs)


def route_kernel(source_ref, spread_ref, out_ref):
    kept = out_ref.shape[1]
    for d in range(out_ref.shape[0]):
        out_ref[d] = spread_ref[source_ref[d], :kept, :]


def call_route(source, spread, kept):
    count, _, lanes = spread.shape
    return pl.pallas_call(
        route_kernel,
        in_specs=[
            pl.BlockSpec(memory_space=pltpu.SMEM),
            pl.BlockSpec(memory_space=pltpu.VMEM),
        ],
        out_specs=pl.BlockSpec(memory_space=pltpu.VMEM),
        out_shape=jax.ShapeDtypeStruct((count, kept, lanes), BF16),
        compiler_params=params(),
        name="route",
    )(source, spread)


def shifted_rows(row, count):
    return pltpu.roll(jnp.broadcast_to(row, (count, row.shape[1])), 0, 1, stride=1, stride_axis=0)


def medium_rows(medium_taps, rows):
    reach = medium_taps.shape[0]
    base = jnp.pad(jnp.transpose(medium_taps[::-1]), ((0, 0), (1, rows - reach - 1)))
    return base.astype(F32)


def long_windows(long_rows, rows, lags):
    groups, length = long_rows.shape
    reach = lags * rows
    padded = jnp.pad(long_rows.astype(F32), ((0, 0), (rows, 0)))
    pieces = [padded[:, p : p + reach + rows] for p in range(0, length, reach)]
    return jnp.stack(pieces, axis=1).reshape(-1, reach + rows)


def mix_kernel(
    size,
    keep_ref,
    q_ref,
    k_ref,
    v_ref,
    gate_ref,
    halo_ref,
    taps_ref,
    base_ref,
    out_ref,
    energy_ref,
    extended_ref,
):
    rows, width = q_ref.shape
    tiles = width // LANES
    groups = LANES // size
    reach = rows // 2
    keep = keep_ref[0:1, :]
    taps = [lane_taps(taps_ref, which, size, width) for which in range(3)]
    lane_group = lax.broadcasted_iota(jnp.int32, (1, 2 * LANES), 1) % LANES // size

    def short(t):
        lanes = slice(t * LANES, (t + 1) * LANES)
        edges = halo_ref[t, reach:, :].astype(F32) * keep

        def feature(ref, which):
            extended_ref[t, which, :EDGE] = edges[which * EDGE : (which + 1) * EDGE]
            extended_ref[t, which, EDGE:] = ref[:, lanes].astype(F32)
            return short_filter(extended_ref.at[t, which], taps[which][:, lanes], EDGE, rows)

        z_own = (feature(k_ref, 1) * feature(v_ref, 2)).astype(BF16)
        z_halo = (halo_ref[t, :reach, :].astype(F32) * keep).astype(BF16)
        window = jnp.concatenate([jnp.concatenate([z_halo, z_own[:reach]], axis=0), z_own], axis=1)
        return feature(q_ref, 0), window

    squares = jnp.zeros((rows, LANES), F32)
    ready = [short(t) for t in range(MIX_AHEAD)]
    for t in range(tiles):
        if t + MIX_AHEAD < tiles:
            ready.append(short(t + MIX_AHEAD))
        q_feat, window = ready[t]
        table = jnp.concatenate(
            [
                shifted_rows(base_ref[g : g + 1, :], reach).astype(BF16)
                for g in range(t * groups, (t + 1) * groups)
            ],
            axis=0,
        )
        every = jnp.dot(table, window, preferred_element_type=F32)
        medium = every[:reach]
        for g in range(1, groups):
            medium = jnp.where(lane_group == g, every[g * reach : (g + 1) * reach], medium)
        mixed = q_feat * jnp.concatenate([medium[:, :LANES], medium[:, LANES:]], axis=0)
        gate = gate_ref[:, t * LANES : (t + 1) * LANES].astype(F32)
        out_ref[t] = jnp.transpose(mixed * gate)
        squares = squares + mixed * mixed
    energy_ref[...] = jnp.sum(jnp.transpose(squares), axis=0, keepdims=True)


def call_mix(keep, q_one, k_one, v_one, k_two, halo, short_taps, medium_base):
    rows, width = q_one.shape
    size = width // short_taps.shape[2]

    def kernel(*refs):
        mix_kernel(size, *refs)

    return pl.pallas_call(
        kernel,
        in_specs=[pl.BlockSpec(memory_space=pltpu.VMEM)] * 8,
        out_specs=[pl.BlockSpec(memory_space=pltpu.VMEM)] * 2,
        out_shape=[
            jax.ShapeDtypeStruct((width // LANES, LANES, rows), F32),
            jax.ShapeDtypeStruct((1, rows), F32),
        ],
        scratch_shapes=[pltpu.VMEM((width // LANES, 3, EDGE + rows, LANES), F32)],
        compiler_params=params(),
        name="mix",
    )(keep, q_one, k_one, v_one, k_two, halo, short_taps, medium_base)


def long_kernel(size, holder_ref, value_ref, window_ref, gain_ref, out_ref, ordered_ref):
    blocks, channels, rows = value_ref.shape
    half = rows // 2
    lags = window_ref.shape[1] // rows - 1
    pieces = blocks // lags
    reach = blocks * size
    holders = [holder_ref[b] for b in range(blocks)]
    for g in range(channels // size):
        here = slice(g * size, (g + 1) * size)
        ordered_ref[g, :reach] = jnp.zeros((reach, rows), BF16)
        for b, holder in enumerate(holders):
            ordered_ref[g, reach + b * size : reach + (b + 1) * size] = value_ref[holder, here]
    for g in range(channels // size):
        here = slice(g * size, (g + 1) * size)
        total = ordered_ref[g, reach:].astype(F32) * jnp.concatenate([gain_ref[here]] * blocks, axis=0)
        for p in range(pieces):
            slot = g * pieces + p
            left = jnp.concatenate(
                [
                    ordered_ref[g, (blocks - lag) * size : (2 * blocks - lag) * size]
                    for lag in range(p * lags, (p + 1) * lags)
                ],
                axis=1,
            )
            strip = shifted_rows(window_ref[slot : slot + 1, :], half).astype(BF16)
            right = jnp.concatenate(
                [
                    strip[:, shift : shift + rows]
                    for lag in range(1, lags + 1)
                    for shift in (lag * rows, lag * rows - half)
                ],
                axis=0,
            )
            total = total + jnp.dot(left, right, preferred_element_type=F32)
        for b, holder in enumerate(holders):
            out_ref[holder, here] = total[b * size : (b + 1) * size].astype(BF16)


def call_long(holder, values, windows, gain, size):
    blocks, channels, rows = values.shape

    def kernel(*refs):
        long_kernel(size, *refs)

    return pl.pallas_call(
        kernel,
        in_specs=[
            pl.BlockSpec(memory_space=pltpu.SMEM),
            pl.BlockSpec(memory_space=pltpu.VMEM),
            pl.BlockSpec(memory_space=pltpu.VMEM),
            pl.BlockSpec(memory_space=pltpu.VMEM),
        ],
        out_specs=pl.BlockSpec(memory_space=pltpu.VMEM),
        out_shape=jax.ShapeDtypeStruct((blocks, channels, rows), BF16),
        scratch_shapes=[
            pltpu.VMEM((channels // size, 2 * blocks * size, rows), BF16),
        ],
        compiler_params=params(),
        name="long",
    )(holder, values, windows, gain)


def gate_kernel(mixed_ref, gate_ref, out_ref):
    for t in range(mixed_ref.shape[0]):
        lanes = slice(t * LANES, (t + 1) * LANES)
        mixed = jnp.transpose(mixed_ref[t]).astype(F32)
        out_ref[:, lanes] = (gate_ref[:, lanes].astype(F32) * mixed).astype(BF16)


def call_gate(mixed, q_two):
    rows, width = q_two.shape
    wide = GATE_TILES * LANES
    column = pl.BlockSpec((rows, wide), lambda i: (0, i))
    return pl.pallas_call(
        gate_kernel,
        grid=(width // wide,),
        in_specs=[pl.BlockSpec((GATE_TILES, LANES, rows), lambda i: (i, 0, 0)), column],
        out_specs=column,
        out_shape=jax.ShapeDtypeStruct((rows, width), BF16),
        compiler_params=params("arbitrary"),
        name="gate",
    )(mixed, q_two)


def exchange(array):
    return lax.all_to_all(array, "ctx", split_axis=0, concat_axis=0, tiled=True)


def sum_by_pairs(array, axis):
    count = lax.axis_size(axis)
    assert count & (count - 1) == 0
    bit = 1
    while bit < count:
        array = array + lax.ppermute(array, axis, [(i, i ^ bit) for i in range(count)])
        bit *= 2
    return array


def per_device(
    q_one,
    k_one,
    v_one,
    q_two,
    k_two,
    short_taps,
    medium_taps,
    long_taps,
    skip_gain,
    block_order,
    prev_owner,
):
    rows, width = q_one.shape
    ctx_count = lax.axis_size("ctx")
    tp_count = lax.axis_size("tp")
    me = lax.axis_index("ctx")
    size = width // short_taps.shape[2]
    reach = medium_taps.shape[0]
    assert rows == 2 * reach and short_taps.shape[1] <= EDGE + 1
    tiles = width // LANES
    shard = width // ctx_count
    shard_groups = shard // size
    full_width = width * tp_count

    slots = jnp.arange(ctx_count, dtype=jnp.int32)
    holder = jnp.sum(jnp.where(block_order[None, :] == slots[:, None], slots[None, :], 0), axis=1)
    source = jnp.take(prev_owner, block_order, mode="clip")
    is_first = jnp.sum(jnp.where(slots == me, block_order, 0)) == 0
    keep = jnp.broadcast_to(jnp.where(is_first, 0.0, 1.0), (EDGE, LANES)).astype(F32)

    tail_rows = reach + 4 * EDGE
    halo_rows = tiles * tail_rows // ctx_count
    carry = ctx_count == tiles
    payload = call_tails(q_one, k_one, v_one, short_taps, long_taps, reach, carry)
    if not carry:
        taps_sent = long_taps.reshape(ctx_count, shard_groups, rows // LANES, LANES)
        taps_sent = jnp.transpose(taps_sent, (0, 2, 1, 3)).reshape(ctx_count, -1, LANES)
        payload = jnp.concatenate([payload.reshape(ctx_count, halo_rows, LANES), taps_sent], axis=1)
    spread = exchange(payload)
    halo = exchange(call_route(source, spread, halo_rows))
    halo = halo.reshape(tiles, tail_rows, LANES)

    medium_base = medium_rows(medium_taps, rows)
    long_rows = spread[:, halo_rows:].reshape(ctx_count, rows // LANES, shard_groups, LANES)
    long_rows = jnp.transpose(long_rows, (2, 0, 1, 3)).reshape(shard_groups, ctx_count * rows)
    windows = long_windows(long_rows, rows, min(ctx_count, 8))

    gated, energy = call_mix(keep, q_one, k_one, v_one, k_two, halo, short_taps, medium_base)
    energy = sum_by_pairs(energy, "tp")
    scale = lax.rsqrt(energy / full_width + EPSILON)
    values = (gated * scale[None]).astype(BF16).reshape(ctx_count, shard, rows)
    values = exchange(values)

    gain = lax.dynamic_slice_in_dim(skip_gain, me * shard, shard).reshape(shard, 1)
    returned = exchange(call_long(holder, values, windows, gain, size))
    return call_gate(returned.reshape(tiles, LANES, rows), q_two)


def solution(mesh):
    in_specs = (
        P("ctx", "tp"),
        P("ctx", "tp"),
        P("ctx", "tp"),
        P("ctx", "tp"),
        P("ctx", "tp"),
        P(None, None, "tp"),
        P(None, "tp"),
        P("tp", "ctx"),
        P("tp"),
        P(),
        P(),
    )
    out_specs = P("ctx", "tp")
    return jax.shard_map(
        per_device, mesh=mesh, in_specs=in_specs, out_specs=out_specs, check_vma=False
    )
```

```python
import jax
import jax.numpy as jnp
from jax import lax
from jax.experimental import pallas as pl
from jax.experimental.pallas import tpu as pltpu
from jax.sharding import PartitionSpec as P

EPSILON = 1e-06
LANES = 128
EDGE = 8
VMEM_BYTES = 24 * 1024 * 1024
PACK_TILES = 2
GATE_TILES = 4
F32 = jnp.float32
BF16 = jnp.bfloat16


def params(*semantics):
    return pltpu.CompilerParams(dimension_semantics=semantics, vmem_limit_bytes=VMEM_BYTES)


def in_hbm(array):
    return pltpu.with_memory_space_constraint(array, pltpu.HBM)


def lane_taps(taps_ref, which, size, width, first=0):
    groups = taps_ref.shape[2]
    group = lax.broadcasted_iota(jnp.int32, (groups, width), 0)
    lane = lax.broadcasted_iota(jnp.int32, (groups, width), 1) + first
    spread = (group == lane // size).astype(BF16)
    return jnp.dot(taps_ref[which], spread, preferred_element_type=F32)


def short_filter(extended, taps, start, rows):
    total = extended[start : start + rows] * taps[0:1]
    for j in range(1, taps.shape[0]):
        total = total + extended[start - j : start - j + rows] * taps[j : j + 1]
    return total


def pack_kernel(
    size, q_hbm, k_hbm, v_hbm, taps_hbm, long_hbm, out_ref, q_ref, k_ref, v_ref, taps_ref, long_ref, wide_ref, sems
):
    rows, width = q_hbm.shape
    tiles = width // LANES
    wide = PACK_TILES * LANES
    groups = LANES // size
    taps_copy = pltpu.make_async_copy(taps_hbm, taps_ref, sems.at[0, 3])
    taps_copy.start()
    parts = []
    for p in range(width // wide):
        lanes = pl.ds(p * wide, wide)
        copies = [
            pltpu.make_async_copy(source.at[:, lanes], target.at[:, lanes], sems.at[p, which])
            for which, (source, target) in enumerate(((k_hbm, k_ref), (v_hbm, v_ref), (q_hbm, q_ref)))
        ]
        for copy in copies:
            copy.start()
        parts.append(copies)
    long_copy = pltpu.make_async_copy(long_hbm, long_ref, sems.at[1, 3])
    long_copy.start()
    taps_copy.wait()
    taps = [lane_taps(taps_ref, which, size, width) for which in (1, 2)]
    for t in range(tiles):
        if t % PACK_TILES == 0:
            for copy in parts[t // PACK_TILES]:
                copy.wait()
        lanes = slice(t * LANES, (t + 1) * LANES)
        out_ref[t, :LANES, :] = jnp.transpose(q_ref[:, lanes])
        features = []
        for which, ref in enumerate((k_ref, v_ref)):
            wide_ref[t, which, :EDGE] = jnp.zeros((EDGE, LANES), F32)
            wide_ref[t, which, EDGE:] = ref[:, lanes].astype(F32)
            features.append(short_filter(wide_ref.at[t, which], taps[which][:, lanes], EDGE, rows))
            ends = [wide_ref[t, which, EDGE : 2 * EDGE], wide_ref[t, which, rows : rows + EDGE]]
            out_ref[t, 2 * LANES : 2 * LANES + 2 * EDGE, which * LANES : (which + 1) * LANES] = (
                jnp.concatenate(ends, axis=0).astype(BF16)
            )
        out_ref[t, LANES : 2 * LANES, :] = jnp.transpose((features[0] * features[1]).astype(BF16))
    long_copy.wait()
    for t in range(tiles):
        here = long_ref[t * groups : (t + 1) * groups, :].astype(F32)
        filler = jnp.zeros((2 * EDGE - groups, rows), F32)
        out_ref[t, 2 * LANES + 2 * EDGE :, :] = jnp.concatenate([here, filler], axis=0).astype(BF16)


def call_pack(q_one, k_one, v_one, short_taps, long_taps):
    rows, width = q_one.shape
    tiles = width // LANES
    size = width // short_taps.shape[2]
    assert rows == 2 * LANES and LANES // size <= 2 * EDGE

    def kernel(*refs):
        pack_kernel(size, *refs)

    inputs = [in_hbm(array) for array in (q_one, k_one, v_one, short_taps, long_taps)]
    return pl.pallas_call(
        kernel,
        in_specs=[pl.BlockSpec(memory_space=pltpu.HBM)] * 5,
        out_specs=pl.BlockSpec(memory_space=pltpu.VMEM),
        out_shape=jax.ShapeDtypeStruct((tiles, 2 * LANES + 4 * EDGE, rows), BF16),
        scratch_shapes=[
            pltpu.VMEM((rows, width), BF16),
            pltpu.VMEM((rows, width), BF16),
            pltpu.VMEM((rows, width), BF16),
            pltpu.VMEM(short_taps.shape, BF16),
            pltpu.VMEM(long_taps.shape, BF16),
            pltpu.VMEM((tiles, 2, EDGE + rows, LANES), F32),
            pltpu.SemaphoreType.DMA((tiles // PACK_TILES, 4)),
        ],
        compiler_params=params(),
        name="pack",
    )(*inputs)


def turn_kernel(in_ref, out_ref):
    for t in range(out_ref.shape[0]):
        out_ref[t] = jnp.transpose(in_ref[:, t * LANES : (t + 1) * LANES])


def call_turn(array):
    rows, width = array.shape
    wide = GATE_TILES * LANES
    return pl.pallas_call(
        turn_kernel,
        grid=(width // wide,),
        in_specs=[pl.BlockSpec((rows, wide), lambda i: (0, i))],
        out_specs=pl.BlockSpec((GATE_TILES, LANES, rows), lambda i: (i, 0, 0)),
        out_shape=jax.ShapeDtypeStruct((width // LANES, LANES, rows), BF16),
        compiler_params=params("arbitrary"),
        name="turn",
    )(array)


def shifted_rows(row, count):
    return pltpu.roll(jnp.broadcast_to(row, (count, row.shape[1])), 0, 1, stride=1, stride_axis=0)


def long_windows(long_rows, rows, lags):
    groups, length = long_rows.shape
    reach = lags * rows
    padded = jnp.pad(long_rows.astype(F32), ((0, 0), (rows, 0)))
    pieces = [padded[:, p : p + reach + rows] for p in range(0, length, reach)]
    return jnp.stack(pieces, axis=1).reshape(-1, reach + rows)


def mix_kernel(
    size, holder_ref, moved_ref, ends_ref, taps_ref, column_ref, base_ref, out_ref, energy_ref, extended_ref, squares_ref
):
    blocks, shard, rows = out_ref.shape
    halves = rows // LANES
    span = 2 * EDGE
    holders = [holder_ref[b] for b in range(blocks)]
    ends = [ends_ref[holder, -span:, :].astype(F32) for holder in holders]

    features = []
    for which in range(2):
        lanes = slice(which * shard, (which + 1) * shard)
        extended_ref[which, :EDGE] = jnp.zeros((EDGE, shard), F32)
        for b in range(blocks):
            before = ends[b - 1][EDGE:, lanes] if b else jnp.zeros((EDGE, shard), F32)
            at = EDGE + b * span
            extended_ref[which, at : at + span] = jnp.concatenate([before, ends[b][:EDGE, lanes]], axis=0)
        features.append(
            short_filter(extended_ref.at[which], taps_ref[which + 1], EDGE, blocks * span)
        )
    starts = jnp.transpose((features[0] * features[1]).astype(BF16).astype(F32))
    wide = blocks * span
    lane = lax.broadcasted_iota(jnp.int32, (size, LANES), 1)

    squares_ref[...] = jnp.zeros(squares_ref.shape, F32)
    for g in range(shard // size):
        here = slice(g * size, (g + 1) * size)
        z_there = slice(shard + g * size, shard + (g + 1) * size)
        q_seq = [jnp.zeros((size, LANES), F32)]
        z_seq = [jnp.zeros((size, LANES), BF16)]
        for b, holder in enumerate(holders):
            q_seq.append(moved_ref[holder, here, :].astype(F32))
            z_block = moved_ref[holder, z_there, :]
            first = pltpu.roll(starts[here], (wide - b * span - EDGE) % wide, 1)[:, :LANES]
            z_first = jnp.where(lane < EDGE, first, z_block[:, :LANES].astype(F32)).astype(BF16)
            z_seq.append(jnp.concatenate([z_first, z_block[:, LANES:]], axis=1))
        q_seq = jnp.concatenate(q_seq, axis=1)
        z_seq = jnp.concatenate(z_seq, axis=1)
        q_feat = q_seq * column_ref[here, 0:1]
        for j in range(1, taps_ref.shape[1]):
            q_feat = q_feat + pltpu.roll(q_seq, j, 1) * column_ref[here, j : j + 1]
        table = shifted_rows(base_ref[g : g + 1, :], 2 * LANES)[:, :LANES].astype(BF16)
        windows = [z_seq[:, o * LANES : (o + 2) * LANES] for o in range(blocks * halves)]
        medium = jnp.dot(jnp.concatenate(windows, axis=0), table, preferred_element_type=F32)
        for o in range(blocks * halves):
            mixed = q_feat[:, (o + 1) * LANES : (o + 2) * LANES] * medium[o * size : (o + 1) * size]
            at = (o % halves) * LANES
            out_ref[o // halves, here, at : at + LANES] = mixed
            squares_ref[o] += mixed * mixed
    energy_ref[...] = jnp.sum(squares_ref[...], axis=1)


def call_mix(holder, moved, ends, short_local, medium_local, shard, rows):
    blocks = moved.shape[0]
    size = shard // medium_local.shape[1]
    reach = medium_local.shape[0]
    assert reach == LANES and short_local.shape[1] <= EDGE + 1
    lane_form = jnp.repeat(short_local, size, axis=2).astype(F32)
    base = jnp.pad(jnp.transpose(medium_local).astype(F32), ((0, 0), (LANES, 0)))

    def kernel(*refs):
        mix_kernel(size, *refs)

    return pl.pallas_call(
        kernel,
        in_specs=[pl.BlockSpec(memory_space=pltpu.SMEM)]
        + [pl.BlockSpec(memory_space=pltpu.VMEM)] * 5,
        out_specs=[pl.BlockSpec(memory_space=pltpu.VMEM)] * 2,
        out_shape=[
            jax.ShapeDtypeStruct((blocks, shard, rows), F32),
            jax.ShapeDtypeStruct((blocks * rows // LANES, LANES), F32),
        ],
        scratch_shapes=[
            pltpu.VMEM((2, EDGE + blocks * 2 * EDGE, shard), F32),
            pltpu.VMEM((blocks * rows // LANES, size, LANES), F32),
        ],
        compiler_params=params(),
        name="mix",
    )(holder, moved, ends, lane_form, jnp.transpose(lane_form[0]), base)


def long_kernel(
    full_width, size, holder_ref, mixed_ref, key_ref, energy_ref, window_ref, gain_ref, out_ref, ordered_ref
):
    blocks, shard, rows = mixed_ref.shape
    half = rows // 2
    halves = rows // LANES
    lags = window_ref.shape[1] // rows - 1
    pieces = blocks // lags
    reach = blocks * size
    holders = [holder_ref[b] for b in range(blocks)]
    scale = lax.rsqrt(energy_ref[...] / full_width + EPSILON)
    for b, holder in enumerate(holders):
        line = jnp.concatenate([scale[o : o + 1] for o in range(b * halves, (b + 1) * halves)], axis=1)
        for g in range(shard // size):
            here = slice(g * size, (g + 1) * size)
            value = key_ref[holder, here].astype(F32) * mixed_ref[b, here] * line
            ordered_ref[g, reach + b * size : reach + (b + 1) * size] = value.astype(BF16)
    for g in range(shard // size):
        here = slice(g * size, (g + 1) * size)
        ordered_ref[g, :reach] = jnp.zeros((reach, rows), BF16)
        total = ordered_ref[g, reach:].astype(F32) * jnp.concatenate([gain_ref[here]] * blocks, axis=0)
        for p in range(pieces):
            slot = g * pieces + p
            left = jnp.concatenate(
                [
                    ordered_ref[g, (blocks - lag) * size : (2 * blocks - lag) * size]
                    for lag in range(p * lags, (p + 1) * lags)
                ],
                axis=1,
            )
            strip = shifted_rows(window_ref[slot : slot + 1, :], half).astype(BF16)
            right = jnp.concatenate(
                [
                    strip[:, shift : shift + rows]
                    for lag in range(1, lags + 1)
                    for shift in (lag * rows, lag * rows - half)
                ],
                axis=0,
            )
            total = total + jnp.dot(left, right, preferred_element_type=F32)
        for b, holder in enumerate(holders):
            out_ref[holder, here] = total[b * size : (b + 1) * size].astype(BF16)


def call_long(holder, mixed, keys, energy, windows, gain, size, full_width):
    blocks, shard, rows = mixed.shape

    def kernel(*refs):
        long_kernel(full_width, size, *refs)

    return pl.pallas_call(
        kernel,
        in_specs=[pl.BlockSpec(memory_space=pltpu.SMEM)]
        + [pl.BlockSpec(memory_space=pltpu.VMEM)] * 5,
        out_specs=pl.BlockSpec(memory_space=pltpu.VMEM),
        out_shape=jax.ShapeDtypeStruct((blocks, shard, rows), BF16),
        scratch_shapes=[pltpu.VMEM((shard // size, 2 * blocks * size, rows), BF16)],
        compiler_params=params(),
        name="long",
    )(holder, mixed, keys, energy, windows, gain)


def gate_kernel(mixed_ref, gate_ref, out_ref):
    for t in range(mixed_ref.shape[0]):
        lanes = slice(t * LANES, (t + 1) * LANES)
        mixed = jnp.transpose(mixed_ref[t]).astype(F32)
        out_ref[:, lanes] = (gate_ref[:, lanes].astype(F32) * mixed).astype(BF16)


def call_gate(mixed, q_two):
    rows, width = q_two.shape
    wide = GATE_TILES * LANES
    column = pl.BlockSpec((rows, wide), lambda i: (0, i))
    return pl.pallas_call(
        gate_kernel,
        grid=(width // wide,),
        in_specs=[pl.BlockSpec((GATE_TILES, LANES, rows), lambda i: (i, 0, 0)), column],
        out_specs=column,
        out_shape=jax.ShapeDtypeStruct((rows, width), BF16),
        compiler_params=params("arbitrary"),
        name="gate",
    )(mixed, q_two)


def exchange(array):
    return lax.all_to_all(array, "ctx", split_axis=0, concat_axis=0, tiled=True)


def sum_by_pairs(array, axis):
    count = lax.axis_size(axis)
    assert count & (count - 1) == 0
    bit = 1
    while bit < count:
        array = array + lax.ppermute(array, axis, [(i, i ^ bit) for i in range(count)])
        bit *= 2
    return array


def per_device(
    q_one,
    k_one,
    v_one,
    q_two,
    k_two,
    short_taps,
    medium_taps,
    long_taps,
    skip_gain,
    block_order,
    prev_owner,
):
    rows, width = q_one.shape
    ctx_count = lax.axis_size("ctx")
    tp_count = lax.axis_size("tp")
    me = lax.axis_index("ctx")
    size = width // short_taps.shape[2]
    tiles = width // LANES
    tile_groups = LANES // size
    shard = width // ctx_count
    shard_groups = shard // size

    slots = jnp.arange(ctx_count, dtype=jnp.int32)
    holder = jnp.sum(jnp.where(block_order[None, :] == slots[:, None], slots[None, :], 0), axis=1)

    packed = call_pack(q_one, k_one, v_one, short_taps, long_taps)
    span = 2 * EDGE
    if ctx_count == tiles:
        moved = exchange(packed)
        taps_at = 2 * shard + span
        ends = lax.slice_in_dim(moved, 2 * shard, taps_at, axis=1)
    else:
        ends = packed[:, 2 * LANES : 2 * LANES + span].reshape(tiles, span, 2, -1, shard)
        parts = [
            packed[:, :LANES],
            packed[:, LANES : 2 * LANES],
            jnp.transpose(ends, (0, 3, 1, 2, 4)),
            packed[:, 2 * LANES + span : 2 * LANES + span + tile_groups],
        ]
        moved = exchange(
            jnp.concatenate([part.reshape(ctx_count, -1, rows) for part in parts], axis=1)
        )
        taps_at = 2 * shard + span * 2 * shard // rows
        ends = moved[:, 2 * shard : taps_at].reshape(ctx_count, span, 2 * shard)
    moved, k_two = lax.optimization_barrier((moved, k_two))
    keys = exchange(call_turn(k_two).reshape(ctx_count, shard, rows))

    short_local = lax.dynamic_slice_in_dim(short_taps, me * shard_groups, shard_groups, axis=2)
    medium_local = lax.dynamic_slice_in_dim(medium_taps, me * shard_groups, shard_groups, axis=1)
    mixed, energy = call_mix(holder, moved, ends, short_local, medium_local, shard, rows)
    energy = sum_by_pairs(sum_by_pairs(energy, "tp"), "ctx")

    long_rows = moved[:, taps_at : taps_at + shard_groups]
    long_rows = jnp.transpose(long_rows, (1, 0, 2)).reshape(shard_groups, ctx_count * rows)
    windows = long_windows(long_rows, rows, min(ctx_count, 8))
    gain = lax.dynamic_slice_in_dim(skip_gain, me * shard, shard).reshape(shard, 1)
    filtered = call_long(
        holder, mixed, keys, energy, windows, gain, size, width * tp_count
    )
    returned = exchange(filtered)
    return call_gate(returned.reshape(tiles, LANES, rows), q_two)


def solution(mesh):
    in_specs = (
        P("ctx", "tp"),
        P("ctx", "tp"),
        P("ctx", "tp"),
        P("ctx", "tp"),
        P("ctx", "tp"),
        P(None, None, "tp"),
        P(None, "tp"),
        P("tp", "ctx"),
        P("tp"),
        P(),
        P(),
    )
    out_specs = P("ctx", "tp")
    return jax.shard_map(
        per_device, mesh=mesh, in_specs=in_specs, out_specs=out_specs, check_vma=False
    )
```

```python
import jax
import jax.numpy as jnp
from jax import lax
from jax.experimental import pallas as pl
from jax.experimental.pallas import tpu as pltpu
from jax.sharding import PartitionSpec as P

EPSILON = 1e-06
LANES = 128
EDGE = 8
VMEM_BYTES = 24 * 1024 * 1024
PACK_TILES = 2
GATE_TILES = 4
F32 = jnp.float32
BF16 = jnp.bfloat16


def params(*semantics):
    return pltpu.CompilerParams(dimension_semantics=semantics, vmem_limit_bytes=VMEM_BYTES)


def in_hbm(array):
    return pltpu.with_memory_space_constraint(array, pltpu.HBM)


def lane_taps(taps_ref, which, size, width, first=0):
    groups = taps_ref.shape[2]
    group = lax.broadcasted_iota(jnp.int32, (groups, width), 0)
    lane = lax.broadcasted_iota(jnp.int32, (groups, width), 1) + first
    spread = (group == lane // size).astype(BF16)
    return jnp.dot(taps_ref[which], spread, preferred_element_type=F32)


def short_filter(extended, taps, start, rows):
    total = extended[start : start + rows] * taps[0:1]
    for j in range(1, taps.shape[0]):
        total = total + extended[start - j : start - j + rows] * taps[j : j + 1]
    return total


def pack_kernel(
    size, q_hbm, k_hbm, v_hbm, taps_hbm, long_hbm, out_ref, q_ref, k_ref, v_ref, taps_ref, long_ref, wide_ref, sems
):
    rows, width = q_hbm.shape
    tiles = width // LANES
    wide = PACK_TILES * LANES
    groups = LANES // size
    taps_copy = pltpu.make_async_copy(taps_hbm, taps_ref, sems.at[0, 3])
    taps_copy.start()
    parts = []
    for p in range(width // wide):
        lanes = pl.ds(p * wide, wide)
        copies = [
            pltpu.make_async_copy(source.at[:, lanes], target.at[:, lanes], sems.at[p, which])
            for which, (source, target) in enumerate(((k_hbm, k_ref), (v_hbm, v_ref), (q_hbm, q_ref)))
        ]
        for copy in copies:
            copy.start()
        parts.append(copies)
    long_copy = pltpu.make_async_copy(long_hbm, long_ref, sems.at[1, 3])
    long_copy.start()
    taps_copy.wait()
    taps = [lane_taps(taps_ref, which, size, width) for which in (1, 2)]
    for t in range(tiles):
        if t % PACK_TILES == 0:
            for copy in parts[t // PACK_TILES]:
                copy.wait()
        lanes = slice(t * LANES, (t + 1) * LANES)
        turned = jnp.transpose(q_ref[:LANES, lanes])
        at = LANES + LANES // 2
        out_ref[t, LANES:at, :] = jnp.concatenate([turned[: LANES // 2], turned[LANES // 2 :]], axis=1)
        features = []
        for which, ref in enumerate((k_ref, v_ref)):
            wide_ref[t, which, :EDGE] = jnp.zeros((EDGE, LANES), F32)
            wide_ref[t, which, EDGE:] = ref[:, lanes].astype(F32)
            features.append(short_filter(wide_ref.at[t, which], taps[which][:, lanes], EDGE, rows))
            ends = [wide_ref[t, which, EDGE : 2 * EDGE], wide_ref[t, which, rows : rows + EDGE]]
            out_ref[t, at : at + 2 * EDGE, which * LANES : (which + 1) * LANES] = (
                jnp.concatenate(ends, axis=0).astype(BF16)
            )
        out_ref[t, :LANES, :] = jnp.transpose((features[0] * features[1]).astype(BF16))
    long_copy.wait()
    for t in range(tiles):
        lanes = slice(t * LANES, (t + 1) * LANES)
        middle = q_ref[LANES : LANES + 2 * EDGE, lanes].astype(F32)[:EDGE]
        last = q_ref[rows - 2 * EDGE :, lanes].astype(F32)[EDGE:]
        here = long_ref[t * groups : (t + 1) * groups, :].astype(F32)
        lines = jnp.concatenate([jnp.concatenate([middle, last], axis=1), here], axis=0)
        out_ref[t, LANES + LANES // 2 + 2 * EDGE :, :] = lines.astype(BF16)


def call_pack(q_one, k_one, v_one, short_taps, long_taps):
    rows, width = q_one.shape
    tiles = width // LANES
    size = width // short_taps.shape[2]
    groups = LANES // size
    assert rows == 2 * LANES

    def kernel(*refs):
        pack_kernel(size, *refs)

    inputs = [in_hbm(array) for array in (q_one, k_one, v_one, short_taps, long_taps)]
    return pl.pallas_call(
        kernel,
        in_specs=[pl.BlockSpec(memory_space=pltpu.HBM)] * 5,
        out_specs=pl.BlockSpec(memory_space=pltpu.VMEM),
        out_shape=jax.ShapeDtypeStruct((tiles, LANES + LANES // 2 + 3 * EDGE + groups, rows), BF16),
        scratch_shapes=[
            pltpu.VMEM((rows, width), BF16),
            pltpu.VMEM((rows, width), BF16),
            pltpu.VMEM((rows, width), BF16),
            pltpu.VMEM(short_taps.shape, BF16),
            pltpu.VMEM(long_taps.shape, BF16),
            pltpu.VMEM((tiles, 2, EDGE + rows, LANES), F32),
            pltpu.SemaphoreType.DMA((tiles // PACK_TILES, 4)),
        ],
        compiler_params=params(),
        name="pack",
    )(*inputs)


def shifted_rows(row, count):
    return pltpu.roll(jnp.broadcast_to(row, (count, row.shape[1])), 0, 1, stride=1, stride_axis=0)


def long_windows(long_rows, rows, lags):
    groups, length = long_rows.shape
    reach = lags * rows
    padded = jnp.pad(long_rows.astype(F32), ((0, 0), (rows, 0)))
    pieces = [padded[:, p : p + reach + rows] for p in range(0, length, reach)]
    return jnp.stack(pieces, axis=1).reshape(-1, reach + rows)


def early_kernel(
    size, q_ref, k_ref, v_ref, gate_ref, taps_ref, base_ref, out_ref, energy_ref, extended_ref
):
    rows, width = q_ref.shape
    groups = LANES // size
    taps = [lane_taps(taps_ref, which, size, width) for which in range(3)]
    lane_group = lax.broadcasted_iota(jnp.int32, (1, LANES), 1) // size
    own = lax.broadcasted_iota(jnp.int32, (LANES, LANES), 0) >= EDGE
    squares = jnp.zeros((LANES, LANES), F32)
    for t in range(width // LANES):
        lanes = slice(t * LANES, (t + 1) * LANES)
        for which, ref in enumerate((q_ref, k_ref, v_ref)):
            extended_ref[t, which, :EDGE] = jnp.zeros((EDGE, LANES), F32)
            extended_ref[t, which, EDGE:] = ref[:, lanes].astype(F32)
        q_feat = short_filter(extended_ref.at[t, 0], taps[0][:, lanes], EDGE + LANES, LANES)
        k_feat = short_filter(extended_ref.at[t, 1], taps[1][:, lanes], EDGE, rows)
        v_feat = short_filter(extended_ref.at[t, 2], taps[2][:, lanes], EDGE, rows)
        table = jnp.concatenate(
            [
                shifted_rows(base_ref[g : g + 1, :], LANES).astype(BF16)
                for g in range(t * groups, (t + 1) * groups)
            ],
            axis=0,
        )
        every = jnp.dot(table, (k_feat * v_feat).astype(BF16), preferred_element_type=F32)
        medium = every[:LANES]
        for g in range(1, groups):
            medium = jnp.where(lane_group == g, every[g * LANES : (g + 1) * LANES], medium)
        mixed = jnp.where(own, q_feat * medium, 0.0)
        out_ref[t] = jnp.transpose(mixed * gate_ref[LANES:, lanes].astype(F32))
        squares = squares + mixed * mixed
    energy_ref[...] = jnp.sum(jnp.transpose(squares), axis=0, keepdims=True)


def call_early(q_one, k_one, v_one, k_two, short_taps, medium_taps):
    rows, width = q_one.shape
    tiles = width // LANES
    size = width // short_taps.shape[2]
    base = jnp.transpose(medium_taps[::-1])
    base = jnp.pad(base, ((0, 0), (1, rows - medium_taps.shape[0] - 1))).astype(F32)

    def kernel(*refs):
        early_kernel(size, *refs)

    return pl.pallas_call(
        kernel,
        in_specs=[pl.BlockSpec(memory_space=pltpu.VMEM)] * 6,
        out_specs=[pl.BlockSpec(memory_space=pltpu.VMEM)] * 2,
        out_shape=[
            jax.ShapeDtypeStruct((tiles, LANES, LANES), F32),
            jax.ShapeDtypeStruct((1, LANES), F32),
        ],
        scratch_shapes=[pltpu.VMEM((tiles, 3, EDGE + rows, LANES), F32)],
        compiler_params=params(),
        name="early",
    )(q_one, k_one, v_one, k_two, short_taps, base)


def join_kernel(full_width, gate_ref, early_ref, energy_ref, out_ref):
    scale = lax.rsqrt(energy_ref[...] / full_width + EPSILON)
    lane = lax.broadcasted_iota(jnp.int32, (LANES, LANES), 1)
    for t in range(out_ref.shape[0]):
        lanes = slice(t * LANES, (t + 1) * LANES)
        turned = jnp.transpose(gate_ref[:, lanes])
        values = jnp.where(lane < EDGE, turned[:, LANES:].astype(F32), early_ref[t] * scale)
        out_ref[t, :, :LANES] = turned[:, :LANES]
        out_ref[t, :, LANES:] = values.astype(BF16)


def call_join(k_two, early, energy, full_width):
    rows, width = k_two.shape

    def kernel(*refs):
        join_kernel(full_width, *refs)

    return pl.pallas_call(
        kernel,
        in_specs=[pl.BlockSpec(memory_space=pltpu.VMEM)] * 3,
        out_specs=pl.BlockSpec(memory_space=pltpu.VMEM),
        out_shape=jax.ShapeDtypeStruct((width // LANES, LANES, rows), BF16),
        compiler_params=params(),
        name="join",
    )(k_two, early, energy)


def mix_kernel(
    size,
    holder_ref,
    moved_ref,
    ends_ref,
    more_ref,
    taps_ref,
    column_ref,
    base_ref,
    out_ref,
    energy_ref,
    extended_ref,
    q_ends_ref,
    squares_ref,
):
    blocks, shard, rows = out_ref.shape
    halves = rows // LANES
    span = 2 * EDGE
    holders = [holder_ref[b] for b in range(blocks)]
    ends = [ends_ref[holder].astype(F32) for holder in holders]
    more = [more_ref[holder].astype(F32) for holder in holders]

    features = []
    for which in range(2):
        lanes = slice(which * shard, (which + 1) * shard)
        extended_ref[which, :EDGE] = jnp.zeros((EDGE, shard), F32)
        for b in range(blocks):
            before = ends[b - 1][EDGE:, lanes] if b else jnp.zeros((EDGE, shard), F32)
            at = EDGE + b * span
            extended_ref[which, at : at + span] = jnp.concatenate([before, ends[b][:EDGE, lanes]], axis=0)
        features.append(
            short_filter(extended_ref.at[which], taps_ref[which + 1], EDGE, blocks * span)
        )
    starts = jnp.transpose((features[0] * features[1]).astype(BF16).astype(F32))
    wide = blocks * span
    for b in range(blocks):
        before = more[b - 1][:, shard:] if b else jnp.zeros((EDGE, shard), F32)
        q_ends_ref[b * span : (b + 1) * span] = jnp.concatenate([before, more[b][:, :shard]], axis=0)
    q_ends = jnp.transpose(q_ends_ref[...])
    half = shard // 2

    def q_first(holder, g):
        if half % size == 0:
            at = shard + g * size % half
            beside = g * size // half * LANES
            return moved_ref[holder, at : at + size, beside : beside + LANES].astype(F32)
        both = moved_ref[holder, shard : shard + half, :].astype(F32)
        both = jnp.concatenate([both[:, :LANES], both[:, LANES:]], axis=0)
        return both[g * size : (g + 1) * size]

    lane = lax.broadcasted_iota(jnp.int32, (size, LANES), 1)

    squares_ref[...] = jnp.zeros(squares_ref.shape, F32)
    for g in range(shard // size):
        here = slice(g * size, (g + 1) * size)
        z_seq = [jnp.zeros((size, LANES), BF16)]
        q_feats = []
        for b, holder in enumerate(holders):
            z_block = moved_ref[holder, here, :]
            first = pltpu.roll(starts[here], (wide - b * span - EDGE) % wide, 1)[:, :LANES]
            z_first = jnp.where(lane < EDGE, first, z_block[:, :LANES].astype(F32)).astype(BF16)
            z_seq.append(jnp.concatenate([z_first, z_block[:, LANES:]], axis=1))
            before = pltpu.roll(q_ends[here], (wide + LANES - EDGE - b * span) % wide, 1)[:, :LANES]
            after = pltpu.roll(q_ends[here], (wide - b * span - EDGE) % wide, 1)[:, :LANES]
            q_block = jnp.concatenate([before, q_first(holder, g), after], axis=1)
            q_feat = q_block * column_ref[here, 0:1]
            for j in range(1, taps_ref.shape[1]):
                q_feat = q_feat + pltpu.roll(q_block, j, 1) * column_ref[here, j : j + 1]
            q_feats.append(q_feat)
        z_seq = jnp.concatenate(z_seq, axis=1)
        table = shifted_rows(base_ref[g : g + 1, :], 2 * LANES)[:, :LANES].astype(BF16)
        windows = [z_seq[:, o * LANES : (o + 2) * LANES] for o in range(blocks * halves)]
        medium = jnp.dot(jnp.concatenate(windows, axis=0), table, preferred_element_type=F32)
        for o in range(blocks * halves):
            b, at = o // halves, (o % halves) * LANES
            mixed = q_feats[b][:, LANES + at : 2 * LANES + at] * medium[o * size : (o + 1) * size]
            if at:
                mixed = jnp.where(lane < EDGE, mixed, 0.0)
            out_ref[b, here, at : at + LANES] = mixed
            squares_ref[o] += mixed * mixed
    energy_ref[...] = jnp.sum(squares_ref[...], axis=1)


def call_mix(holder, moved, ends, more, short_local, medium_local, shard, rows):
    blocks = moved.shape[0]
    size = shard // medium_local.shape[1]
    reach = medium_local.shape[0]
    assert reach == LANES and short_local.shape[1] <= EDGE + 1
    lane_form = jnp.repeat(short_local, size, axis=2).astype(F32)
    base = jnp.pad(jnp.transpose(medium_local).astype(F32), ((0, 0), (LANES, 0)))

    def kernel(*refs):
        mix_kernel(size, *refs)

    return pl.pallas_call(
        kernel,
        in_specs=[pl.BlockSpec(memory_space=pltpu.SMEM)]
        + [pl.BlockSpec(memory_space=pltpu.VMEM)] * 6,
        out_specs=[pl.BlockSpec(memory_space=pltpu.VMEM)] * 2,
        out_shape=[
            jax.ShapeDtypeStruct((blocks, shard, rows), F32),
            jax.ShapeDtypeStruct((blocks * rows // LANES, LANES), F32),
        ],
        scratch_shapes=[
            pltpu.VMEM((2, EDGE + blocks * 2 * EDGE, shard), F32),
            pltpu.VMEM((blocks * 2 * EDGE, shard), F32),
            pltpu.VMEM((blocks * rows // LANES, size, LANES), F32),
        ],
        compiler_params=params(),
        name="mix",
    )(holder, moved, ends, more, lane_form, jnp.transpose(lane_form[0]), base)


def long_kernel(
    full_width, size, holder_ref, mixed_ref, key_ref, energy_ref, window_ref, gain_ref, out_ref, ordered_ref
):
    blocks, shard, rows = mixed_ref.shape
    half = rows // 2
    halves = rows // LANES
    lags = window_ref.shape[1] // rows - 1
    pieces = blocks // lags
    reach = blocks * size
    holders = [holder_ref[b] for b in range(blocks)]
    scale = lax.rsqrt(energy_ref[...] / full_width + EPSILON)
    own = lax.broadcasted_iota(jnp.int32, (size, rows), 1) >= LANES + EDGE
    for b, holder in enumerate(holders):
        line = jnp.concatenate([scale[o : o + 1] for o in range(b * halves, (b + 1) * halves)], axis=1)
        for g in range(shard // size):
            here = slice(g * size, (g + 1) * size)
            key = key_ref[holder, here].astype(F32)
            value = jnp.where(own, key, key * mixed_ref[b, here] * line)
            ordered_ref[g, reach + b * size : reach + (b + 1) * size] = value.astype(BF16)
    for g in range(shard // size):
        here = slice(g * size, (g + 1) * size)
        ordered_ref[g, :reach] = jnp.zeros((reach, rows), BF16)
        total = ordered_ref[g, reach:].astype(F32) * jnp.concatenate([gain_ref[here]] * blocks, axis=0)
        for p in range(pieces):
            slot = g * pieces + p
            left = jnp.concatenate(
                [
                    ordered_ref[g, (blocks - lag) * size : (2 * blocks - lag) * size]
                    for lag in range(p * lags, (p + 1) * lags)
                ],
                axis=1,
            )
            strip = shifted_rows(window_ref[slot : slot + 1, :], half).astype(BF16)
            right = jnp.concatenate(
                [
                    strip[:, shift : shift + rows]
                    for lag in range(1, lags + 1)
                    for shift in (lag * rows, lag * rows - half)
                ],
                axis=0,
            )
            total = total + jnp.dot(left, right, preferred_element_type=F32)
        for b, holder in enumerate(holders):
            out_ref[holder, here] = total[b * size : (b + 1) * size].astype(BF16)


def call_long(holder, mixed, keys, energy, windows, gain, size, full_width):
    blocks, shard, rows = mixed.shape

    def kernel(*refs):
        long_kernel(full_width, size, *refs)

    return pl.pallas_call(
        kernel,
        in_specs=[pl.BlockSpec(memory_space=pltpu.SMEM)]
        + [pl.BlockSpec(memory_space=pltpu.VMEM)] * 5,
        out_specs=pl.BlockSpec(memory_space=pltpu.VMEM),
        out_shape=jax.ShapeDtypeStruct((blocks, shard, rows), BF16),
        scratch_shapes=[pltpu.VMEM((shard // size, 2 * blocks * size, rows), BF16)],
        compiler_params=params(),
        name="long",
    )(holder, mixed, keys, energy, windows, gain)


def gate_kernel(mixed_ref, gate_ref, out_ref):
    for t in range(mixed_ref.shape[0]):
        lanes = slice(t * LANES, (t + 1) * LANES)
        mixed = jnp.transpose(mixed_ref[t]).astype(F32)
        out_ref[:, lanes] = (gate_ref[:, lanes].astype(F32) * mixed).astype(BF16)


def call_gate(mixed, q_two):
    rows, width = q_two.shape
    wide = GATE_TILES * LANES
    column = pl.BlockSpec((rows, wide), lambda i: (0, i))
    return pl.pallas_call(
        gate_kernel,
        grid=(width // wide,),
        in_specs=[pl.BlockSpec((GATE_TILES, LANES, rows), lambda i: (i, 0, 0)), column],
        out_specs=column,
        out_shape=jax.ShapeDtypeStruct((rows, width), BF16),
        compiler_params=params("arbitrary"),
        name="gate",
    )(mixed, q_two)


def exchange(array):
    return lax.all_to_all(array, "ctx", split_axis=0, concat_axis=0, tiled=True)


def sum_by_pairs(array, axis):
    count = lax.axis_size(axis)
    assert count & (count - 1) == 0
    bit = 1
    while bit < count:
        array = array + lax.ppermute(array, axis, [(i, i ^ bit) for i in range(count)])
        bit *= 2
    return array


def per_device(
    q_one,
    k_one,
    v_one,
    q_two,
    k_two,
    short_taps,
    medium_taps,
    long_taps,
    skip_gain,
    block_order,
    prev_owner,
):
    rows, width = q_one.shape
    ctx_count = lax.axis_size("ctx")
    tp_count = lax.axis_size("tp")
    me = lax.axis_index("ctx")
    size = width // short_taps.shape[2]
    tiles = width // LANES
    tile_groups = LANES // size
    shard = width // ctx_count
    shard_groups = shard // size
    full_width = width * tp_count

    slots = jnp.arange(ctx_count, dtype=jnp.int32)
    holder = jnp.sum(jnp.where(block_order[None, :] == slots[:, None], slots[None, :], 0), axis=1)

    packed = call_pack(q_one, k_one, v_one, short_taps, long_taps)
    span = 2 * EDGE
    if ctx_count != tiles:
        half = LANES // 2
        sizes = (LANES, half, span, EDGE, tile_groups)
        z, q, ends, more, taps = jnp.split(packed, [sum(sizes[:n]) for n in range(1, 5)], axis=1)
        q = jnp.transpose(q.reshape(tiles, half, 2, LANES), (0, 2, 1, 3))
        q = jnp.transpose(q.reshape(ctx_count, 2, shard // 2, LANES), (0, 2, 1, 3))
        ends = jnp.transpose(ends.reshape(tiles, span, 2, -1, shard), (0, 3, 1, 2, 4))
        more = jnp.transpose(more.reshape(tiles, EDGE, 2, -1, shard), (0, 3, 1, 2, 4))
        parts = [part.reshape(ctx_count, -1, rows) for part in (z, q, ends, more, taps)]
        packed = jnp.concatenate(parts, axis=1)
    moved = exchange(packed)
    ends_at = shard + shard // 2
    more_at = ends_at + span * 2 * shard // rows
    taps_at = more_at + EDGE * 2 * shard // rows
    ends = moved[:, ends_at:more_at].reshape(ctx_count, span, 2 * shard)
    more = moved[:, more_at:taps_at].reshape(ctx_count, EDGE, 2 * shard)

    early, early_energy = call_early(q_one, k_one, v_one, k_two, short_taps, medium_taps)
    early_energy = sum_by_pairs(early_energy, "tp")
    joined = call_join(k_two, early, early_energy, full_width)
    moved, joined = lax.optimization_barrier((moved, joined))

    short_local = lax.dynamic_slice_in_dim(short_taps, me * shard_groups, shard_groups, axis=2)
    medium_local = lax.dynamic_slice_in_dim(medium_taps, me * shard_groups, shard_groups, axis=1)
    mixed, energy = call_mix(holder, moved, ends, more, short_local, medium_local, shard, rows)
    energy, joined = lax.optimization_barrier((energy, joined))
    keys = exchange(joined.reshape(ctx_count, shard, rows))
    energy = sum_by_pairs(sum_by_pairs(energy, "tp"), "ctx")

    long_rows = moved[:, taps_at : taps_at + shard_groups]
    long_rows = jnp.transpose(long_rows, (1, 0, 2)).reshape(shard_groups, ctx_count * rows)
    windows = long_windows(long_rows, rows, min(ctx_count, 8))
    gain = lax.dynamic_slice_in_dim(skip_gain, me * shard, shard).reshape(shard, 1)
    filtered = call_long(
        holder, mixed, keys, energy, windows, gain, size, full_width
    )
    returned = exchange(filtered)
    return call_gate(returned.reshape(tiles, LANES, rows), q_two)


def solution(mesh):
    in_specs = (
        P("ctx", "tp"),
        P("ctx", "tp"),
        P("ctx", "tp"),
        P("ctx", "tp"),
        P("ctx", "tp"),
        P(None, None, "tp"),
        P(None, "tp"),
        P("tp", "ctx"),
        P("tp"),
        P(),
        P(),
    )
    out_specs = P("ctx", "tp")
    return jax.shard_map(
        per_device, mesh=mesh, in_specs=in_specs, out_specs=out_specs, check_vma=False
    )
```

```python
import jax
import jax.numpy as jnp
from jax import lax
from jax.experimental import pallas as pl
from jax.experimental.pallas import tpu as pltpu
from jax.sharding import PartitionSpec as P

EPSILON = 1e-06
LANES = 128
EDGE = 8
VMEM_BYTES = 24 * 1024 * 1024
PACK_TILES = 4
GATE_TILES = 4
F32 = jnp.float32
BF16 = jnp.bfloat16


def params(*semantics):
    return pltpu.CompilerParams(dimension_semantics=semantics, vmem_limit_bytes=VMEM_BYTES)


def in_hbm(array):
    return pltpu.with_memory_space_constraint(array, pltpu.HBM)


def lane_taps(taps_ref, which, size, width, first=0):
    groups = taps_ref.shape[2]
    group = lax.broadcasted_iota(jnp.int32, (groups, width), 0)
    lane = lax.broadcasted_iota(jnp.int32, (groups, width), 1) + first
    spread = (group == lane // size).astype(BF16)
    return jnp.dot(taps_ref[which], spread, preferred_element_type=F32)


def short_filter(extended, taps, start, rows):
    total = extended[start : start + rows] * taps[0:1]
    for j in range(1, taps.shape[0]):
        total = total + extended[start - j : start - j + rows] * taps[j : j + 1]
    return total


def pack_kernel(
    size, q_hbm, k_hbm, v_hbm, taps_hbm, long_hbm, out_ref, q_ref, k_ref, v_ref, taps_ref, long_ref, wide_ref, sems
):
    rows, width = q_hbm.shape
    tiles = width // LANES
    wide = PACK_TILES * LANES
    groups = LANES // size
    taps_copy = pltpu.make_async_copy(taps_hbm, taps_ref, sems.at[0, 3])
    taps_copy.start()
    parts = []
    for p in range(width // wide):
        lanes = pl.ds(p * wide, wide)
        copies = [
            pltpu.make_async_copy(source.at[:, lanes], target.at[:, lanes], sems.at[p, which])
            for which, (source, target) in enumerate(((k_hbm, k_ref), (v_hbm, v_ref), (q_hbm, q_ref)))
        ]
        for copy in copies:
            copy.start()
        parts.append(copies)
    long_copy = pltpu.make_async_copy(long_hbm, long_ref, sems.at[1, 3])
    long_copy.start()
    taps_copy.wait()
    taps = [lane_taps(taps_ref, which, size, width) for which in (1, 2)]
    for t in range(tiles):
        if t % PACK_TILES == 0:
            for copy in parts[t // PACK_TILES]:
                copy.wait()
        lanes = slice(t * LANES, (t + 1) * LANES)
        turned = jnp.transpose(q_ref[:LANES, lanes])
        at = LANES + LANES // 2
        out_ref[t, LANES:at, :] = jnp.concatenate([turned[: LANES // 2], turned[LANES // 2 :]], axis=1)
        features = []
        for which, ref in enumerate((k_ref, v_ref)):
            wide_ref[t, which, :EDGE] = jnp.zeros((EDGE, LANES), F32)
            wide_ref[t, which, EDGE:] = ref[:, lanes].astype(F32)
            features.append(short_filter(wide_ref.at[t, which], taps[which][:, lanes], EDGE, rows))
            ends = [wide_ref[t, which, EDGE : 2 * EDGE], wide_ref[t, which, rows : rows + EDGE]]
            out_ref[t, at : at + 2 * EDGE, which * LANES : (which + 1) * LANES] = (
                jnp.concatenate(ends, axis=0).astype(BF16)
            )
        out_ref[t, :LANES, :] = jnp.transpose((features[0] * features[1]).astype(BF16))
    long_copy.wait()
    for t in range(tiles):
        lanes = slice(t * LANES, (t + 1) * LANES)
        middle = q_ref[LANES : LANES + 2 * EDGE, lanes].astype(F32)[:EDGE]
        last = q_ref[rows - 2 * EDGE :, lanes].astype(F32)[EDGE:]
        here = long_ref[t * groups : (t + 1) * groups, :].astype(F32)
        lines = jnp.concatenate([jnp.concatenate([middle, last], axis=1), here], axis=0)
        out_ref[t, LANES + LANES // 2 + 2 * EDGE :, :] = lines.astype(BF16)


def call_pack(q_one, k_one, v_one, short_taps, long_taps):
    rows, width = q_one.shape
    tiles = width // LANES
    size = width // short_taps.shape[2]
    groups = LANES // size
    assert rows == 2 * LANES

    def kernel(*refs):
        pack_kernel(size, *refs)

    inputs = [in_hbm(array) for array in (q_one, k_one, v_one, short_taps, long_taps)]
    return pl.pallas_call(
        kernel,
        in_specs=[pl.BlockSpec(memory_space=pltpu.HBM)] * 5,
        out_specs=pl.BlockSpec(memory_space=pltpu.VMEM),
        out_shape=jax.ShapeDtypeStruct((tiles, LANES + LANES // 2 + 3 * EDGE + groups, rows), BF16),
        scratch_shapes=[
            pltpu.VMEM((rows, width), BF16),
            pltpu.VMEM((rows, width), BF16),
            pltpu.VMEM((rows, width), BF16),
            pltpu.VMEM(short_taps.shape, BF16),
            pltpu.VMEM(long_taps.shape, BF16),
            pltpu.VMEM((tiles, 2, EDGE + rows, LANES), F32),
            pltpu.SemaphoreType.DMA((tiles // PACK_TILES, 4)),
        ],
        compiler_params=params(),
        name="pack",
    )(*inputs)


def shifted_rows(row, count):
    return pltpu.roll(jnp.broadcast_to(row, (count, row.shape[1])), 0, 1, stride=1, stride_axis=0)


def long_windows(long_rows, rows, lags):
    groups, length = long_rows.shape
    reach = lags * rows
    padded = jnp.pad(long_rows.astype(F32), ((0, 0), (rows, 0)))
    pieces = [padded[:, p : p + reach + rows] for p in range(0, length, reach)]
    return jnp.stack(pieces, axis=1).reshape(-1, reach + rows)


def early_kernel(
    size, q_ref, k_ref, v_ref, gate_ref, taps_ref, base_ref, out_ref, energy_ref, extended_ref
):
    rows, width = q_ref.shape
    groups = LANES // size
    taps = [lane_taps(taps_ref, which, size, width) for which in range(3)]
    lane_group = lax.broadcasted_iota(jnp.int32, (1, LANES), 1) // size
    own = lax.broadcasted_iota(jnp.int32, (LANES, LANES), 0) >= EDGE
    squares = jnp.zeros((LANES, LANES), F32)
    for t in range(width // LANES):
        lanes = slice(t * LANES, (t + 1) * LANES)
        for which, ref in enumerate((q_ref, k_ref, v_ref)):
            extended_ref[t, which, :EDGE] = jnp.zeros((EDGE, LANES), F32)
            extended_ref[t, which, EDGE:] = ref[:, lanes].astype(F32)
        q_feat = short_filter(extended_ref.at[t, 0], taps[0][:, lanes], EDGE + LANES, LANES)
        k_feat = short_filter(extended_ref.at[t, 1], taps[1][:, lanes], EDGE, rows)
        v_feat = short_filter(extended_ref.at[t, 2], taps[2][:, lanes], EDGE, rows)
        table = jnp.concatenate(
            [
                shifted_rows(base_ref[g : g + 1, :], LANES).astype(BF16)
                for g in range(t * groups, (t + 1) * groups)
            ],
            axis=0,
        )
        every = jnp.dot(table, (k_feat * v_feat).astype(BF16), preferred_element_type=F32)
        medium = every[:LANES]
        for g in range(1, groups):
            medium = jnp.where(lane_group == g, every[g * LANES : (g + 1) * LANES], medium)
        mixed = jnp.where(own, q_feat * medium, 0.0)
        out_ref[t] = jnp.transpose(mixed * gate_ref[LANES:, lanes].astype(F32))
        squares = squares + mixed * mixed
    energy_ref[...] = jnp.sum(jnp.transpose(squares), axis=0, keepdims=True)


def call_early(q_one, k_one, v_one, k_two, short_taps, medium_taps):
    rows, width = q_one.shape
    tiles = width // LANES
    size = width // short_taps.shape[2]
    base = jnp.transpose(medium_taps[::-1])
    base = jnp.pad(base, ((0, 0), (1, rows - medium_taps.shape[0] - 1))).astype(F32)

    def kernel(*refs):
        early_kernel(size, *refs)

    return pl.pallas_call(
        kernel,
        in_specs=[pl.BlockSpec(memory_space=pltpu.VMEM)] * 6,
        out_specs=[pl.BlockSpec(memory_space=pltpu.VMEM)] * 2,
        out_shape=[
            jax.ShapeDtypeStruct((tiles, LANES, LANES), F32),
            jax.ShapeDtypeStruct((1, LANES), F32),
        ],
        scratch_shapes=[pltpu.VMEM((tiles, 3, EDGE + rows, LANES), F32)],
        compiler_params=params(),
        name="early",
    )(q_one, k_one, v_one, k_two, short_taps, base)


def join_kernel(full_width, gate_ref, early_ref, energy_ref, out_ref):
    scale = lax.rsqrt(energy_ref[...] / full_width + EPSILON)
    lane = lax.broadcasted_iota(jnp.int32, (LANES, LANES), 1)
    for t in range(out_ref.shape[0]):
        lanes = slice(t * LANES, (t + 1) * LANES)
        turned = jnp.transpose(gate_ref[:, lanes])
        values = jnp.where(lane < EDGE, turned[:, LANES:].astype(F32), early_ref[t] * scale)
        out_ref[t, :, :LANES] = turned[:, :LANES]
        out_ref[t, :, LANES:] = values.astype(BF16)


def call_join(k_two, early, energy, full_width):
    rows, width = k_two.shape

    def kernel(*refs):
        join_kernel(full_width, *refs)

    return pl.pallas_call(
        kernel,
        in_specs=[pl.BlockSpec(memory_space=pltpu.VMEM)] * 3,
        out_specs=pl.BlockSpec(memory_space=pltpu.VMEM),
        out_shape=jax.ShapeDtypeStruct((width // LANES, LANES, rows), BF16),
        compiler_params=params(),
        name="join",
    )(k_two, early, energy)


def mix_kernel(
    size,
    holder_ref,
    moved_ref,
    ends_ref,
    more_ref,
    taps_ref,
    q_base_ref,
    base_ref,
    out_ref,
    energy_ref,
    extended_ref,
    q_ends_ref,
    q_ref,
    z_ref,
    medium_ref,
):
    blocks, shard, rows = out_ref.shape
    halves = rows // LANES
    span = 2 * EDGE
    holders = [holder_ref[b] for b in range(blocks)]
    ends = [ends_ref[holder].astype(F32) for holder in holders]
    more = [more_ref[holder].astype(F32) for holder in holders]

    features = []
    for which in range(2):
        lanes = slice(which * shard, (which + 1) * shard)
        extended_ref[which, :EDGE] = jnp.zeros((EDGE, shard), F32)
        for b in range(blocks):
            before = ends[b - 1][EDGE:, lanes] if b else jnp.zeros((EDGE, shard), F32)
            at = EDGE + b * span
            extended_ref[which, at : at + span] = jnp.concatenate([before, ends[b][:EDGE, lanes]], axis=0)
        features.append(
            short_filter(extended_ref.at[which], taps_ref[which + 1], EDGE, blocks * span)
        )
    starts = jnp.transpose((features[0] * features[1]).astype(BF16))
    wide = blocks * span
    for b in range(blocks):
        before = more[b - 1][:, shard:] if b else jnp.zeros((EDGE, shard), F32)
        q_ends_ref[b * span : (b + 1) * span] = jnp.concatenate([before, more[b][:, :shard]], axis=0)
    q_ends = jnp.transpose(q_ends_ref[...].astype(BF16))

    lane = lax.broadcasted_iota(jnp.int32, (shard, LANES), 1)
    if wide == LANES:
        source = lax.broadcasted_iota(jnp.int32, (wide, blocks * LANES), 0)
        target = lax.broadcasted_iota(jnp.int32, (wide, blocks * LANES), 1)
        place = ((target + target // LANES * span + EDGE - source) % wide == 0).astype(F32).astype(BF16)
        both = jnp.dot(
            jnp.concatenate([starts, q_ends], axis=0), place, preferred_element_type=F32
        )
        firsts = [both[:shard, b * LANES : (b + 1) * LANES] for b in range(blocks)]
        arounds = [both[shard:, b * LANES : (b + 1) * LANES] for b in range(blocks)]
    else:
        firsts, arounds = [], []
        for b in range(blocks):
            shift = (wide - b * span - EDGE) % wide
            firsts.append(pltpu.roll(starts.astype(F32), shift, 1)[:, :LANES])
            turned = pltpu.roll(q_ends.astype(F32), shift, 1)
            arounds.append(jnp.where(lane < EDGE, turned[:, :LANES], turned[:, wide - LANES :]))

    half = shard // 2
    z_ref[:, :LANES] = jnp.zeros((shard, LANES), BF16)
    for b, holder in enumerate(holders):
        at = LANES + b * rows
        z_own = moved_ref[holder, :shard, :LANES].astype(F32)
        z_ref[:, at : at + LANES] = jnp.where(lane < EDGE, firsts[b], z_own).astype(BF16)
        z_ref[:, at + LANES : at + rows] = moved_ref[holder, :shard, LANES:]
        both = moved_ref[holder, shard : shard + half, :].astype(F32)
        q_own = jnp.concatenate([both[:, :LANES], both[:, LANES:]], axis=0)
        q_ref[b] = jnp.concatenate([q_own, arounds[b]], axis=1).astype(BF16)
    for g in range(shard // size):
        here = slice(g * size, (g + 1) * size)
        table = shifted_rows(q_base_ref[g : g + 1, :], 2 * LANES).astype(BF16)
        left = jnp.concatenate([q_ref[b, here] for b in range(blocks)], axis=0)
        q_feat = jnp.dot(left, table, preferred_element_type=F32)
        for b in range(blocks):
            out_ref[b, here] = q_feat[b * size : (b + 1) * size]
        table = shifted_rows(base_ref[g : g + 1, :], 2 * LANES)[:, :LANES].astype(BF16)
        windows = [z_ref[here, o * LANES : (o + 2) * LANES] for o in range(blocks * halves)]
        medium_ref[g] = jnp.dot(jnp.concatenate(windows, axis=0), table, preferred_element_type=F32)
    for o in range(blocks * halves):
        b, at = o // halves, (o % halves) * LANES
        medium = medium_ref[:, o * size : (o + 1) * size, :].reshape(shard, LANES)
        mixed = out_ref[b, :, at : at + LANES] * medium
        if at:
            mixed = jnp.where(lane < EDGE, mixed, 0.0)
        out_ref[b, :, at : at + LANES] = mixed
        energy_ref[o : o + 1, :] = jnp.sum(mixed * mixed, axis=0, keepdims=True)


def call_mix(holder, moved, ends, more, short_local, medium_local, shard, rows):
    blocks = moved.shape[0]
    size = shard // medium_local.shape[1]
    reach = medium_local.shape[0]
    assert reach == LANES and short_local.shape[1] <= EDGE + 1
    lane_form = jnp.repeat(short_local, size, axis=2).astype(F32)
    base = jnp.pad(jnp.transpose(medium_local).astype(F32), ((0, 0), (LANES, 0)))
    q_base = jnp.transpose(short_local[0]).astype(F32)
    q_base = jnp.pad(q_base, ((0, 0), (0, rows - q_base.shape[1])))

    def kernel(*refs):
        mix_kernel(size, *refs)

    return pl.pallas_call(
        kernel,
        in_specs=[pl.BlockSpec(memory_space=pltpu.SMEM)]
        + [pl.BlockSpec(memory_space=pltpu.VMEM)] * 6,
        out_specs=[pl.BlockSpec(memory_space=pltpu.VMEM)] * 2,
        out_shape=[
            jax.ShapeDtypeStruct((blocks, shard, rows), F32),
            jax.ShapeDtypeStruct((blocks * rows // LANES, LANES), F32),
        ],
        scratch_shapes=[
            pltpu.VMEM((2, EDGE + blocks * 2 * EDGE, shard), F32),
            pltpu.VMEM((blocks * 2 * EDGE, shard), F32),
            pltpu.VMEM((blocks, shard, rows), BF16),
            pltpu.VMEM((shard, LANES + blocks * rows), BF16),
            pltpu.VMEM((shard // size, blocks * rows // LANES * size, LANES), F32),
        ],
        compiler_params=params(),
        name="mix",
    )(holder, moved, ends, more, lane_form, q_base, base)


def long_kernel(
    full_width, size, holder_ref, mixed_ref, key_ref, energy_ref, window_ref, gain_ref, out_ref, ordered_ref
):
    blocks, shard, rows = mixed_ref.shape
    half = rows // 2
    halves = rows // LANES
    lags = window_ref.shape[1] // rows - 1
    pieces = blocks // lags
    reach = blocks * size
    holders = [holder_ref[b] for b in range(blocks)]
    scale = lax.rsqrt(energy_ref[...] / full_width + EPSILON)
    own = lax.broadcasted_iota(jnp.int32, (size, rows), 1) >= LANES + EDGE
    for b, holder in enumerate(holders):
        line = jnp.concatenate([scale[o : o + 1] for o in range(b * halves, (b + 1) * halves)], axis=1)
        for g in range(shard // size):
            here = slice(g * size, (g + 1) * size)
            key = key_ref[holder, here].astype(F32)
            value = jnp.where(own, key, key * mixed_ref[b, here] * line)
            ordered_ref[g, reach + b * size : reach + (b + 1) * size] = value.astype(BF16)
    for g in range(shard // size):
        here = slice(g * size, (g + 1) * size)
        ordered_ref[g, :reach] = jnp.zeros((reach, rows), BF16)
        total = ordered_ref[g, reach:].astype(F32) * jnp.concatenate([gain_ref[here]] * blocks, axis=0)
        for p in range(pieces):
            slot = g * pieces + p
            left = jnp.concatenate(
                [
                    ordered_ref[g, (blocks - lag) * size : (2 * blocks - lag) * size]
                    for lag in range(p * lags, (p + 1) * lags)
                ],
                axis=1,
            )
            strip = shifted_rows(window_ref[slot : slot + 1, :], half).astype(BF16)
            right = jnp.concatenate(
                [
                    strip[:, shift : shift + rows]
                    for lag in range(1, lags + 1)
                    for shift in (lag * rows, lag * rows - half)
                ],
                axis=0,
            )
            total = total + jnp.dot(left, right, preferred_element_type=F32)
        for b, holder in enumerate(holders):
            out_ref[holder, here] = total[b * size : (b + 1) * size].astype(BF16)


def call_long(holder, mixed, keys, energy, windows, gain, size, full_width):
    blocks, shard, rows = mixed.shape

    def kernel(*refs):
        long_kernel(full_width, size, *refs)

    return pl.pallas_call(
        kernel,
        in_specs=[pl.BlockSpec(memory_space=pltpu.SMEM)]
        + [pl.BlockSpec(memory_space=pltpu.VMEM)] * 5,
        out_specs=pl.BlockSpec(memory_space=pltpu.VMEM),
        out_shape=jax.ShapeDtypeStruct((blocks, shard, rows), BF16),
        scratch_shapes=[pltpu.VMEM((shard // size, 2 * blocks * size, rows), BF16)],
        compiler_params=params(),
        name="long",
    )(holder, mixed, keys, energy, windows, gain)


def gate_kernel(mixed_ref, gate_ref, out_ref):
    for t in range(mixed_ref.shape[0]):
        lanes = slice(t * LANES, (t + 1) * LANES)
        mixed = jnp.transpose(mixed_ref[t]).astype(F32)
        out_ref[:, lanes] = (gate_ref[:, lanes].astype(F32) * mixed).astype(BF16)


def call_gate(mixed, q_two):
    rows, width = q_two.shape
    wide = GATE_TILES * LANES
    column = pl.BlockSpec((rows, wide), lambda i: (0, i))
    return pl.pallas_call(
        gate_kernel,
        grid=(width // wide,),
        in_specs=[pl.BlockSpec((GATE_TILES, LANES, rows), lambda i: (i, 0, 0)), column],
        out_specs=column,
        out_shape=jax.ShapeDtypeStruct((rows, width), BF16),
        compiler_params=params("arbitrary"),
        name="gate",
    )(mixed, q_two)


def exchange(array):
    return lax.all_to_all(array, "ctx", split_axis=0, concat_axis=0, tiled=True)


def sum_by_pairs(array, axis):
    count = lax.axis_size(axis)
    assert count & (count - 1) == 0
    bit = 1
    while bit < count:
        array = array + lax.ppermute(array, axis, [(i, i ^ bit) for i in range(count)])
        bit *= 2
    return array


def per_device(
    q_one,
    k_one,
    v_one,
    q_two,
    k_two,
    short_taps,
    medium_taps,
    long_taps,
    skip_gain,
    block_order,
    prev_owner,
):
    rows, width = q_one.shape
    ctx_count = lax.axis_size("ctx")
    tp_count = lax.axis_size("tp")
    me = lax.axis_index("ctx")
    size = width // short_taps.shape[2]
    tiles = width // LANES
    tile_groups = LANES // size
    shard = width // ctx_count
    shard_groups = shard // size
    full_width = width * tp_count

    slots = jnp.arange(ctx_count, dtype=jnp.int32)
    holder = jnp.sum(jnp.where(block_order[None, :] == slots[:, None], slots[None, :], 0), axis=1)

    packed = call_pack(q_one, k_one, v_one, short_taps, long_taps)
    span = 2 * EDGE
    if ctx_count != tiles:
        half = LANES // 2
        sizes = (LANES, half, span, EDGE, tile_groups)
        z, q, ends, more, taps = jnp.split(packed, [sum(sizes[:n]) for n in range(1, 5)], axis=1)
        q = jnp.transpose(q.reshape(tiles, half, 2, LANES), (0, 2, 1, 3))
        q = jnp.transpose(q.reshape(ctx_count, 2, shard // 2, LANES), (0, 2, 1, 3))
        ends = jnp.transpose(ends.reshape(tiles, span, 2, -1, shard), (0, 3, 1, 2, 4))
        more = jnp.transpose(more.reshape(tiles, EDGE, 2, -1, shard), (0, 3, 1, 2, 4))
        parts = [part.reshape(ctx_count, -1, rows) for part in (z, q, ends, more, taps)]
        packed = jnp.concatenate(parts, axis=1)
    moved = exchange(packed)
    ends_at = shard + shard // 2
    more_at = ends_at + span * 2 * shard // rows
    taps_at = more_at + EDGE * 2 * shard // rows
    ends = moved[:, ends_at:more_at].reshape(ctx_count, span, 2 * shard)
    more = moved[:, more_at:taps_at].reshape(ctx_count, EDGE, 2 * shard)

    early, early_energy = call_early(q_one, k_one, v_one, k_two, short_taps, medium_taps)
    early_energy = sum_by_pairs(early_energy, "tp")
    joined = call_join(k_two, early, early_energy, full_width)
    moved, joined = lax.optimization_barrier((moved, joined))

    short_local = lax.dynamic_slice_in_dim(short_taps, me * shard_groups, shard_groups, axis=2)
    medium_local = lax.dynamic_slice_in_dim(medium_taps, me * shard_groups, shard_groups, axis=1)
    mixed, energy = call_mix(holder, moved, ends, more, short_local, medium_local, shard, rows)
    energy, joined = lax.optimization_barrier((energy, joined))
    keys = exchange(joined.reshape(ctx_count, shard, rows))
    energy = sum_by_pairs(sum_by_pairs(energy, "tp"), "ctx")

    long_rows = moved[:, taps_at : taps_at + shard_groups]
    long_rows = jnp.transpose(long_rows, (1, 0, 2)).reshape(shard_groups, ctx_count * rows)
    windows = long_windows(long_rows, rows, min(ctx_count, 8))
    gain = lax.dynamic_slice_in_dim(skip_gain, me * shard, shard).reshape(shard, 1)
    filtered = call_long(
        holder, mixed, keys, energy, windows, gain, size, full_width
    )
    returned = exchange(filtered)
    return call_gate(returned.reshape(tiles, LANES, rows), q_two)


def solution(mesh):
    in_specs = (
        P("ctx", "tp"),
        P("ctx", "tp"),
        P("ctx", "tp"),
        P("ctx", "tp"),
        P("ctx", "tp"),
        P(None, None, "tp"),
        P(None, "tp"),
        P("tp", "ctx"),
        P("tp"),
        P(),
        P(),
    )
    out_specs = P("ctx", "tp")
    return jax.shard_map(
        per_device, mesh=mesh, in_specs=in_specs, out_specs=out_specs, check_vma=False
    )
```

```python
import jax
import jax.numpy as jnp
from jax import lax
from jax.experimental import pallas as pl
from jax.experimental.pallas import tpu as pltpu
from jax.sharding import PartitionSpec as P

EPSILON = 1e-06
LANES = 128
EDGE = 8
VMEM_BYTES = 24 * 1024 * 1024
PACK_TILES = 4
GATE_TILES = 4
F32 = jnp.float32
BF16 = jnp.bfloat16


def params(*semantics):
    return pltpu.CompilerParams(dimension_semantics=semantics, vmem_limit_bytes=VMEM_BYTES)


def in_hbm(array):
    return pltpu.with_memory_space_constraint(array, pltpu.HBM)


def lane_taps(taps_ref, which, size, width, first=0):
    groups = taps_ref.shape[2]
    group = lax.broadcasted_iota(jnp.int32, (groups, width), 0)
    lane = lax.broadcasted_iota(jnp.int32, (groups, width), 1) + first
    spread = (group == lane // size).astype(BF16)
    return jnp.dot(taps_ref[which], spread, preferred_element_type=F32)


def short_filter(extended, taps, start, rows):
    total = extended[start : start + rows] * taps[0:1]
    for j in range(1, taps.shape[0]):
        total = total + extended[start - j : start - j + rows] * taps[j : j + 1]
    return total


def pack_kernel(
    size, q_hbm, k_hbm, v_hbm, taps_hbm, long_hbm, out_ref, q_ref, k_ref, v_ref, taps_ref, long_ref, wide_ref, sems
):
    rows, width = q_hbm.shape
    tiles = width // LANES
    wide = PACK_TILES * LANES
    groups = LANES // size
    taps_copy = pltpu.make_async_copy(taps_hbm, taps_ref, sems.at[0, 3])
    taps_copy.start()
    parts = []
    for p in range(width // wide):
        lanes = pl.ds(p * wide, wide)
        copies = [
            pltpu.make_async_copy(source.at[:, lanes], target.at[:, lanes], sems.at[p, which])
            for which, (source, target) in enumerate(((k_hbm, k_ref), (v_hbm, v_ref), (q_hbm, q_ref)))
        ]
        for copy in copies:
            copy.start()
        parts.append(copies)
    long_copy = pltpu.make_async_copy(long_hbm, long_ref, sems.at[1, 3])
    long_copy.start()
    taps_copy.wait()
    taps = [lane_taps(taps_ref, which, size, width) for which in (1, 2)]
    for t in range(tiles):
        if t % PACK_TILES == 0:
            for copy in parts[t // PACK_TILES]:
                copy.wait()
        lanes = slice(t * LANES, (t + 1) * LANES)
        turned = jnp.transpose(q_ref[:LANES, lanes])
        at = LANES + LANES // 2
        out_ref[t, LANES:at, :] = jnp.concatenate([turned[: LANES // 2], turned[LANES // 2 :]], axis=1)
        features = []
        for which, ref in enumerate((k_ref, v_ref)):
            wide_ref[t, which, :EDGE] = jnp.zeros((EDGE, LANES), F32)
            wide_ref[t, which, EDGE:] = ref[:, lanes].astype(F32)
            features.append(short_filter(wide_ref.at[t, which], taps[which][:, lanes], EDGE, rows))
            ends = [wide_ref[t, which, EDGE : 2 * EDGE], wide_ref[t, which, rows : rows + EDGE]]
            out_ref[t, at : at + 2 * EDGE, which * LANES : (which + 1) * LANES] = (
                jnp.concatenate(ends, axis=0).astype(BF16)
            )
        out_ref[t, :LANES, :] = jnp.transpose((features[0] * features[1]).astype(BF16))
    long_copy.wait()
    for t in range(tiles):
        lanes = slice(t * LANES, (t + 1) * LANES)
        middle = q_ref[LANES : LANES + 2 * EDGE, lanes].astype(F32)[:EDGE]
        last = q_ref[rows - 2 * EDGE :, lanes].astype(F32)[EDGE:]
        here = long_ref[t * groups : (t + 1) * groups, :].astype(F32)
        lines = jnp.concatenate([jnp.concatenate([middle, last], axis=1), here], axis=0)
        out_ref[t, LANES + LANES // 2 + 2 * EDGE :, :] = lines.astype(BF16)


def call_pack(q_one, k_one, v_one, short_taps, long_taps):
    rows, width = q_one.shape
    tiles = width // LANES
    size = width // short_taps.shape[2]
    groups = LANES // size
    assert rows == 2 * LANES

    def kernel(*refs):
        pack_kernel(size, *refs)

    inputs = [in_hbm(array) for array in (q_one, k_one, v_one, short_taps, long_taps)]
    return pl.pallas_call(
        kernel,
        in_specs=[pl.BlockSpec(memory_space=pltpu.HBM)] * 5,
        out_specs=pl.BlockSpec(memory_space=pltpu.VMEM),
        out_shape=jax.ShapeDtypeStruct((tiles, LANES + LANES // 2 + 3 * EDGE + groups, rows), BF16),
        scratch_shapes=[
            pltpu.VMEM((rows, width), BF16),
            pltpu.VMEM((rows, width), BF16),
            pltpu.VMEM((rows, width), BF16),
            pltpu.VMEM(short_taps.shape, BF16),
            pltpu.VMEM(long_taps.shape, BF16),
            pltpu.VMEM((tiles, 2, EDGE + rows, LANES), F32),
            pltpu.SemaphoreType.DMA((tiles // PACK_TILES, 4)),
        ],
        compiler_params=params(),
        name="pack",
    )(*inputs)


def shifted_rows(row, count):
    return pltpu.roll(jnp.broadcast_to(row, (count, row.shape[1])), 0, 1, stride=1, stride_axis=0)


def long_windows(long_rows, rows, lags):
    groups, length = long_rows.shape
    reach = lags * rows
    padded = jnp.pad(long_rows.astype(F32), ((0, 0), (rows, 0)))
    pieces = [padded[:, p : p + reach + rows] for p in range(0, length, reach)]
    return jnp.stack(pieces, axis=1).reshape(-1, reach + rows)


def early_kernel(
    size, q_ref, k_ref, v_ref, gate_ref, taps_ref, base_ref, out_ref, energy_ref, extended_ref
):
    rows, width = q_ref.shape
    groups = LANES // size
    taps = [lane_taps(taps_ref, which, size, width) for which in range(3)]
    lane_group = lax.broadcasted_iota(jnp.int32, (1, LANES), 1) // size
    own = lax.broadcasted_iota(jnp.int32, (LANES, LANES), 0) >= EDGE
    squares = jnp.zeros((LANES, LANES), F32)
    for t in range(width // LANES):
        lanes = slice(t * LANES, (t + 1) * LANES)
        for which, ref in enumerate((q_ref, k_ref, v_ref)):
            extended_ref[t, which, :EDGE] = jnp.zeros((EDGE, LANES), F32)
            extended_ref[t, which, EDGE:] = ref[:, lanes].astype(F32)
        q_feat = short_filter(extended_ref.at[t, 0], taps[0][:, lanes], EDGE + LANES, LANES)
        k_feat = short_filter(extended_ref.at[t, 1], taps[1][:, lanes], EDGE, rows)
        v_feat = short_filter(extended_ref.at[t, 2], taps[2][:, lanes], EDGE, rows)
        table = jnp.concatenate(
            [
                shifted_rows(base_ref[g : g + 1, :], LANES).astype(BF16)
                for g in range(t * groups, (t + 1) * groups)
            ],
            axis=0,
        )
        every = jnp.dot(table, (k_feat * v_feat).astype(BF16), preferred_element_type=F32)
        medium = every[:LANES]
        for g in range(1, groups):
            medium = jnp.where(lane_group == g, every[g * LANES : (g + 1) * LANES], medium)
        mixed = jnp.where(own, q_feat * medium, 0.0)
        out_ref[t] = jnp.transpose(mixed * gate_ref[LANES:, lanes].astype(F32))
        squares = squares + mixed * mixed
    energy_ref[...] = jnp.sum(jnp.transpose(squares), axis=0, keepdims=True)


def call_early(q_one, k_one, v_one, k_two, short_taps, medium_taps):
    rows, width = q_one.shape
    tiles = width // LANES
    size = width // short_taps.shape[2]
    base = jnp.transpose(medium_taps[::-1])
    base = jnp.pad(base, ((0, 0), (1, rows - medium_taps.shape[0] - 1))).astype(F32)

    def kernel(*refs):
        early_kernel(size, *refs)

    return pl.pallas_call(
        kernel,
        in_specs=[pl.BlockSpec(memory_space=pltpu.VMEM)] * 6,
        out_specs=[pl.BlockSpec(memory_space=pltpu.VMEM)] * 2,
        out_shape=[
            jax.ShapeDtypeStruct((tiles, LANES, LANES), F32),
            jax.ShapeDtypeStruct((1, LANES), F32),
        ],
        scratch_shapes=[pltpu.VMEM((tiles, 3, EDGE + rows, LANES), F32)],
        compiler_params=params(),
        name="early",
    )(q_one, k_one, v_one, k_two, short_taps, base)


def join_kernel(full_width, gate_ref, early_ref, energy_ref, out_ref):
    scale = lax.rsqrt(energy_ref[...] / full_width + EPSILON)
    lane = lax.broadcasted_iota(jnp.int32, (LANES, LANES), 1)
    for t in range(out_ref.shape[0]):
        lanes = slice(t * LANES, (t + 1) * LANES)
        turned = jnp.transpose(gate_ref[:, lanes])
        values = jnp.where(lane < EDGE, turned[:, LANES:].astype(F32), early_ref[t] * scale)
        out_ref[t, :, :LANES] = turned[:, :LANES]
        out_ref[t, :, LANES:] = values.astype(BF16)


def call_join(k_two, early, energy, full_width):
    rows, width = k_two.shape

    def kernel(*refs):
        join_kernel(full_width, *refs)

    return pl.pallas_call(
        kernel,
        in_specs=[pl.BlockSpec(memory_space=pltpu.VMEM)] * 3,
        out_specs=pl.BlockSpec(memory_space=pltpu.VMEM),
        out_shape=jax.ShapeDtypeStruct((width // LANES, LANES, rows), BF16),
        compiler_params=params(),
        name="join",
    )(k_two, early, energy)


def mix_kernel(
    size,
    holder_ref,
    moved_ref,
    ends_ref,
    more_ref,
    taps_ref,
    q_base_ref,
    base_ref,
    out_ref,
    energy_ref,
    extended_ref,
    q_ends_ref,
    q_ref,
    z_ref,
    medium_ref,
):
    blocks, shard, rows = out_ref.shape
    halves = rows // LANES
    span = 2 * EDGE
    holders = [holder_ref[b] for b in range(blocks)]
    ends = [ends_ref[holder].astype(F32) for holder in holders]
    more = [more_ref[holder].astype(F32) for holder in holders]

    features = []
    for which in range(2):
        lanes = slice(which * shard, (which + 1) * shard)
        extended_ref[which, :EDGE] = jnp.zeros((EDGE, shard), F32)
        for b in range(blocks):
            before = ends[b - 1][EDGE:, lanes] if b else jnp.zeros((EDGE, shard), F32)
            at = EDGE + b * span
            extended_ref[which, at : at + span] = jnp.concatenate([before, ends[b][:EDGE, lanes]], axis=0)
        features.append(
            short_filter(extended_ref.at[which], taps_ref[which + 1], EDGE, blocks * span)
        )
    starts = jnp.transpose((features[0] * features[1]).astype(BF16))
    wide = blocks * span
    for b in range(blocks):
        before = more[b - 1][:, shard:] if b else jnp.zeros((EDGE, shard), F32)
        q_ends_ref[b * span : (b + 1) * span] = jnp.concatenate([before, more[b][:, :shard]], axis=0)
    q_ends = jnp.transpose(q_ends_ref[...].astype(BF16))

    lane = lax.broadcasted_iota(jnp.int32, (shard, LANES), 1)
    if wide == LANES:
        source = lax.broadcasted_iota(jnp.int32, (wide, blocks * LANES), 0)
        target = lax.broadcasted_iota(jnp.int32, (wide, blocks * LANES), 1)
        place = ((target + target // LANES * span + EDGE - source) % wide == 0).astype(F32).astype(BF16)
        both = jnp.dot(
            jnp.concatenate([starts, q_ends], axis=0), place, preferred_element_type=F32
        )
        firsts = [both[:shard, b * LANES : (b + 1) * LANES] for b in range(blocks)]
        arounds = [both[shard:, b * LANES : (b + 1) * LANES] for b in range(blocks)]
    else:
        firsts, arounds = [], []
        for b in range(blocks):
            shift = (wide - b * span - EDGE) % wide
            firsts.append(pltpu.roll(starts.astype(F32), shift, 1)[:, :LANES])
            turned = pltpu.roll(q_ends.astype(F32), shift, 1)
            arounds.append(jnp.where(lane < EDGE, turned[:, :LANES], turned[:, wide - LANES :]))

    half = shard // 2
    z_ref[:, :LANES] = jnp.zeros((shard, LANES), BF16)
    for b, holder in enumerate(holders):
        at = LANES + b * rows
        z_own = moved_ref[holder, :shard, :LANES].astype(F32)
        z_ref[:, at : at + LANES] = jnp.where(lane < EDGE, firsts[b], z_own).astype(BF16)
        z_ref[:, at + LANES : at + rows] = moved_ref[holder, :shard, LANES:]
        both = moved_ref[holder, shard : shard + half, :].astype(F32)
        q_own = jnp.concatenate([both[:, :LANES], both[:, LANES:]], axis=0)
        q_ref[b] = jnp.concatenate([q_own, arounds[b]], axis=1).astype(BF16)
    for g in range(shard // size):
        here = slice(g * size, (g + 1) * size)
        table = shifted_rows(q_base_ref[g : g + 1, :], 2 * LANES).astype(BF16)
        left = jnp.concatenate([q_ref[b, here] for b in range(blocks)], axis=0)
        q_feat = jnp.dot(left, table, preferred_element_type=F32)
        for b in range(blocks):
            out_ref[b, here] = q_feat[b * size : (b + 1) * size]
        table = shifted_rows(base_ref[g : g + 1, :], 2 * LANES)[:, :LANES].astype(BF16)
        windows = [z_ref[here, o * LANES : (o + 2) * LANES] for o in range(blocks * halves)]
        medium_ref[g] = jnp.dot(jnp.concatenate(windows, axis=0), table, preferred_element_type=F32)
    for o in range(blocks * halves):
        b, at = o // halves, (o % halves) * LANES
        medium = medium_ref[:, o * size : (o + 1) * size, :].reshape(shard, LANES)
        mixed = out_ref[b, :, at : at + LANES] * medium
        if at:
            mixed = jnp.where(lane < EDGE, mixed, 0.0)
        out_ref[b, :, at : at + LANES] = mixed
        energy_ref[o : o + 1, :] = jnp.sum(mixed * mixed, axis=0, keepdims=True)


def call_mix(holder, moved, ends, more, short_local, medium_local, shard, rows):
    blocks = moved.shape[0]
    size = shard // medium_local.shape[1]
    reach = medium_local.shape[0]
    assert reach == LANES and short_local.shape[1] <= EDGE + 1
    lane_form = jnp.repeat(short_local, size, axis=2).astype(F32)
    base = jnp.pad(jnp.transpose(medium_local).astype(F32), ((0, 0), (LANES, 0)))
    q_base = jnp.transpose(short_local[0]).astype(F32)
    q_base = jnp.pad(q_base, ((0, 0), (0, rows - q_base.shape[1])))

    def kernel(*refs):
        mix_kernel(size, *refs)

    return pl.pallas_call(
        kernel,
        in_specs=[pl.BlockSpec(memory_space=pltpu.SMEM)]
        + [pl.BlockSpec(memory_space=pltpu.VMEM)] * 6,
        out_specs=[pl.BlockSpec(memory_space=pltpu.VMEM)] * 2,
        out_shape=[
            jax.ShapeDtypeStruct((blocks, shard, rows), F32),
            jax.ShapeDtypeStruct((blocks * rows // LANES, LANES), F32),
        ],
        scratch_shapes=[
            pltpu.VMEM((2, EDGE + blocks * 2 * EDGE, shard), F32),
            pltpu.VMEM((blocks * 2 * EDGE, shard), F32),
            pltpu.VMEM((blocks, shard, rows), BF16),
            pltpu.VMEM((shard, LANES + blocks * rows), BF16),
            pltpu.VMEM((shard // size, blocks * rows // LANES * size, LANES), F32),
        ],
        compiler_params=params(),
        name="mix",
    )(holder, moved, ends, more, lane_form, q_base, base)


def long_kernel(
    full_width, size, holder_ref, mixed_ref, key_ref, energy_ref, window_ref, gain_ref, out_ref, ordered_ref, strip_ref
):
    blocks, shard, rows = mixed_ref.shape
    half = rows // 2
    halves = rows // LANES
    lags = window_ref.shape[1] // rows - 1
    pieces = blocks // lags
    reach = blocks * size
    holders = [holder_ref[b] for b in range(blocks)]
    scale = lax.rsqrt(energy_ref[...] / full_width + EPSILON)
    own = lax.broadcasted_iota(jnp.int32, (size, rows), 1) >= LANES + EDGE
    for b, holder in enumerate(holders):
        line = jnp.concatenate([scale[o : o + 1] for o in range(b * halves, (b + 1) * halves)], axis=1)
        for g in range(shard // size):
            here = slice(g * size, (g + 1) * size)
            key = key_ref[holder, here].astype(F32)
            value = jnp.where(own, key, key * mixed_ref[b, here] * line)
            ordered_ref[g, reach + b * size : reach + (b + 1) * size] = value.astype(BF16)
    for slot in range(window_ref.shape[0]):
        strip_ref[slot] = shifted_rows(window_ref[slot : slot + 1, :], half)[:, half:].astype(BF16)
    for g in range(shard // size):
        here = slice(g * size, (g + 1) * size)
        ordered_ref[g, :reach] = jnp.zeros((reach, rows), BF16)
        total = ordered_ref[g, reach:].astype(F32) * jnp.concatenate([gain_ref[here]] * blocks, axis=0)
        for p in range(pieces):
            slot = g * pieces + p
            left = jnp.concatenate(
                [
                    ordered_ref[g, (blocks - lag) * size : (2 * blocks - lag) * size]
                    for lag in range(p * lags, (p + 1) * lags)
                ],
                axis=1,
            )
            right = jnp.concatenate(
                [
                    strip_ref[slot, :, shift - half : shift - half + rows]
                    for lag in range(1, lags + 1)
                    for shift in (lag * rows, lag * rows - half)
                ],
                axis=0,
            )
            total = total + jnp.dot(left, right, preferred_element_type=F32)
        for b, holder in enumerate(holders):
            out_ref[holder, here] = total[b * size : (b + 1) * size].astype(BF16)


def call_long(holder, mixed, keys, energy, windows, gain, size, full_width):
    blocks, shard, rows = mixed.shape

    def kernel(*refs):
        long_kernel(full_width, size, *refs)

    return pl.pallas_call(
        kernel,
        in_specs=[pl.BlockSpec(memory_space=pltpu.SMEM)]
        + [pl.BlockSpec(memory_space=pltpu.VMEM)] * 5,
        out_specs=pl.BlockSpec(memory_space=pltpu.VMEM),
        out_shape=jax.ShapeDtypeStruct((blocks, shard, rows), BF16),
        scratch_shapes=[pltpu.VMEM((shard // size, 2 * blocks * size, rows), BF16), pltpu.VMEM((windows.shape[0], rows // 2, windows.shape[1] - rows // 2), BF16)],
        compiler_params=params(),
        name="long",
    )(holder, mixed, keys, energy, windows, gain)


def gate_kernel(mixed_ref, gate_ref, out_hbm, out_ref, sems):
    copies = []
    for t in range(mixed_ref.shape[0]):
        lanes = slice(t * LANES, (t + 1) * LANES)
        mixed = jnp.transpose(mixed_ref[t]).astype(F32)
        out_ref[:, lanes] = (gate_ref[:, lanes].astype(F32) * mixed).astype(BF16)
        if (t + 1) % GATE_TILES == 0:
            part = t // GATE_TILES
            done = pl.ds(part * GATE_TILES * LANES, GATE_TILES * LANES)
            copy = pltpu.make_async_copy(out_ref.at[:, done], out_hbm.at[:, done], sems.at[part])
            copy.start()
            copies.append(copy)
    for copy in copies:
        copy.wait()


def call_gate(mixed, q_two):
    rows, width = q_two.shape
    return pl.pallas_call(
        gate_kernel,
        in_specs=[pl.BlockSpec(memory_space=pltpu.VMEM)] * 2,
        out_specs=pl.BlockSpec(memory_space=pltpu.HBM),
        out_shape=pltpu.HBM((rows, width), BF16),
        scratch_shapes=[
            pltpu.VMEM((rows, width), BF16),
            pltpu.SemaphoreType.DMA((width // LANES // GATE_TILES,)),
        ],
        compiler_params=params(),
        name="gate",
    )(mixed, q_two)


def exchange(array):
    return lax.all_to_all(array, "ctx", split_axis=0, concat_axis=0, tiled=True)


def sum_by_pairs(array, axis):
    count = lax.axis_size(axis)
    assert count & (count - 1) == 0
    bit = 1
    while bit < count:
        array = array + lax.ppermute(array, axis, [(i, i ^ bit) for i in range(count)])
        bit *= 2
    return array


def sum_over_all(array):
    axes = ("ctx", "tp")
    count = lax.axis_size("ctx") * lax.axis_size("tp")
    assert count & (count - 1) == 0
    masks, bit = [1], 2
    while True:
        parts = [lax.ppermute(array, axes, [(i, i ^ mask) for i in range(count)]) for mask in masks]
        for part in parts:
            array = array + part
        if bit >= count:
            return array
        masks = [bit, 2 * bit, 3 * bit] if 2 * bit < count else [bit]
        bit *= 4


def per_device(
    q_one,
    k_one,
    v_one,
    q_two,
    k_two,
    short_taps,
    medium_taps,
    long_taps,
    skip_gain,
    block_order,
    prev_owner,
):
    rows, width = q_one.shape
    ctx_count = lax.axis_size("ctx")
    tp_count = lax.axis_size("tp")
    me = lax.axis_index("ctx")
    size = width // short_taps.shape[2]
    tiles = width // LANES
    tile_groups = LANES // size
    shard = width // ctx_count
    shard_groups = shard // size
    full_width = width * tp_count

    slots = jnp.arange(ctx_count, dtype=jnp.int32)
    holder = jnp.sum(jnp.where(block_order[None, :] == slots[:, None], slots[None, :], 0), axis=1)

    packed = call_pack(q_one, k_one, v_one, short_taps, long_taps)
    span = 2 * EDGE
    if ctx_count != tiles:
        half = LANES // 2
        sizes = (LANES, half, span, EDGE, tile_groups)
        z, q, ends, more, taps = jnp.split(packed, [sum(sizes[:n]) for n in range(1, 5)], axis=1)
        q = jnp.transpose(q.reshape(tiles, half, 2, LANES), (0, 2, 1, 3))
        q = jnp.transpose(q.reshape(ctx_count, 2, shard // 2, LANES), (0, 2, 1, 3))
        ends = jnp.transpose(ends.reshape(tiles, span, 2, -1, shard), (0, 3, 1, 2, 4))
        more = jnp.transpose(more.reshape(tiles, EDGE, 2, -1, shard), (0, 3, 1, 2, 4))
        parts = [part.reshape(ctx_count, -1, rows) for part in (z, q, ends, more, taps)]
        packed = jnp.concatenate(parts, axis=1)
    moved = exchange(packed)
    ends_at = shard + shard // 2
    more_at = ends_at + span * 2 * shard // rows
    taps_at = more_at + EDGE * 2 * shard // rows
    ends = moved[:, ends_at:more_at].reshape(ctx_count, span, 2 * shard)
    more = moved[:, more_at:taps_at].reshape(ctx_count, EDGE, 2 * shard)

    early, early_energy = call_early(q_one, k_one, v_one, k_two, short_taps, medium_taps)
    early_energy = sum_by_pairs(early_energy, "tp")
    joined = call_join(k_two, early, early_energy, full_width)
    moved, joined = lax.optimization_barrier((moved, joined))

    short_local = lax.dynamic_slice_in_dim(short_taps, me * shard_groups, shard_groups, axis=2)
    medium_local = lax.dynamic_slice_in_dim(medium_taps, me * shard_groups, shard_groups, axis=1)
    mixed, energy = call_mix(holder, moved, ends, more, short_local, medium_local, shard, rows)
    energy, joined = lax.optimization_barrier((energy, joined))
    keys = exchange(joined.reshape(ctx_count, shard, rows))
    energy = sum_over_all(energy)

    long_rows = moved[:, taps_at : taps_at + shard_groups]
    long_rows = jnp.transpose(long_rows, (1, 0, 2)).reshape(shard_groups, ctx_count * rows)
    windows = long_windows(long_rows, rows, min(ctx_count, 8))
    gain = lax.dynamic_slice_in_dim(skip_gain, me * shard, shard).reshape(shard, 1)
    filtered = call_long(
        holder, mixed, keys, energy, windows, gain, size, full_width
    )
    returned = exchange(filtered)
    return call_gate(returned.reshape(tiles, LANES, rows), q_two)


def solution(mesh):
    in_specs = (
        P("ctx", "tp"),
        P("ctx", "tp"),
        P("ctx", "tp"),
        P("ctx", "tp"),
        P("ctx", "tp"),
        P(None, None, "tp"),
        P(None, "tp"),
        P("tp", "ctx"),
        P("tp"),
        P(),
        P(),
    )
    out_specs = P("ctx", "tp")
    return jax.shard_map(
        per_device, mesh=mesh, in_specs=in_specs, out_specs=out_specs, check_vma=False
    )
```

```python
import jax
import jax.numpy as jnp
from jax import lax
from jax.experimental import pallas as pl
from jax.experimental.pallas import tpu as pltpu
from jax.sharding import PartitionSpec as P

EPSILON = 1e-06
LANES = 128
EDGE = 8
VMEM_BYTES = 24 * 1024 * 1024
PACK_TILES = 4
GATE_TILES = 4
F32 = jnp.float32
BF16 = jnp.bfloat16


def params(*semantics):
    return pltpu.CompilerParams(dimension_semantics=semantics, vmem_limit_bytes=VMEM_BYTES)


def in_hbm(array):
    return pltpu.with_memory_space_constraint(array, pltpu.HBM)


def lane_taps(taps_ref, which, size, width, first=0):
    groups = taps_ref.shape[2]
    group = lax.broadcasted_iota(jnp.int32, (groups, width), 0)
    lane = lax.broadcasted_iota(jnp.int32, (groups, width), 1) + first
    spread = (group == lane // size).astype(BF16)
    return jnp.dot(taps_ref[which], spread, preferred_element_type=F32)


def short_filter(extended, taps, start, rows):
    total = extended[start : start + rows] * taps[0:1]
    for j in range(1, taps.shape[0]):
        total = total + extended[start - j : start - j + rows] * taps[j : j + 1]
    return total


def pack_kernel(
    size, q_hbm, k_hbm, v_hbm, taps_hbm, out_hbm, q_ref, k_ref, v_ref, taps_ref, wide_ref, out_ref, sems, out_sems
):
    rows, width = q_hbm.shape
    tiles = width // LANES
    wide = PACK_TILES * LANES
    taps_copy = pltpu.make_async_copy(taps_hbm, taps_ref, sems.at[0, 3])
    taps_copy.start()
    parts = []
    for p in range(width // wide):
        lanes = pl.ds(p * wide, wide)
        copies = [
            pltpu.make_async_copy(source.at[:, lanes], target.at[:, lanes], sems.at[p, which])
            for which, (source, target) in enumerate(((k_hbm, k_ref), (v_hbm, v_ref), (q_hbm, q_ref)))
        ]
        for copy in copies:
            copy.start()
        parts.append(copies)
    taps_copy.wait()
    taps = [lane_taps(taps_ref, which, size, width) for which in (1, 2)]
    sent = []
    for t in range(tiles):
        if t % PACK_TILES == 0:
            for copy in parts[t // PACK_TILES]:
                copy.wait()
        lanes = slice(t * LANES, (t + 1) * LANES)
        turned = jnp.transpose(q_ref[:LANES, lanes])
        at = LANES + LANES // 2
        out_ref[t, LANES:at, :] = jnp.concatenate([turned[: LANES // 2], turned[LANES // 2 :]], axis=1)
        features = []
        for which, ref in enumerate((k_ref, v_ref)):
            wide_ref[t, which, :EDGE] = jnp.zeros((EDGE, LANES), F32)
            wide_ref[t, which, EDGE:] = ref[:, lanes].astype(F32)
            features.append(short_filter(wide_ref.at[t, which], taps[which][:, lanes], EDGE, rows))
            ends = [wide_ref[t, which, EDGE : 2 * EDGE], wide_ref[t, which, rows : rows + EDGE]]
            out_ref[t, at : at + 2 * EDGE, which * LANES : (which + 1) * LANES] = (
                jnp.concatenate(ends, axis=0).astype(BF16)
            )
        out_ref[t, :LANES, :] = jnp.transpose((features[0] * features[1]).astype(BF16))
        middle = q_ref[LANES : LANES + 2 * EDGE, lanes].astype(F32)[:EDGE]
        last = q_ref[rows - 2 * EDGE :, lanes].astype(F32)[EDGE:]
        out_ref[t, at + 2 * EDGE :, :] = jnp.concatenate([middle, last], axis=1).astype(BF16)
        if (t + 1) % PACK_TILES == 0:
            part = t // PACK_TILES
            done = pl.ds(part * PACK_TILES, PACK_TILES)
            copy = pltpu.make_async_copy(out_ref.at[done], out_hbm.at[done], out_sems.at[part])
            copy.start()
            sent.append(copy)
    for copy in sent:
        copy.wait()


def call_pack(q_one, k_one, v_one, short_taps):
    rows, width = q_one.shape
    tiles = width // LANES
    size = width // short_taps.shape[2]
    assert rows == 2 * LANES
    out_shape = (tiles, LANES + LANES // 2 + 3 * EDGE, rows)

    def kernel(*refs):
        pack_kernel(size, *refs)

    inputs = [in_hbm(array) for array in (q_one, k_one, v_one, short_taps)]
    return pl.pallas_call(
        kernel,
        in_specs=[pl.BlockSpec(memory_space=pltpu.HBM)] * 4,
        out_specs=pl.BlockSpec(memory_space=pltpu.HBM),
        out_shape=pltpu.HBM(out_shape, BF16),
        scratch_shapes=[
            pltpu.VMEM((rows, width), BF16),
            pltpu.VMEM((rows, width), BF16),
            pltpu.VMEM((rows, width), BF16),
            pltpu.VMEM(short_taps.shape, BF16),
            pltpu.VMEM((tiles, 2, EDGE + rows, LANES), F32),
            pltpu.VMEM(out_shape, BF16),
            pltpu.SemaphoreType.DMA((tiles // PACK_TILES, 4)),
            pltpu.SemaphoreType.DMA((tiles // PACK_TILES,)),
        ],
        compiler_params=params(),
        name="pack",
    )(*inputs)


def shifted_rows(row, count):
    return pltpu.roll(jnp.broadcast_to(row, (count, row.shape[1])), 0, 1, stride=1, stride_axis=0)


def long_windows(long_rows, rows, lags):
    groups, length = long_rows.shape
    reach = lags * rows
    padded = jnp.pad(long_rows.astype(F32), ((0, 0), (rows, 0)))
    pieces = [padded[:, p : p + reach + rows] for p in range(0, length, reach)]
    return jnp.stack(pieces, axis=1).reshape(-1, reach + rows)


def early_kernel(
    size, q_ref, k_ref, v_ref, gate_ref, taps_ref, base_ref, out_ref, energy_ref, extended_ref
):
    rows, width = q_ref.shape
    groups = LANES // size
    taps = [lane_taps(taps_ref, which, size, width) for which in range(3)]
    lane_group = lax.broadcasted_iota(jnp.int32, (1, LANES), 1) // size
    own = lax.broadcasted_iota(jnp.int32, (LANES, LANES), 0) >= EDGE
    squares = jnp.zeros((LANES, LANES), F32)
    for t in range(width // LANES):
        lanes = slice(t * LANES, (t + 1) * LANES)
        for which, ref in enumerate((q_ref, k_ref, v_ref)):
            extended_ref[t, which, :EDGE] = jnp.zeros((EDGE, LANES), F32)
            extended_ref[t, which, EDGE:] = ref[:, lanes].astype(F32)
        q_feat = short_filter(extended_ref.at[t, 0], taps[0][:, lanes], EDGE + LANES, LANES)
        k_feat = short_filter(extended_ref.at[t, 1], taps[1][:, lanes], EDGE, rows)
        v_feat = short_filter(extended_ref.at[t, 2], taps[2][:, lanes], EDGE, rows)
        table = jnp.concatenate(
            [
                shifted_rows(base_ref[g : g + 1, :], LANES).astype(BF16)
                for g in range(t * groups, (t + 1) * groups)
            ],
            axis=0,
        )
        every = jnp.dot(table, (k_feat * v_feat).astype(BF16), preferred_element_type=F32)
        medium = every[:LANES]
        for g in range(1, groups):
            medium = jnp.where(lane_group == g, every[g * LANES : (g + 1) * LANES], medium)
        mixed = jnp.where(own, q_feat * medium, 0.0)
        out_ref[t] = jnp.transpose(mixed * gate_ref[LANES:, lanes].astype(F32))
        squares = squares + mixed * mixed
    energy_ref[...] = jnp.sum(jnp.transpose(squares), axis=0, keepdims=True)


def call_early(q_one, k_one, v_one, k_two, short_taps, medium_taps):
    rows, width = q_one.shape
    tiles = width // LANES
    size = width // short_taps.shape[2]
    base = jnp.transpose(medium_taps[::-1])
    base = jnp.pad(base, ((0, 0), (1, rows - medium_taps.shape[0] - 1))).astype(F32)

    def kernel(*refs):
        early_kernel(size, *refs)

    return pl.pallas_call(
        kernel,
        in_specs=[pl.BlockSpec(memory_space=pltpu.VMEM)] * 6,
        out_specs=[pl.BlockSpec(memory_space=pltpu.VMEM)] * 2,
        out_shape=[
            jax.ShapeDtypeStruct((tiles, LANES, LANES), F32),
            jax.ShapeDtypeStruct((1, LANES), F32),
        ],
        scratch_shapes=[pltpu.VMEM((tiles, 3, EDGE + rows, LANES), F32)],
        compiler_params=params(),
        name="early",
    )(q_one, k_one, v_one, k_two, short_taps, base)


def join_kernel(full_width, gate_ref, early_ref, energy_ref, long_ref, out_ref):
    tiles = out_ref.shape[0]
    groups = long_ref.shape[0] // tiles
    scale = lax.rsqrt(energy_ref[...] / full_width + EPSILON)
    lane = lax.broadcasted_iota(jnp.int32, (LANES, LANES), 1)
    for t in range(tiles):
        lanes = slice(t * LANES, (t + 1) * LANES)
        turned = jnp.transpose(gate_ref[:, lanes])
        values = jnp.where(lane < EDGE, turned[:, LANES:].astype(F32), early_ref[t] * scale)
        out_ref[t, :LANES, :LANES] = turned[:, :LANES]
        out_ref[t, :LANES, LANES:] = values.astype(BF16)
        out_ref[t, LANES:, :] = long_ref[t * groups : (t + 1) * groups, :].astype(F32).astype(BF16)


def call_join(k_two, early, energy, long_taps, full_width):
    rows, width = k_two.shape
    tiles = width // LANES

    def kernel(*refs):
        join_kernel(full_width, *refs)

    return pl.pallas_call(
        kernel,
        in_specs=[pl.BlockSpec(memory_space=pltpu.VMEM)] * 4,
        out_specs=pl.BlockSpec(memory_space=pltpu.VMEM),
        out_shape=jax.ShapeDtypeStruct((tiles, LANES + long_taps.shape[0] // tiles, rows), BF16),
        compiler_params=params(),
        name="join",
    )(k_two, early, energy, long_taps)


def mix_kernel(
    size,
    holder_ref,
    moved_ref,
    ends_ref,
    more_ref,
    taps_ref,
    q_base_ref,
    base_ref,
    out_ref,
    energy_ref,
    extended_ref,
    q_ends_ref,
    q_ref,
    z_ref,
    medium_ref,
):
    blocks, shard, rows = out_ref.shape
    halves = rows // LANES
    span = 2 * EDGE
    holders = [holder_ref[b] for b in range(blocks)]
    ends = [ends_ref[holder].astype(F32) for holder in holders]
    more = [more_ref[holder].astype(F32) for holder in holders]

    features = []
    for which in range(2):
        lanes = slice(which * shard, (which + 1) * shard)
        extended_ref[which, :EDGE] = jnp.zeros((EDGE, shard), F32)
        for b in range(blocks):
            before = ends[b - 1][EDGE:, lanes] if b else jnp.zeros((EDGE, shard), F32)
            at = EDGE + b * span
            extended_ref[which, at : at + span] = jnp.concatenate([before, ends[b][:EDGE, lanes]], axis=0)
        features.append(
            short_filter(extended_ref.at[which], taps_ref[which + 1], EDGE, blocks * span)
        )
    starts = jnp.transpose((features[0] * features[1]).astype(BF16))
    wide = blocks * span
    for b in range(blocks):
        before = more[b - 1][:, shard:] if b else jnp.zeros((EDGE, shard), F32)
        q_ends_ref[b * span : (b + 1) * span] = jnp.concatenate([before, more[b][:, :shard]], axis=0)
    q_ends = jnp.transpose(q_ends_ref[...].astype(BF16))

    lane = lax.broadcasted_iota(jnp.int32, (shard, LANES), 1)
    if wide == LANES:
        source = lax.broadcasted_iota(jnp.int32, (wide, blocks * LANES), 0)
        target = lax.broadcasted_iota(jnp.int32, (wide, blocks * LANES), 1)
        place = ((target + target // LANES * span + EDGE - source) % wide == 0).astype(F32).astype(BF16)
        both = jnp.dot(
            jnp.concatenate([starts, q_ends], axis=0), place, preferred_element_type=F32
        )
        firsts = [both[:shard, b * LANES : (b + 1) * LANES] for b in range(blocks)]
        arounds = [both[shard:, b * LANES : (b + 1) * LANES] for b in range(blocks)]
    else:
        firsts, arounds = [], []
        for b in range(blocks):
            shift = (wide - b * span - EDGE) % wide
            firsts.append(pltpu.roll(starts.astype(F32), shift, 1)[:, :LANES])
            turned = pltpu.roll(q_ends.astype(F32), shift, 1)
            arounds.append(jnp.where(lane < EDGE, turned[:, :LANES], turned[:, wide - LANES :]))

    half = shard // 2
    z_ref[:, :LANES] = jnp.zeros((shard, LANES), BF16)
    for b, holder in enumerate(holders):
        at = LANES + b * rows
        z_own = moved_ref[holder, :shard, :LANES].astype(F32)
        z_ref[:, at : at + LANES] = jnp.where(lane < EDGE, firsts[b], z_own).astype(BF16)
        z_ref[:, at + LANES : at + rows] = moved_ref[holder, :shard, LANES:]
        both = moved_ref[holder, shard : shard + half, :].astype(F32)
        q_own = jnp.concatenate([both[:, :LANES], both[:, LANES:]], axis=0)
        q_ref[b] = jnp.concatenate([q_own, arounds[b]], axis=1).astype(BF16)
    for g in range(shard // size):
        here = slice(g * size, (g + 1) * size)
        table = shifted_rows(q_base_ref[g : g + 1, :], 2 * LANES).astype(BF16)
        left = jnp.concatenate([q_ref[b, here] for b in range(blocks)], axis=0)
        q_feat = jnp.dot(left, table, preferred_element_type=F32)
        for b in range(blocks):
            out_ref[b, here] = q_feat[b * size : (b + 1) * size]
        table = shifted_rows(base_ref[g : g + 1, :], 2 * LANES)[:, :LANES].astype(BF16)
        windows = [z_ref[here, o * LANES : (o + 2) * LANES] for o in range(blocks * halves)]
        medium_ref[g] = jnp.dot(jnp.concatenate(windows, axis=0), table, preferred_element_type=F32)
    for o in range(blocks * halves):
        b, at = o // halves, (o % halves) * LANES
        medium = medium_ref[:, o * size : (o + 1) * size, :].reshape(shard, LANES)
        mixed = out_ref[b, :, at : at + LANES] * medium
        if at:
            mixed = jnp.where(lane < EDGE, mixed, 0.0)
        out_ref[b, :, at : at + LANES] = mixed
        energy_ref[o : o + 1, :] = jnp.sum(mixed * mixed, axis=0, keepdims=True)


def call_mix(holder, moved, ends, more, short_local, medium_local, shard, rows):
    blocks = moved.shape[0]
    size = shard // medium_local.shape[1]
    reach = medium_local.shape[0]
    assert reach == LANES and short_local.shape[1] <= EDGE + 1
    lane_form = jnp.repeat(short_local, size, axis=2).astype(F32)
    base = jnp.pad(jnp.transpose(medium_local).astype(F32), ((0, 0), (LANES, 0)))
    q_base = jnp.transpose(short_local[0]).astype(F32)
    q_base = jnp.pad(q_base, ((0, 0), (0, rows - q_base.shape[1])))

    def kernel(*refs):
        mix_kernel(size, *refs)

    return pl.pallas_call(
        kernel,
        in_specs=[pl.BlockSpec(memory_space=pltpu.SMEM)]
        + [pl.BlockSpec(memory_space=pltpu.VMEM)] * 6,
        out_specs=[pl.BlockSpec(memory_space=pltpu.VMEM)] * 2,
        out_shape=[
            jax.ShapeDtypeStruct((blocks, shard, rows), F32),
            jax.ShapeDtypeStruct((blocks * rows // LANES, LANES), F32),
        ],
        scratch_shapes=[
            pltpu.VMEM((2, EDGE + blocks * 2 * EDGE, shard), F32),
            pltpu.VMEM((blocks * 2 * EDGE, shard), F32),
            pltpu.VMEM((blocks, shard, rows), BF16),
            pltpu.VMEM((shard, LANES + blocks * rows), BF16),
            pltpu.VMEM((shard // size, blocks * rows // LANES * size, LANES), F32),
        ],
        compiler_params=params(),
        name="mix",
    )(holder, moved, ends, more, lane_form, q_base, base)


def long_kernel(
    full_width, size, holder_ref, mixed_ref, key_ref, energy_ref, window_ref, gain_ref, out_ref, ordered_ref, strip_ref
):
    blocks, shard, rows = mixed_ref.shape
    half = rows // 2
    halves = rows // LANES
    lags = window_ref.shape[1] // rows - 1
    pieces = blocks // lags
    reach = blocks * size
    holders = [holder_ref[b] for b in range(blocks)]
    scale = lax.rsqrt(energy_ref[...] / full_width + EPSILON)
    own = lax.broadcasted_iota(jnp.int32, (size, rows), 1) >= LANES + EDGE
    for b, holder in enumerate(holders):
        line = jnp.concatenate([scale[o : o + 1] for o in range(b * halves, (b + 1) * halves)], axis=1)
        for g in range(shard // size):
            here = slice(g * size, (g + 1) * size)
            key = key_ref[holder, here].astype(F32)
            value = jnp.where(own, key, key * mixed_ref[b, here] * line)
            ordered_ref[g, reach + b * size : reach + (b + 1) * size] = value.astype(BF16)
    for slot in range(window_ref.shape[0]):
        strip_ref[slot] = shifted_rows(window_ref[slot : slot + 1, :], half)[:, half:].astype(BF16)
    for g in range(shard // size):
        here = slice(g * size, (g + 1) * size)
        ordered_ref[g, :reach] = jnp.zeros((reach, rows), BF16)
        total = ordered_ref[g, reach:].astype(F32) * jnp.concatenate([gain_ref[here]] * blocks, axis=0)
        for p in range(pieces):
            slot = g * pieces + p
            left = jnp.concatenate(
                [
                    ordered_ref[g, (blocks - lag) * size : (2 * blocks - lag) * size]
                    for lag in range(p * lags, (p + 1) * lags)
                ],
                axis=1,
            )
            right = jnp.concatenate(
                [
                    strip_ref[slot, :, shift - half : shift - half + rows]
                    for lag in range(1, lags + 1)
                    for shift in (lag * rows, lag * rows - half)
                ],
                axis=0,
            )
            total = total + jnp.dot(left, right, preferred_element_type=F32)
        for b, holder in enumerate(holders):
            out_ref[holder, here] = total[b * size : (b + 1) * size].astype(BF16)


def call_long(holder, mixed, keys, energy, windows, gain, size, full_width):
    blocks, shard, rows = mixed.shape

    def kernel(*refs):
        long_kernel(full_width, size, *refs)

    return pl.pallas_call(
        kernel,
        in_specs=[pl.BlockSpec(memory_space=pltpu.SMEM)]
        + [pl.BlockSpec(memory_space=pltpu.VMEM)] * 5,
        out_specs=pl.BlockSpec(memory_space=pltpu.VMEM),
        out_shape=jax.ShapeDtypeStruct((blocks, shard, rows), BF16),
        scratch_shapes=[pltpu.VMEM((shard // size, 2 * blocks * size, rows), BF16), pltpu.VMEM((windows.shape[0], rows // 2, windows.shape[1] - rows // 2), BF16)],
        compiler_params=params(),
        name="long",
    )(holder, mixed, keys, energy, windows, gain)


def gate_kernel(mixed_ref, gate_ref, out_hbm, out_ref, sems):
    copies = []
    for t in range(mixed_ref.shape[0]):
        lanes = slice(t * LANES, (t + 1) * LANES)
        mixed = jnp.transpose(mixed_ref[t]).astype(F32)
        out_ref[:, lanes] = (gate_ref[:, lanes].astype(F32) * mixed).astype(BF16)
        if (t + 1) % GATE_TILES == 0:
            part = t // GATE_TILES
            done = pl.ds(part * GATE_TILES * LANES, GATE_TILES * LANES)
            copy = pltpu.make_async_copy(out_ref.at[:, done], out_hbm.at[:, done], sems.at[part])
            copy.start()
            copies.append(copy)
    for copy in copies:
        copy.wait()


def call_gate(mixed, q_two):
    rows, width = q_two.shape
    return pl.pallas_call(
        gate_kernel,
        in_specs=[pl.BlockSpec(memory_space=pltpu.VMEM)] * 2,
        out_specs=pl.BlockSpec(memory_space=pltpu.HBM),
        out_shape=pltpu.HBM((rows, width), BF16),
        scratch_shapes=[
            pltpu.VMEM((rows, width), BF16),
            pltpu.SemaphoreType.DMA((width // LANES // GATE_TILES,)),
        ],
        compiler_params=params(),
        name="gate",
    )(mixed, q_two)


def exchange(array):
    return lax.all_to_all(array, "ctx", split_axis=0, concat_axis=0, tiled=True)


def sum_by_pairs(array, axis):
    count = lax.axis_size(axis)
    assert count & (count - 1) == 0
    bit = 1
    while bit < count:
        array = array + lax.ppermute(array, axis, [(i, i ^ bit) for i in range(count)])
        bit *= 2
    return array


def per_device(
    q_one,
    k_one,
    v_one,
    q_two,
    k_two,
    short_taps,
    medium_taps,
    long_taps,
    skip_gain,
    block_order,
    prev_owner,
):
    rows, width = q_one.shape
    ctx_count = lax.axis_size("ctx")
    tp_count = lax.axis_size("tp")
    me = lax.axis_index("ctx")
    size = width // short_taps.shape[2]
    tiles = width // LANES
    tile_groups = LANES // size
    shard = width // ctx_count
    shard_groups = shard // size
    full_width = width * tp_count

    slots = jnp.arange(ctx_count, dtype=jnp.int32)
    holder = jnp.sum(jnp.where(block_order[None, :] == slots[:, None], slots[None, :], 0), axis=1)

    packed = call_pack(q_one, k_one, v_one, short_taps)
    span = 2 * EDGE
    if ctx_count != tiles:
        half = LANES // 2
        sizes = (LANES, half, span, EDGE)
        z, q, ends, more = jnp.split(packed, [sum(sizes[:n]) for n in range(1, 4)], axis=1)
        q = jnp.transpose(q.reshape(tiles, half, 2, LANES), (0, 2, 1, 3))
        q = jnp.transpose(q.reshape(ctx_count, 2, shard // 2, LANES), (0, 2, 1, 3))
        ends = jnp.transpose(ends.reshape(tiles, span, 2, -1, shard), (0, 3, 1, 2, 4))
        more = jnp.transpose(more.reshape(tiles, EDGE, 2, -1, shard), (0, 3, 1, 2, 4))
        parts = [part.reshape(ctx_count, -1, rows) for part in (z, q, ends, more)]
        packed = jnp.concatenate(parts, axis=1)
    moved = exchange(packed)
    ends_at = shard + shard // 2
    more_at = ends_at + span * 2 * shard // rows
    more_to = more_at + EDGE * 2 * shard // rows
    ends = moved[:, ends_at:more_at].reshape(ctx_count, span, 2 * shard)
    more = moved[:, more_at:more_to].reshape(ctx_count, EDGE, 2 * shard)

    early, early_energy = call_early(q_one, k_one, v_one, k_two, short_taps, medium_taps)
    early_energy = sum_by_pairs(early_energy, "tp")
    joined = call_join(k_two, early, early_energy, long_taps, full_width)
    if ctx_count != tiles:
        taps = joined[:, LANES : LANES + tile_groups].reshape(ctx_count, shard_groups, rows)
        joined = jnp.concatenate([joined[:, :LANES].reshape(ctx_count, shard, rows), taps], axis=1)
    moved, joined = lax.optimization_barrier((moved, joined))

    short_local = lax.dynamic_slice_in_dim(short_taps, me * shard_groups, shard_groups, axis=2)
    medium_local = lax.dynamic_slice_in_dim(medium_taps, me * shard_groups, shard_groups, axis=1)
    mixed, energy = call_mix(holder, moved, ends, more, short_local, medium_local, shard, rows)
    energy, joined = lax.optimization_barrier((energy, joined))
    keys = exchange(joined)
    energy = sum_by_pairs(sum_by_pairs(energy, "tp"), "ctx")

    long_rows = keys[:, shard : shard + shard_groups]
    long_rows = jnp.transpose(long_rows, (1, 0, 2)).reshape(shard_groups, ctx_count * rows)
    windows = long_windows(long_rows, rows, min(ctx_count, 8))
    gain = lax.dynamic_slice_in_dim(skip_gain, me * shard, shard).reshape(shard, 1)
    filtered = call_long(
        holder, mixed, keys, energy, windows, gain, size, full_width
    )
    returned = exchange(filtered)
    return call_gate(returned.reshape(tiles, LANES, rows), q_two)


def solution(mesh):
    in_specs = (
        P("ctx", "tp"),
        P("ctx", "tp"),
        P("ctx", "tp"),
        P("ctx", "tp"),
        P("ctx", "tp"),
        P(None, None, "tp"),
        P(None, "tp"),
        P("tp", "ctx"),
        P("tp"),
        P(),
        P(),
    )
    out_specs = P("ctx", "tp")
    return jax.shard_map(
        per_device, mesh=mesh, in_specs=in_specs, out_specs=out_specs, check_vma=False
    )
```

```python
import jax
import jax.numpy as jnp
from jax import lax
from jax.experimental import pallas as pl
from jax.experimental.pallas import tpu as pltpu
from jax.sharding import PartitionSpec as P

EPSILON = 1e-06
LANES = 128
EDGE = 8
VMEM_BYTES = 24 * 1024 * 1024
PACK_TILES = 4
GATE_TILES = 4
F32 = jnp.float32
BF16 = jnp.bfloat16


def params(*semantics):
    return pltpu.CompilerParams(dimension_semantics=semantics, vmem_limit_bytes=VMEM_BYTES)


def in_hbm(array):
    return pltpu.with_memory_space_constraint(array, pltpu.HBM)


def lane_taps(taps_ref, which, size, width, first=0):
    groups = taps_ref.shape[2]
    group = lax.broadcasted_iota(jnp.int32, (groups, width), 0)
    lane = lax.broadcasted_iota(jnp.int32, (groups, width), 1) + first
    spread = (group == lane // size).astype(BF16)
    return jnp.dot(taps_ref[which], spread, preferred_element_type=F32)


def short_filter(extended, taps, start, rows):
    total = extended[start : start + rows] * taps[0:1]
    for j in range(1, taps.shape[0]):
        total = total + extended[start - j : start - j + rows] * taps[j : j + 1]
    return total


def pack_kernel(
    size, q_hbm, k_hbm, v_hbm, taps_hbm, out_hbm, q_ref, k_ref, v_ref, taps_ref, wide_ref, out_ref, sems, out_sems
):
    rows, width = q_hbm.shape
    tiles = width // LANES
    wide = PACK_TILES * LANES
    taps_copy = pltpu.make_async_copy(taps_hbm, taps_ref, sems.at[0, 3])
    taps_copy.start()
    parts = []
    for p in range(width // wide):
        lanes = pl.ds(p * wide, wide)
        copies = [
            pltpu.make_async_copy(source.at[:, lanes], target.at[:, lanes], sems.at[p, which])
            for which, (source, target) in enumerate(((k_hbm, k_ref), (v_hbm, v_ref), (q_hbm, q_ref)))
        ]
        for copy in copies:
            copy.start()
        parts.append(copies)
    taps_copy.wait()
    taps = [lane_taps(taps_ref, which, size, width) for which in (1, 2)]
    sent = []
    for t in range(tiles):
        if t % PACK_TILES == 0:
            for copy in parts[t // PACK_TILES]:
                copy.wait()
        lanes = slice(t * LANES, (t + 1) * LANES)
        turned = jnp.transpose(q_ref[:LANES, lanes])
        at = LANES + LANES // 2
        out_ref[t, LANES:at, :] = jnp.concatenate([turned[: LANES // 2], turned[LANES // 2 :]], axis=1)
        features = []
        for which, ref in enumerate((k_ref, v_ref)):
            wide_ref[t, which, :EDGE] = jnp.zeros((EDGE, LANES), F32)
            wide_ref[t, which, EDGE:] = ref[:, lanes].astype(F32)
            features.append(short_filter(wide_ref.at[t, which], taps[which][:, lanes], EDGE, rows))
            ends = [wide_ref[t, which, EDGE : 2 * EDGE], wide_ref[t, which, rows : rows + EDGE]]
            out_ref[t, at : at + 2 * EDGE, which * LANES : (which + 1) * LANES] = (
                jnp.concatenate(ends, axis=0).astype(BF16)
            )
        out_ref[t, :LANES, :] = jnp.transpose((features[0] * features[1]).astype(BF16))
        middle = q_ref[LANES : LANES + 2 * EDGE, lanes].astype(F32)[:EDGE]
        last = q_ref[rows - 2 * EDGE :, lanes].astype(F32)[EDGE:]
        out_ref[t, at + 2 * EDGE :, :] = jnp.concatenate([middle, last], axis=1).astype(BF16)
        if (t + 1) % PACK_TILES == 0:
            part = t // PACK_TILES
            done = pl.ds(part * PACK_TILES, PACK_TILES)
            copy = pltpu.make_async_copy(out_ref.at[done], out_hbm.at[done], out_sems.at[part])
            copy.start()
            sent.append(copy)
    for copy in sent:
        copy.wait()


def call_pack(q_one, k_one, v_one, short_taps):
    rows, width = q_one.shape
    tiles = width // LANES
    size = width // short_taps.shape[2]
    assert rows == 2 * LANES
    out_shape = (tiles, LANES + LANES // 2 + 3 * EDGE, rows)

    def kernel(*refs):
        pack_kernel(size, *refs)

    inputs = [in_hbm(array) for array in (q_one, k_one, v_one, short_taps)]
    return pl.pallas_call(
        kernel,
        in_specs=[pl.BlockSpec(memory_space=pltpu.HBM)] * 4,
        out_specs=pl.BlockSpec(memory_space=pltpu.HBM),
        out_shape=pltpu.HBM(out_shape, BF16),
        scratch_shapes=[
            pltpu.VMEM((rows, width), BF16),
            pltpu.VMEM((rows, width), BF16),
            pltpu.VMEM((rows, width), BF16),
            pltpu.VMEM(short_taps.shape, BF16),
            pltpu.VMEM((tiles, 2, EDGE + rows, LANES), F32),
            pltpu.VMEM(out_shape, BF16),
            pltpu.SemaphoreType.DMA((tiles // PACK_TILES, 4)),
            pltpu.SemaphoreType.DMA((tiles // PACK_TILES,)),
        ],
        compiler_params=params(),
        name="pack",
    )(*inputs)


def shifted_rows(row, count):
    return pltpu.roll(jnp.broadcast_to(row, (count, row.shape[1])), 0, 1, stride=1, stride_axis=0)


def long_windows(long_rows, rows, lags):
    groups, length = long_rows.shape
    reach = lags * rows
    padded = jnp.pad(long_rows.astype(F32), ((0, 0), (rows, 0)))
    pieces = [padded[:, p : p + reach + rows] for p in range(0, length, reach)]
    return jnp.stack(pieces, axis=1).reshape(-1, reach + rows)


def early_kernel(
    size, q_ref, k_ref, v_ref, gate_ref, taps_ref, base_ref, out_ref, energy_ref, extended_ref
):
    rows, width = q_ref.shape
    groups = LANES // size
    taps = [lane_taps(taps_ref, which, size, width) for which in range(3)]
    lane_group = lax.broadcasted_iota(jnp.int32, (1, LANES), 1) // size
    own = lax.broadcasted_iota(jnp.int32, (LANES, LANES), 0) >= EDGE
    squares = jnp.zeros((LANES, LANES), F32)
    for t in range(width // LANES):
        lanes = slice(t * LANES, (t + 1) * LANES)
        for which, ref in enumerate((q_ref, k_ref, v_ref)):
            extended_ref[t, which, :EDGE] = jnp.zeros((EDGE, LANES), F32)
            extended_ref[t, which, EDGE:] = ref[:, lanes].astype(F32)
        q_feat = short_filter(extended_ref.at[t, 0], taps[0][:, lanes], EDGE + LANES, LANES)
        k_feat = short_filter(extended_ref.at[t, 1], taps[1][:, lanes], EDGE, rows)
        v_feat = short_filter(extended_ref.at[t, 2], taps[2][:, lanes], EDGE, rows)
        table = jnp.concatenate(
            [
                shifted_rows(base_ref[g : g + 1, :], LANES).astype(BF16)
                for g in range(t * groups, (t + 1) * groups)
            ],
            axis=0,
        )
        every = jnp.dot(table, (k_feat * v_feat).astype(BF16), preferred_element_type=F32)
        medium = every[:LANES]
        for g in range(1, groups):
            medium = jnp.where(lane_group == g, every[g * LANES : (g + 1) * LANES], medium)
        mixed = jnp.where(own, q_feat * medium, 0.0)
        out_ref[t] = jnp.transpose(mixed * gate_ref[LANES:, lanes].astype(F32))
        squares = squares + mixed * mixed
    energy_ref[...] = jnp.sum(jnp.transpose(squares), axis=0, keepdims=True)


def call_early(q_one, k_one, v_one, k_two, short_taps, medium_taps):
    rows, width = q_one.shape
    tiles = width // LANES
    size = width // short_taps.shape[2]
    base = jnp.transpose(medium_taps[::-1])
    base = jnp.pad(base, ((0, 0), (1, rows - medium_taps.shape[0] - 1))).astype(F32)

    def kernel(*refs):
        early_kernel(size, *refs)

    return pl.pallas_call(
        kernel,
        in_specs=[pl.BlockSpec(memory_space=pltpu.VMEM)] * 6,
        out_specs=[pl.BlockSpec(memory_space=pltpu.VMEM)] * 2,
        out_shape=[
            jax.ShapeDtypeStruct((tiles, LANES, LANES), F32),
            jax.ShapeDtypeStruct((1, LANES), F32),
        ],
        scratch_shapes=[pltpu.VMEM((tiles, 3, EDGE + rows, LANES), F32)],
        compiler_params=params(),
        name="early",
    )(q_one, k_one, v_one, k_two, short_taps, base)


def join_kernel(full_width, gate_ref, early_ref, energy_ref, long_ref, out_ref):
    tiles = out_ref.shape[0]
    groups = long_ref.shape[0] // tiles
    scale = lax.rsqrt(energy_ref[...] / full_width + EPSILON)
    lane = lax.broadcasted_iota(jnp.int32, (LANES, LANES), 1)
    for t in range(tiles):
        lanes = slice(t * LANES, (t + 1) * LANES)
        turned = jnp.transpose(gate_ref[:, lanes])
        values = jnp.where(lane < EDGE, turned[:, LANES:].astype(F32), early_ref[t] * scale)
        out_ref[t, :LANES, :LANES] = turned[:, :LANES]
        out_ref[t, :LANES, LANES:] = values.astype(BF16)
        out_ref[t, LANES:, :] = long_ref[t * groups : (t + 1) * groups, :].astype(F32).astype(BF16)


def call_join(k_two, early, energy, long_taps, full_width):
    rows, width = k_two.shape
    tiles = width // LANES

    def kernel(*refs):
        join_kernel(full_width, *refs)

    return pl.pallas_call(
        kernel,
        in_specs=[pl.BlockSpec(memory_space=pltpu.VMEM)] * 4,
        out_specs=pl.BlockSpec(memory_space=pltpu.VMEM),
        out_shape=jax.ShapeDtypeStruct((tiles, LANES + long_taps.shape[0] // tiles, rows), BF16),
        compiler_params=params(),
        name="join",
    )(k_two, early, energy, long_taps)


def mix_kernel(
    size,
    holder_ref,
    moved_ref,
    ends_ref,
    more_ref,
    taps_ref,
    q_base_ref,
    base_ref,
    out_ref,
    energy_ref,
    extended_ref,
    q_ends_ref,
    q_ref,
    z_ref,
    medium_ref,
):
    blocks, shard, rows = out_ref.shape
    halves = rows // LANES
    span = 2 * EDGE
    holders = [holder_ref[b] for b in range(blocks)]
    ends = [ends_ref[holder].astype(F32) for holder in holders]
    more = [more_ref[holder].astype(F32) for holder in holders]

    features = []
    for which in range(2):
        lanes = slice(which * shard, (which + 1) * shard)
        extended_ref[which, :EDGE] = jnp.zeros((EDGE, shard), F32)
        for b in range(blocks):
            before = ends[b - 1][EDGE:, lanes] if b else jnp.zeros((EDGE, shard), F32)
            at = EDGE + b * span
            extended_ref[which, at : at + span] = jnp.concatenate([before, ends[b][:EDGE, lanes]], axis=0)
        features.append(
            short_filter(extended_ref.at[which], taps_ref[which + 1], EDGE, blocks * span)
        )
    starts = jnp.transpose((features[0] * features[1]).astype(BF16))
    wide = blocks * span
    for b in range(blocks):
        before = more[b - 1][:, shard:] if b else jnp.zeros((EDGE, shard), F32)
        q_ends_ref[b * span : (b + 1) * span] = jnp.concatenate([before, more[b][:, :shard]], axis=0)
    q_ends = jnp.transpose(q_ends_ref[...].astype(BF16))

    lane = lax.broadcasted_iota(jnp.int32, (shard, LANES), 1)
    if wide == LANES:
        source = lax.broadcasted_iota(jnp.int32, (wide, blocks * LANES), 0)
        target = lax.broadcasted_iota(jnp.int32, (wide, blocks * LANES), 1)
        place = ((target + target // LANES * span + EDGE - source) % wide == 0).astype(F32).astype(BF16)
        both = jnp.dot(
            jnp.concatenate([starts, q_ends], axis=0), place, preferred_element_type=F32
        )
        firsts = [both[:shard, b * LANES : (b + 1) * LANES] for b in range(blocks)]
        arounds = [both[shard:, b * LANES : (b + 1) * LANES] for b in range(blocks)]
    else:
        firsts, arounds = [], []
        for b in range(blocks):
            shift = (wide - b * span - EDGE) % wide
            firsts.append(pltpu.roll(starts.astype(F32), shift, 1)[:, :LANES])
            turned = pltpu.roll(q_ends.astype(F32), shift, 1)
            arounds.append(jnp.where(lane < EDGE, turned[:, :LANES], turned[:, wide - LANES :]))

    half = shard // 2
    z_ref[:, :LANES] = jnp.zeros((shard, LANES), BF16)
    for b, holder in enumerate(holders):
        at = LANES + b * rows
        z_own = moved_ref[holder, :shard, :LANES].astype(F32)
        z_ref[:, at : at + LANES] = jnp.where(lane < EDGE, firsts[b], z_own).astype(BF16)
        z_ref[:, at + LANES : at + rows] = moved_ref[holder, :shard, LANES:]
        both = moved_ref[holder, shard : shard + half, :].astype(F32)
        q_own = jnp.concatenate([both[:, :LANES], both[:, LANES:]], axis=0)
        q_ref[b] = jnp.concatenate([q_own, arounds[b]], axis=1).astype(BF16)
    for g in range(shard // size):
        here = slice(g * size, (g + 1) * size)
        table = shifted_rows(q_base_ref[g : g + 1, :], 2 * LANES).astype(BF16)
        left = jnp.concatenate([q_ref[b, here] for b in range(blocks)], axis=0)
        q_feat = jnp.dot(left, table, preferred_element_type=F32)
        for b in range(blocks):
            out_ref[b, here] = q_feat[b * size : (b + 1) * size]
        table = shifted_rows(base_ref[g : g + 1, :], 2 * LANES)[:, :LANES].astype(BF16)
        windows = [z_ref[here, o * LANES : (o + 2) * LANES] for o in range(blocks * halves)]
        medium_ref[g] = jnp.dot(jnp.concatenate(windows, axis=0), table, preferred_element_type=F32)
    for o in range(blocks * halves):
        b, at = o // halves, (o % halves) * LANES
        medium = medium_ref[:, o * size : (o + 1) * size, :].reshape(shard, LANES)
        mixed = out_ref[b, :, at : at + LANES] * medium
        if at:
            mixed = jnp.where(lane < EDGE, mixed, 0.0)
        out_ref[b, :, at : at + LANES] = mixed
        energy_ref[o : o + 1, :] = jnp.sum(mixed * mixed, axis=0, keepdims=True)


def call_mix(holder, moved, ends, more, short_local, medium_local, shard, rows):
    blocks = moved.shape[0]
    size = shard // medium_local.shape[1]
    reach = medium_local.shape[0]
    assert reach == LANES and short_local.shape[1] <= EDGE + 1
    lane_form = jnp.repeat(short_local, size, axis=2).astype(F32)
    base = jnp.pad(jnp.transpose(medium_local).astype(F32), ((0, 0), (LANES, 0)))
    q_base = jnp.transpose(short_local[0]).astype(F32)
    q_base = jnp.pad(q_base, ((0, 0), (0, rows - q_base.shape[1])))

    def kernel(*refs):
        mix_kernel(size, *refs)

    return pl.pallas_call(
        kernel,
        in_specs=[pl.BlockSpec(memory_space=pltpu.SMEM)]
        + [pl.BlockSpec(memory_space=pltpu.VMEM)] * 6,
        out_specs=[pl.BlockSpec(memory_space=pltpu.VMEM)] * 2,
        out_shape=[
            jax.ShapeDtypeStruct((blocks, shard, rows), F32),
            jax.ShapeDtypeStruct((blocks * rows // LANES, LANES), F32),
        ],
        scratch_shapes=[
            pltpu.VMEM((2, EDGE + blocks * 2 * EDGE, shard), F32),
            pltpu.VMEM((blocks * 2 * EDGE, shard), F32),
            pltpu.VMEM((blocks, shard, rows), BF16),
            pltpu.VMEM((shard, LANES + blocks * rows), BF16),
            pltpu.VMEM((shard // size, blocks * rows // LANES * size, LANES), F32),
        ],
        compiler_params=params(),
        name="mix",
    )(holder, moved, ends, more, lane_form, q_base, base)


def long_kernel(
    full_width, size, holder_ref, mixed_ref, key_ref, energy_ref, window_ref, gain_ref, out_ref, ordered_ref, strip_ref
):
    blocks, shard, rows = mixed_ref.shape
    half = rows // 2
    halves = rows // LANES
    lags = window_ref.shape[1] // rows - 1
    pieces = blocks // lags
    reach = blocks * size
    holders = [holder_ref[b] for b in range(blocks)]
    scale = lax.rsqrt(energy_ref[...] / full_width + EPSILON)
    own = lax.broadcasted_iota(jnp.int32, (size, rows), 1) >= LANES + EDGE
    for b, holder in enumerate(holders):
        line = jnp.concatenate([scale[o : o + 1] for o in range(b * halves, (b + 1) * halves)], axis=1)
        for g in range(shard // size):
            here = slice(g * size, (g + 1) * size)
            key = key_ref[holder, here].astype(F32)
            value = jnp.where(own, key, key * mixed_ref[b, here] * line)
            ordered_ref[g, reach + b * size : reach + (b + 1) * size] = value.astype(BF16)
    for slot in range(window_ref.shape[0]):
        strip_ref[slot] = shifted_rows(window_ref[slot : slot + 1, :], half)[:, half:].astype(BF16)
    for g in range(shard // size):
        here = slice(g * size, (g + 1) * size)
        ordered_ref[g, :reach] = jnp.zeros((reach, rows), BF16)
        total = ordered_ref[g, reach:].astype(F32) * jnp.concatenate([gain_ref[here]] * blocks, axis=0)
        for slot_lag in range(0, blocks, lags // 2):
            slot = g * pieces + slot_lag // lags
            first = slot_lag * size
            left = jnp.concatenate(
                [
                    ordered_ref[g, reach + first - lag * size : 2 * reach - lag * size]
                    for lag in range(slot_lag, slot_lag + lags // 2)
                ],
                axis=1,
            )
            at = slot_lag % lags
            right = jnp.concatenate(
                [
                    strip_ref[slot, :, shift - half : shift - half + rows]
                    for lag in range(at + 1, at + lags // 2 + 1)
                    for shift in (lag * rows, lag * rows - half)
                ],
                axis=0,
            )
            added = total[first:] + jnp.dot(left, right, preferred_element_type=F32)
            total = jnp.concatenate([total[:first], added], axis=0) if first else added
        for b, holder in enumerate(holders):
            out_ref[holder, here] = total[b * size : (b + 1) * size].astype(BF16)


def call_long(holder, mixed, keys, energy, windows, gain, size, full_width):
    blocks, shard, rows = mixed.shape

    def kernel(*refs):
        long_kernel(full_width, size, *refs)

    return pl.pallas_call(
        kernel,
        in_specs=[pl.BlockSpec(memory_space=pltpu.SMEM)]
        + [pl.BlockSpec(memory_space=pltpu.VMEM)] * 5,
        out_specs=pl.BlockSpec(memory_space=pltpu.VMEM),
        out_shape=jax.ShapeDtypeStruct((blocks, shard, rows), BF16),
        scratch_shapes=[
            pltpu.VMEM((shard // size, 2 * blocks * size, rows), BF16),
            pltpu.VMEM((windows.shape[0], rows // 2, windows.shape[1] - rows // 2), BF16),
        ],
        compiler_params=params(),
        name="long",
    )(holder, mixed, keys, energy, windows, gain)


def gate_kernel(mixed_ref, gate_ref, out_hbm, out_ref, sems):
    copies = []
    for t in range(mixed_ref.shape[0]):
        lanes = slice(t * LANES, (t + 1) * LANES)
        mixed = jnp.transpose(mixed_ref[t]).astype(F32)
        out_ref[:, lanes] = (gate_ref[:, lanes].astype(F32) * mixed).astype(BF16)
        if (t + 1) % GATE_TILES == 0:
            part = t // GATE_TILES
            done = pl.ds(part * GATE_TILES * LANES, GATE_TILES * LANES)
            copy = pltpu.make_async_copy(out_ref.at[:, done], out_hbm.at[:, done], sems.at[part])
            copy.start()
            copies.append(copy)
    for copy in copies:
        copy.wait()


def call_gate(mixed, q_two):
    rows, width = q_two.shape
    return pl.pallas_call(
        gate_kernel,
        in_specs=[pl.BlockSpec(memory_space=pltpu.VMEM)] * 2,
        out_specs=pl.BlockSpec(memory_space=pltpu.HBM),
        out_shape=pltpu.HBM((rows, width), BF16),
        scratch_shapes=[
            pltpu.VMEM((rows, width), BF16),
            pltpu.SemaphoreType.DMA((width // LANES // GATE_TILES,)),
        ],
        compiler_params=params(),
        name="gate",
    )(mixed, q_two)


def exchange(array):
    return lax.all_to_all(array, "ctx", split_axis=0, concat_axis=0, tiled=True)


def sum_by_pairs(array, axis):
    count = lax.axis_size(axis)
    assert count & (count - 1) == 0
    bit = 1
    while bit < count:
        array = array + lax.ppermute(array, axis, [(i, i ^ bit) for i in range(count)])
        bit *= 2
    return array


def per_device(
    q_one,
    k_one,
    v_one,
    q_two,
    k_two,
    short_taps,
    medium_taps,
    long_taps,
    skip_gain,
    block_order,
    prev_owner,
):
    rows, width = q_one.shape
    ctx_count = lax.axis_size("ctx")
    tp_count = lax.axis_size("tp")
    me = lax.axis_index("ctx")
    size = width // short_taps.shape[2]
    tiles = width // LANES
    tile_groups = LANES // size
    shard = width // ctx_count
    shard_groups = shard // size
    full_width = width * tp_count

    slots = jnp.arange(ctx_count, dtype=jnp.int32)
    holder = jnp.sum(jnp.where(block_order[None, :] == slots[:, None], slots[None, :], 0), axis=1)

    packed = call_pack(q_one, k_one, v_one, short_taps)
    span = 2 * EDGE
    if ctx_count != tiles:
        half = LANES // 2
        sizes = (LANES, half, span, EDGE)
        z, q, ends, more = jnp.split(packed, [sum(sizes[:n]) for n in range(1, 4)], axis=1)
        q = jnp.transpose(q.reshape(tiles, half, 2, LANES), (0, 2, 1, 3))
        q = jnp.transpose(q.reshape(ctx_count, 2, shard // 2, LANES), (0, 2, 1, 3))
        ends = jnp.transpose(ends.reshape(tiles, span, 2, -1, shard), (0, 3, 1, 2, 4))
        more = jnp.transpose(more.reshape(tiles, EDGE, 2, -1, shard), (0, 3, 1, 2, 4))
        parts = [part.reshape(ctx_count, -1, rows) for part in (z, q, ends, more)]
        packed = jnp.concatenate(parts, axis=1)
    moved = exchange(packed)
    ends_at = shard + shard // 2
    more_at = ends_at + span * 2 * shard // rows
    more_to = more_at + EDGE * 2 * shard // rows
    ends = moved[:, ends_at:more_at].reshape(ctx_count, span, 2 * shard)
    more = moved[:, more_at:more_to].reshape(ctx_count, EDGE, 2 * shard)

    early, early_energy = call_early(q_one, k_one, v_one, k_two, short_taps, medium_taps)
    early_energy = sum_by_pairs(early_energy, "tp")
    joined = call_join(k_two, early, early_energy, long_taps, full_width)
    if ctx_count != tiles:
        taps = joined[:, LANES : LANES + tile_groups].reshape(ctx_count, shard_groups, rows)
        joined = jnp.concatenate([joined[:, :LANES].reshape(ctx_count, shard, rows), taps], axis=1)
    moved, joined = lax.optimization_barrier((moved, joined))

    short_local = lax.dynamic_slice_in_dim(short_taps, me * shard_groups, shard_groups, axis=2)
    medium_local = lax.dynamic_slice_in_dim(medium_taps, me * shard_groups, shard_groups, axis=1)
    mixed, energy = call_mix(holder, moved, ends, more, short_local, medium_local, shard, rows)
    energy, joined = lax.optimization_barrier((energy, joined))
    keys = exchange(joined)
    energy = sum_by_pairs(sum_by_pairs(energy, "tp"), "ctx")

    long_rows = keys[:, shard : shard + shard_groups]
    long_rows = jnp.transpose(long_rows, (1, 0, 2)).reshape(shard_groups, ctx_count * rows)
    windows = long_windows(long_rows, rows, min(ctx_count, 8))
    gain = lax.dynamic_slice_in_dim(skip_gain, me * shard, shard).reshape(shard, 1)
    filtered = call_long(
        holder, mixed, keys, energy, windows, gain, size, full_width
    )
    returned = exchange(filtered)
    return call_gate(returned.reshape(tiles, LANES, rows), q_two)


def solution(mesh):
    in_specs = (
        P("ctx", "tp"),
        P("ctx", "tp"),
        P("ctx", "tp"),
        P("ctx", "tp"),
        P("ctx", "tp"),
        P(None, None, "tp"),
        P(None, "tp"),
        P("tp", "ctx"),
        P("tp"),
        P(),
        P(),
    )
    out_specs = P("ctx", "tp")
    return jax.shard_map(
        per_device, mesh=mesh, in_specs=in_specs, out_specs=out_specs, check_vma=False
    )
```
